32 devices in a mesh: expert: 8 (over z, y), segment: 4 (over x, core).
Axes of the slice: x: 2, y: 2, z: 4, core: 2. Of those that a mesh axis runs over, the one named last changes fastest.
Arguments:
- tokens: bfloat16 [4, 8, 128, 1664], P('segment', 'expert'), may hold values from -6 to 6
- route_ids: int32 [4, 8, 128, 2], P('segment', 'expert'), may hold values from 0 to 7, all different within a row; in each aligned block of 128 rows (0 to 127, 128 to 255, ..., all dimensions but the last counted through in order) at most 48 rows name the same one
- cotangent: bfloat16 [4, 8, 128, 1664], P('segment', 'expert'), may hold values from -6 to 6
- first_gain: float32 [1664], replicated, may hold values from 0.25 to 1.75
- in_projection: bfloat16 [1664, 2496], replicated, may hold values from -0.3125 to 0.3125
- out_projection: bfloat16 [832, 1664], replicated, may hold values from -0.21875 to 0.21875
- second_gain: float32 [1664], replicated, may hold values from 0.25 to 1.75
- router_weight: bfloat16 [1664, 8], replicated, may hold values from -0.15625 to 0.15625
- up_weight: bfloat16 [4, 8, 1664, 1024], P('segment', 'expert'), may hold values from -0.15625 to 0.15625
- down_weight: bfloat16 [4, 8, 1024, 1664], P('segment', 'expert'), may hold values from -0.09375 to 0.09375
Outputs:
- layer_out: bfloat16 [4, 8, 128, 1664], P('segment', 'expert')
- input_grad: bfloat16 [4, 8, 128, 1664], P('segment', 'expert')
The draws below stay inside these ranges and needn't reach their ends.
Inputs may be any that keep to these rules, and one draw needn't show every extreme that they name: `route_ids`: the 2 experts of a token differ; among the 128 tokens of one image no expert is named more than 48 times, and in every draw some image names some expert exactly 48 times.
All inputs are finite; a program needn't handle non-finite values.
Results may differ from the reference program's by a relative error of at most 0.023.
Values may be sent and summed in bfloat16 or wider, within the bound.
No kernel may reach another device: no remote copies, remote signals or barrier semaphores. Data moves between devices by JAX's collectives and lax.ppermute only.
A program may use at most 128 MiB of HBM per device.

```python
import math
from functools import partial
import jax
import jax.numpy as jnp
import numpy as np
from jax import lax

D = 1664
HEADS = 8
HD = 104
FF = 4096
PARTS_SIZE = 4
TOP = 2
SEQ = 128
SECTIONS = 4
IMAGES = 8
EXP_SEC = 2
EXPERTS = 8
FFQ = 1024
CAP = 48
N_EXPERT = 8


def steps_of(stream_key, dims, split, low, largest):
    def one(axis_at, blocks):
        heights = jax.random.uniform(jax.random.fold_in(jax.random.fold_in(stream_key, 6), axis_at), (blocks,), jnp.float32, low / len(split), largest / len(split))
        return jnp.repeat(jnp.exp(heights), dims[axis_at] // blocks).reshape((-1,) + (1,) * (len(dims) - axis_at - 1))

    gain = one(*split[0])
    for cut in split[1:]:
        gain = gain * one(*cut)
    return gain


def deal_out(stream_key, own, number, rows, number_of, top, most, slope):
    sequence = jax.random.permutation(stream_key, number_of)
    heavy_load, usual = shares(number_of, rows * top, most, slope, True), shares(number_of, rows * top, most, slope, False)
    places = jnp.arange(number_of)

    def named(lengths, rotation):
        used = int((lengths > 0).sum())
        fixed = max(1, used // 4)
        moved = fixed + (places - fixed + rotation * (used - fixed)) % max(1, number_of - fixed)
        return jnp.zeros((number_of,), jnp.int32).at[sequence[jnp.where(places < fixed, places, moved)]].set(jnp.asarray(lengths, jnp.int32))

    lengths = jnp.where(number % 4 == 0, named(heavy_load, number // 4), named(usual, number - number // 4 - 1))
    mixed = jax.random.permutation(jax.random.fold_in(own, 3), number_of)
    donor, sink = mixed[0:number_of // 2 * 2:2], mixed[1:number_of // 2 * 2:2]
    room = jnp.minimum(lengths[donor] - 1, most - lengths[sink]) // 2
    room = jnp.where((donor == sequence[0]) | (sink == sequence[0]) | (lengths[sink] == 0), 0, jnp.maximum(room, 0))
    moved = jax.random.randint(jax.random.fold_in(own, 4), (number_of // 2,), 0, 1 << 20) % (room + 1)
    lengths = lengths.at[donor].add(-moved).at[sink].add(moved)
    labels = jnp.searchsorted(jnp.cumsum(lengths), jnp.arange(rows * top), side="right").astype(jnp.int32)
    grid = labels.reshape(top, rows).T
    grid = grid[jax.random.permutation(jax.random.fold_in(own, 1), rows)]
    rotation = jax.random.randint(jax.random.fold_in(own, 2), (rows, 1), 0, top)
    return jnp.take_along_axis(grid, (jnp.arange(top)[None, :] + rotation) % top, axis=1)


def shares(number_of, total, limit, slope, full):
    portions = [(1 << 20) // math.isqrt(grade ** slope) + 1 for grade in range(1, number_of + 1)]
    largest = limit if full else min(limit, max(-(-total // number_of), total * portions[0] // sum(portions)))
    least = 1 if total - largest >= number_of - 1 else 0
    holding, surplus = [largest] + [least] * (number_of - 1), total - largest - least * (number_of - 1)
    while surplus > 0:
        candidates = [i for i in range(1, number_of) if holding[i] < largest] or [i for i in range(1, number_of) if holding[i] < limit]
        whole, remaining = sum([portions[i] for i in candidates]), surplus
        for i in candidates:
            extra = min(limit - holding[i], max(1, remaining * portions[i] // whole), surplus)
            holding[i] = holding[i] + extra
            surplus = surplus - extra
    return np.array(holding)


def noise(rng, extent, scale, limit, split=(), kind=jnp.bfloat16):
    factor_of = steps_of(rng, extent, split, -0.22, 0.18) if split else 1.0
    array = jax.random.normal(rng, extent, jnp.float32) * scale * factor_of
    return jnp.minimum(jnp.maximum(array, -limit), limit).astype(kind)


def setup_inputs(seed: int = 0) -> dict:
    streams_of = jax.random.split(jax.random.key(seed), 11)
    tokens = noise(streams_of[0], (SECTIONS, IMAGES, SEQ, D), 1.0, 6.0, ((0, 4), (1, 8)))
    route_ids_keys = jax.random.split(jax.random.fold_in(streams_of[1], 1), SECTIONS * IMAGES * SEQ // SEQ)
    route_ids_turns = jax.random.permutation(jax.random.fold_in(streams_of[1], 3), SECTIONS * IMAGES * SEQ // SEQ)
    route_ids = jax.vmap(lambda own, number: deal_out(jax.random.fold_in(streams_of[1], 2), own, number, SEQ, EXPERTS, TOP, CAP, 2))(route_ids_keys, route_ids_turns).reshape((SECTIONS, IMAGES, SEQ, TOP))
    cotangent = noise(streams_of[2], (SECTIONS, IMAGES, SEQ, D), 1.0, 6.0, ((0, 4), (1, 8)))
    first_gain = jnp.clip(1.0 + 0.15 * jax.random.normal(streams_of[3], (D,), jnp.float32), 0.25, 1.75)
    in_projection = noise(streams_of[4], (D, 3 * HEADS * HD), (D // 4) ** -0.5, 0.3125)
    out_projection = noise(streams_of[5], (HEADS * HD, D), (HEADS * HD) ** -0.5, 0.21875)
    second_gain = jnp.clip(1.0 + 0.15 * jax.random.normal(streams_of[6], (D,), jnp.float32), 0.25, 1.75)
    router_weight = noise(streams_of[7], (D, EXPERTS), D ** -0.5, 0.15625)
    up_weight = noise(streams_of[8], (SECTIONS, N_EXPERT, D, FFQ), D ** -0.5, 0.15625, ((0, 4), (1, 8)))
    down_weight = noise(streams_of[9], (SECTIONS, N_EXPERT, FFQ, D), FF ** -0.5, 0.09375, ((0, 4), (1, 8)))
    return dict(tokens=tokens, route_ids=route_ids, cotangent=cotangent, first_gain=first_gain, in_projection=in_projection, out_projection=out_projection, second_gain=second_gain, router_weight=router_weight, up_weight=up_weight, down_weight=down_weight)


EPSILON = 1e-06
ROOT_HALF = 0.7071067811865476
INV_ROOT_TWO_PI = 0.3989422804014327
HIGHEST = lax.Precision.HIGHEST

def layer_norm(row_block, gain_vector):
    center = row_block - lax.optimization_barrier(jnp.mean(row_block, axis=-1, keepdims=True))
    spread = lax.optimization_barrier(jnp.mean(center * center, axis=-1, keepdims=True))
    return center * lax.rsqrt(spread + EPSILON) * gain_vector

def gelu_exact(preact):
    return 0.5 * preact * (1.0 + lax.erf(preact * ROOT_HALF))

def gelu_slope(preact):
    return 0.5 * (1.0 + lax.erf(preact * ROOT_HALF)) + preact * INV_ROOT_TWO_PI * jnp.exp(-0.5 * preact * preact)

def round_half(values):
    return lax.optimization_barrier(values.astype(jnp.bfloat16)).astype(jnp.float32)

def attention_branch(picture, first_gain, in_projection, out_projection):
    head_width = HEADS * HD
    normed = layer_norm(picture, first_gain).astype(jnp.bfloat16)
    joined = jnp.dot(normed, in_projection, preferred_element_type=jnp.float32).astype(jnp.bfloat16)
    queries = joined[:, :head_width].reshape(SEQ, HEADS, HD).astype(jnp.float32)
    key_rows = joined[:, head_width:2 * head_width].reshape(SEQ, HEADS, HD).astype(jnp.float32)
    value_rows = joined[:, 2 * head_width:].reshape(SEQ, HEADS, HD).astype(jnp.float32)
    scores = jnp.einsum('qhd,khd->hqk', queries, key_rows, precision=HIGHEST) * HD ** (-0.5)
    weights = jnp.exp(scores)
    attention = (weights / lax.optimization_barrier(jnp.sum(weights, axis=-1, keepdims=True))).astype(jnp.bfloat16)
    context = jnp.einsum('hqk,khd->qhd', attention.astype(jnp.float32), value_rows, precision=HIGHEST).astype(jnp.bfloat16)
    return picture + jnp.dot(context.reshape(SEQ, head_width), out_projection, preferred_element_type=jnp.float32)

def reference(tokens, route_ids, cotangent, first_gain, in_projection, out_projection, second_gain, router_weight, up_weight, down_weight):
    blocks = SECTIONS * IMAGES
    routes = SEQ * TOP
    pictures = tokens.reshape(blocks, SEQ, D).astype(jnp.float32)
    upstream = cotangent.reshape(blocks, SEQ, D).astype(jnp.float32)
    chosen = route_ids.reshape(blocks, SEQ, TOP)
    flat_ids = chosen.reshape(blocks, routes)

    def branch(row_block):
        return jax.vmap(lambda single: attention_branch(single, first_gain, in_projection, out_projection))(row_block)
    residual, attention_back = jax.vjp(branch, pictures)
    normed, norm_back = jax.vjp(partial(layer_norm, gain_vector=second_gain), residual)
    router_input = normed.astype(jnp.bfloat16)
    logits = jnp.einsum('bsd,de->bse', router_input.astype(jnp.float32), router_weight.astype(jnp.float32), precision=HIGHEST)
    picked = jnp.take_along_axis(logits, chosen, axis=2)
    gate_values = 1.0 / (1.0 + jnp.exp(picked[:, :, ::-1] - picked))
    route_grad = (gate_values[:, :, :, None] * upstream[:, :, None, :]).astype(jnp.bfloat16).reshape(blocks, routes, D)
    onehot = (flat_ids[:, :, None] == jnp.arange(EXPERTS, dtype=jnp.int32)[None, None, :]).astype(jnp.int32)
    slot_index = lax.optimization_barrier(jnp.sum(jnp.cumsum(onehot, axis=1) * onehot, axis=2)) - 1
    mixed_wide = router_input.astype(jnp.float32)
    grad_wide = route_grad.astype(jnp.float32)

    def per_expert(state_pair, expert):
        picked_out, expert_grad = state_pair
        section = (expert // EXP_SEC).astype(jnp.int32)
        first_part = (expert % EXP_SEC * PARTS_SIZE).astype(jnp.int32)
        up_parts = lax.dynamic_slice_in_dim(lax.dynamic_index_in_dim(up_weight, section, 0, keepdims=False), first_part, PARTS_SIZE, 0)
        down_parts = lax.dynamic_slice_in_dim(lax.dynamic_index_in_dim(down_weight, section, 0, keepdims=False), first_part, PARTS_SIZE, 0)
        hit = (flat_ids == expert)[:, None, :] & (slot_index[:, None, :] == jnp.arange(CAP, dtype=jnp.int32)[None, :, None])
        send_rows = hit.astype(jnp.float32)
        token_rows = lax.optimization_barrier(jnp.sum(send_rows.reshape(blocks, CAP, SEQ, TOP), axis=3))
        mixed_rows = jnp.einsum('bcs,bsd->bcd', token_rows, mixed_wide, precision=HIGHEST).astype(jnp.bfloat16).reshape(blocks * CAP, D)
        grad_rows = jnp.einsum('bcr,brd->bcd', send_rows, grad_wide, precision=HIGHEST).astype(jnp.bfloat16).reshape(blocks * CAP, D)
        out_sum = jnp.zeros((blocks * CAP, D), jnp.float32)
        in_sum = jnp.zeros((blocks * CAP, D), jnp.float32)
        for part_index in range(PARTS_SIZE):
            preact = jnp.dot(mixed_rows, up_parts[part_index], preferred_element_type=jnp.float32)
            hidden = gelu_exact(preact).astype(jnp.bfloat16)
            out_sum = out_sum + round_half(jnp.dot(hidden, down_parts[part_index], preferred_element_type=jnp.float32))
            slope_rows = jnp.dot(grad_rows, down_parts[part_index].T, preferred_element_type=jnp.float32) * gelu_slope(preact)
            hidden_grad = slope_rows.astype(jnp.bfloat16)
            in_sum = in_sum + round_half(jnp.dot(hidden_grad, up_parts[part_index].T, preferred_element_type=jnp.float32))
        expert_out = round_half(out_sum).reshape(blocks, CAP, D)
        picked_out = picked_out + jnp.einsum('bcr,bcd->brd', send_rows, expert_out, precision=HIGHEST)
        expert_grad = expert_grad + jnp.einsum('bcs,bcd->bsd', token_rows, in_sum.reshape(blocks, CAP, D), precision=HIGHEST)
        return ((picked_out, expert_grad), None)
    start = (jnp.zeros((blocks, routes, D), jnp.float32), jnp.zeros((blocks, SEQ, D), jnp.float32))
    (picked_out, expert_grad), unused = lax.scan(per_expert, start, jnp.arange(EXPERTS, dtype=jnp.int32))
    picked_out = picked_out.reshape(blocks, SEQ, TOP, D)
    expert_total = lax.optimization_barrier(jnp.sum(gate_values[:, :, :, None] * picked_out, axis=2))
    layer_out = (residual + expert_total).astype(jnp.bfloat16)
    gate_grad = lax.optimization_barrier(jnp.sum(upstream[:, :, None, :] * picked_out, axis=3))
    logit_grad = gate_values * (gate_grad - lax.optimization_barrier(jnp.sum(gate_values * gate_grad, axis=2, keepdims=True)))
    choose_table = (chosen[:, :, :, None] == jnp.arange(EXPERTS, dtype=jnp.int32)[None, None, None, :]).astype(jnp.float32)
    spread_grad = lax.optimization_barrier(jnp.sum(logit_grad[:, :, :, None] * choose_table, axis=2))
    mixed_grad = expert_grad + jnp.einsum('bse,de->bsd', spread_grad, router_weight.astype(jnp.float32), precision=HIGHEST)
    residual_grad = upstream + norm_back(mixed_grad)[0]
    input_grad = attention_back(residual_grad)[0].astype(jnp.bfloat16)
    return (layer_out.reshape(SECTIONS, IMAGES, SEQ, D), input_grad.reshape(SECTIONS, IMAGES, SEQ, D))
```

```python
from functools import partial

import jax
import jax.numpy as jnp
from jax import lax
from jax.sharding import PartitionSpec as P

HD = 104
PARTS_SIZE = 4
TOP = 2


EPSILON = 1e-06
ROOT_HALF = 0.7071067811865476
INV_ROOT_TWO_PI = 0.3989422804014327


def layer_norm(row_block, gain_vector):
    center = row_block - jnp.mean(row_block, axis=-1, keepdims=True)
    spread = jnp.mean(center * center, axis=-1, keepdims=True)
    return center * lax.rsqrt(spread + EPSILON) * gain_vector


def gelu_parts(preact):
    half_cdf = 0.5 * (1.0 + lax.erf(preact * ROOT_HALF))
    slope = half_cdf + preact * INV_ROOT_TWO_PI * jnp.exp(-0.5 * preact * preact)
    return preact * half_cdf, slope


def attention_branch(picture, first_gain, in_projection, out_projection):
    seq_len = picture.shape[0]
    head_width = out_projection.shape[0]
    head_count = head_width // HD
    normed = layer_norm(picture, first_gain).astype(jnp.bfloat16)
    joined = jnp.dot(normed, in_projection, preferred_element_type=jnp.float32).astype(jnp.bfloat16)
    queries = joined[:, :head_width].reshape(seq_len, head_count, HD)
    key_rows = joined[:, head_width : 2 * head_width].reshape(seq_len, head_count, HD)
    value_rows = joined[:, 2 * head_width :].reshape(seq_len, head_count, HD)
    scores = jnp.einsum(
        "qhd,khd->hqk", queries, key_rows, preferred_element_type=jnp.float32
    ) * HD ** (-0.5)
    weights = jnp.exp(scores)
    attention = (weights / jnp.sum(weights, axis=-1, keepdims=True)).astype(jnp.bfloat16)
    context = jnp.einsum(
        "hqk,khd->qhd", attention, value_rows, preferred_element_type=jnp.float32
    ).astype(jnp.bfloat16)
    return picture + jnp.dot(
        context.reshape(seq_len, head_width), out_projection, preferred_element_type=jnp.float32
    )


def slot_of(hits):
    seq_len = hits.shape[-1]
    order = jnp.arange(seq_len)
    before = (order[:, None] < order[None, :]).astype(jnp.bfloat16)
    return jnp.dot(
        hits.astype(jnp.bfloat16), before, preferred_element_type=jnp.float32
    ).astype(jnp.int32)


def row_table(ids, experts_here, capacity):
    images, seq_len, _ = ids.shape
    hits = jnp.any(ids[None] == experts_here[:, None, None, None], axis=-1)
    sections = hits.shape[0]
    slots = slot_of(hits.reshape(-1, seq_len)).reshape(hits.shape)
    rows = slots + jnp.arange(images)[None, :, None] * capacity
    rows = jnp.where(hits, rows, -1).reshape(sections, 1, images * seq_len)
    return (rows == jnp.arange(images * capacity)[None, :, None]).astype(jnp.bfloat16)


def shards(
    tokens,
    route_ids,
    cotangent,
    first_gain,
    in_projection,
    out_projection,
    second_gain,
    router_weight,
    up_weight,
    down_weight,
):
    picture = tokens[0, 0].astype(jnp.float32)
    chosen = route_ids[0, 0]
    upstream = cotangent[0, 0]
    up_local = up_weight[0, 0]
    down_local = down_weight[0, 0]
    seq_len, width = picture.shape
    experts = router_weight.shape[1]
    sections = lax.axis_size("segment")
    members = lax.axis_size("expert")
    per_section = members // PARTS_SIZE
    capacity = 3 * seq_len // experts
    line = members // 2
    here = lax.axis_index("expert")
    section = lax.axis_index("segment")
    place, side = here // 2, here % 2
    group = here // PARTS_SIZE
    my_expert = section * per_section + group
    experts_here = jnp.arange(sections) * per_section + group

    def along(value, steps):
        pairs = [(j, (j + 2 * steps) % members) for j in range(members)]
        return lax.ppermute(value, "expert", pairs)

    def across(value):
        return lax.ppermute(value, "expert", [(j, j ^ 1) for j in range(members)])

    def deal(value):
        return lax.all_to_all(value, "segment", split_axis=0, concat_axis=0, tiled=True)

    half = line // 2
    chunks = [list(range(1, half + 1)), list(range(half + 1, line)) + [0]]

    all_ids = lax.all_gather(chosen, ("segment", "expert")).reshape(
        sections, members, seq_len, TOP
    )
    lane_ids = lax.dynamic_index_in_dim(all_ids, section, 0, keepdims=False)

    def sources(chunk):
        spots = (place - jnp.array(chunk)) % line
        return jnp.concatenate([2 * spots + side, 2 * spots + 1 - side])

    cot_dense = {0: upstream}
    for step in range(1, line):
        cot_dense[step] = along(upstream, step)
    tables, cot_rows = {}, {}
    for index in (1, 0):
        chunk = chunks[index]
        count = len(chunk)
        ids = jnp.take(lane_ids, sources(chunk), axis=0)
        tables[index] = (
            row_table(ids[:count], experts_here, capacity),
            row_table(ids[count:], experts_here, capacity),
        )
        dense = jnp.concatenate([cot_dense[step] for step in chunk], axis=0)
        packed = jnp.einsum(
            "srt,td->srd", tables[index][0], dense, preferred_element_type=jnp.float32
        ).astype(jnp.bfloat16)
        mine = deal(packed)
        cot_rows[index] = jnp.stack([mine, across(mine)], axis=1)

    def branch(row_block):
        return attention_branch(row_block, first_gain, in_projection, out_projection)

    residual, attention_back = jax.vjp(branch, picture)
    normed, norm_back = jax.vjp(partial(layer_norm, gain_vector=second_gain), residual)
    mixed = normed.astype(jnp.bfloat16)
    own_logits = jnp.dot(mixed, router_weight, preferred_element_type=jnp.float32)

    mixed_dense = {0: mixed}
    for step in range(1, line):
        mixed_dense[step] = along(mixed, step)

    out_dense, grad_dense, scores = {}, {}, {}
    for index in (0, 1):
        chunk = chunks[index]
        count = len(chunk)
        rows = count * capacity
        near, far = tables[index]
        dense = jnp.concatenate([mixed_dense[step] for step in chunk], axis=0)
        dense_far = across(dense)
        packed = jnp.stack(
            [
                jnp.einsum("srt,td->srd", table, block, preferred_element_type=jnp.float32)
                for table, block in ((near, dense), (far, dense_far))
            ],
            axis=1,
        ).astype(jnp.bfloat16)
        mixed_rows = deal(packed).reshape(-1, width)
        grads_in = cot_rows[index].reshape(-1, width)

        ids = jnp.take(all_ids, sources(chunk), axis=1)
        hits = jnp.any(ids == my_expert, axis=-1)
        slots = jnp.where(
            hits, slot_of(hits.reshape(-1, seq_len)).reshape(hits.shape), -1
        )
        others = jnp.sum(ids, axis=-1) - my_expert
        slot_hits = slots[:, :, None, :] == jnp.arange(capacity)[None, None, :, None]
        slot_other = jnp.sum(jnp.where(slot_hits, others[:, :, None, :], 0), axis=-1).reshape(-1)

        logits = jnp.dot(mixed_rows, router_weight, preferred_element_type=jnp.float32)
        lanes = jnp.arange(experts)
        mine_logit = jnp.sum(jnp.where(lanes[None, :] == my_expert, logits, 0.0), axis=1)
        other_logit = jnp.sum(jnp.where(lanes[None, :] == slot_other[:, None], logits, 0.0), axis=1)
        gate = (1.0 / (1.0 + jnp.exp(other_logit - mine_logit)))[:, None]

        preact = jnp.dot(mixed_rows, up_local, preferred_element_type=jnp.float32)
        hidden_wide, slope = gelu_parts(preact)
        hidden = hidden_wide.astype(jnp.bfloat16)
        out_rows = (
            jnp.dot(hidden, down_local, preferred_element_type=jnp.float32) * gate
        ).astype(jnp.bfloat16)
        pulled = (
            jnp.einsum("rd,fd->rf", grads_in, down_local, preferred_element_type=jnp.float32)
            * gate
        )
        scores[index] = jnp.sum(hidden.astype(jnp.float32) * pulled, axis=1)
        hidden_grad = (pulled * slope).astype(jnp.bfloat16)
        grad_rows = jnp.einsum(
            "rf,df->rd", hidden_grad, up_local, preferred_element_type=jnp.float32
        ).astype(jnp.bfloat16)

        out_rows = out_rows.reshape(sections, 2, rows, width)
        met = across(out_rows[:, 1])
        summed = (out_rows[:, 0].astype(jnp.float32) + met.astype(jnp.float32)).astype(jnp.bfloat16)
        back = deal(summed)
        out_block = jnp.einsum(
            "srt,srd->td", near, back, preferred_element_type=jnp.float32
        )
        back = deal(grad_rows.reshape(sections, 2, rows, width))
        grad_far = jnp.einsum(
            "srt,srd->td", far, back[:, 1], preferred_element_type=jnp.float32
        ).astype(jnp.bfloat16)
        grad_near = jnp.einsum("srt,srd->td", near, back[:, 0], preferred_element_type=jnp.float32)
        grad_block = grad_near + across(grad_far).astype(jnp.float32)
        for spot, step in enumerate(chunk):
            part_out = out_block[spot * seq_len : (spot + 1) * seq_len]
            part_grad = grad_block[spot * seq_len : (spot + 1) * seq_len]
            if step:
                part_out = along(part_out.astype(jnp.bfloat16), -step)
                part_grad = along(part_grad.astype(jnp.bfloat16), -step)
            out_dense[step] = part_out
            grad_dense[step] = part_grad

    expert_total = sum(out_dense[step].astype(jnp.float32) for step in range(line))
    input_total = sum(grad_dense[step].astype(jnp.float32) for step in range(line))
    layer_out = (residual + expert_total).astype(jnp.bfloat16)

    score_table = jnp.concatenate(
        [scores[index].reshape(sections, 2, len(chunks[index]), capacity) for index in (0, 1)],
        axis=2,
    )
    spot_of = {step: spot for spot, step in enumerate(chunks[0] + chunks[1])}
    spots = jnp.array([spot_of[step] for step in range(line)])
    all_scores = lax.all_gather(score_table, ("segment", "expert")).reshape(
        sections, members, sections, 2, line, capacity
    )
    all_scores = lax.dynamic_index_in_dim(all_scores, section, 2, keepdims=False)
    member = jnp.arange(members)
    pick_side = (member % 2 != side).astype(jnp.int32)
    pick_spot = spots[(member // 2 - place) % line]
    picked = all_scores[:, member, pick_side, pick_spot]
    expert_scores = jnp.sum(
        picked.reshape(sections, per_section, PARTS_SIZE, capacity), axis=2
    ).reshape(experts, capacity)
    expert_list = jnp.arange(experts)
    named = chosen[:, :, None] == expert_list
    hits = jnp.any(named, axis=1)
    own_slots = slot_of(hits.T)
    at_slot = (own_slots[:, :, None] == jnp.arange(capacity)) & hits.T[:, :, None]
    token_scores = jnp.sum(jnp.where(at_slot, expert_scores[:, None, :], 0.0), axis=2).T
    picked_logit = jnp.sum(jnp.where(named, own_logits[:, None, :], 0.0), axis=2)
    gate_values = 1.0 / (1.0 + jnp.exp(picked_logit[:, ::-1] - picked_logit))
    gate_spread = jnp.sum(jnp.where(named, gate_values[:, :, None], 0.0), axis=1)
    spread_grad = token_scores - gate_spread * jnp.sum(token_scores, axis=1, keepdims=True)
    mixed_grad = input_total + jnp.einsum(
        "se,de->sd", spread_grad, router_weight.astype(jnp.float32), precision=lax.Precision.HIGHEST
    )
    residual_grad = upstream.astype(jnp.float32) + norm_back(mixed_grad)[0]
    input_grad = attention_back(residual_grad)[0].astype(jnp.bfloat16)
    return (layer_out[None, None], input_grad[None, None])


def solution(mesh):
    placed = (
        P("segment", "expert", None, None),
        P("segment", "expert", None, None),
        P("segment", "expert", None, None),
        P(),
        P(),
        P(),
        P(),
        P(),
        P("segment", "expert", None, None),
        P("segment", "expert", None, None),
    )
    return jax.shard_map(
        shards,
        mesh=mesh,
        in_specs=placed,
        out_specs=(P("segment", "expert", None, None), P("segment", "expert", None, None)),
        check_vma=False,
    )
```

```python
from functools import partial

import jax
import jax.numpy as jnp
from jax import lax
from jax.sharding import PartitionSpec as P

HD = 104
PARTS_SIZE = 4
TOP = 2


EPSILON = 1e-06
ROOT_HALF = 0.7071067811865476
INV_ROOT_TWO_PI = 0.3989422804014327


def layer_norm(row_block, gain_vector):
    center = row_block - jnp.mean(row_block, axis=-1, keepdims=True)
    spread = jnp.mean(center * center, axis=-1, keepdims=True)
    return center * lax.rsqrt(spread + EPSILON) * gain_vector


def gelu_parts(preact):
    half_cdf = 0.5 * (1.0 + lax.erf(preact * ROOT_HALF))
    slope = half_cdf + preact * INV_ROOT_TWO_PI * jnp.exp(-0.5 * preact * preact)
    return preact * half_cdf, slope


def attention_branch(picture, first_gain, in_projection, out_projection):
    seq_len = picture.shape[0]
    head_width = out_projection.shape[0]
    head_count = head_width // HD
    normed = layer_norm(picture, first_gain).astype(jnp.bfloat16)
    joined = jnp.dot(normed, in_projection, preferred_element_type=jnp.float32).astype(jnp.bfloat16)
    queries = joined[:, :head_width].reshape(seq_len, head_count, HD)
    key_rows = joined[:, head_width : 2 * head_width].reshape(seq_len, head_count, HD)
    value_rows = joined[:, 2 * head_width :].reshape(seq_len, head_count, HD)
    scores = jnp.einsum(
        "qhd,khd->hqk", queries, key_rows, preferred_element_type=jnp.float32
    ) * HD ** (-0.5)
    weights = jnp.exp(scores)
    attention = (weights / jnp.sum(weights, axis=-1, keepdims=True)).astype(jnp.bfloat16)
    context = jnp.einsum(
        "hqk,khd->qhd", attention, value_rows, preferred_element_type=jnp.float32
    ).astype(jnp.bfloat16)
    return picture + jnp.dot(
        context.reshape(seq_len, head_width), out_projection, preferred_element_type=jnp.float32
    )


def slot_of(hits):
    seq_len = hits.shape[-1]
    order = jnp.arange(seq_len)
    before = (order[:, None] < order[None, :]).astype(jnp.bfloat16)
    return jnp.dot(
        hits.astype(jnp.bfloat16), before, preferred_element_type=jnp.float32
    ).astype(jnp.int32)


def row_table(ids, experts_here, capacity):
    images, seq_len, _ = ids.shape
    hits = jnp.any(ids[None] == experts_here[:, None, None, None], axis=-1)
    sections = hits.shape[0]
    slots = slot_of(hits.reshape(-1, seq_len)).reshape(hits.shape)
    rows = slots + jnp.arange(images)[None, :, None] * capacity
    rows = jnp.where(hits, rows, -1).reshape(sections, 1, images * seq_len)
    return (rows == jnp.arange(images * capacity)[None, :, None]).astype(jnp.bfloat16)


def shards(
    tokens,
    route_ids,
    cotangent,
    first_gain,
    in_projection,
    out_projection,
    second_gain,
    router_weight,
    up_weight,
    down_weight,
):
    picture = tokens[0, 0].astype(jnp.float32)
    chosen = route_ids[0, 0]
    upstream = cotangent[0, 0]
    up_local = up_weight[0, 0]
    down_local = down_weight[0, 0]
    seq_len, width = picture.shape
    experts = router_weight.shape[1]
    sections = lax.axis_size("segment")
    members = lax.axis_size("expert")
    per_section = members // PARTS_SIZE
    capacity = 3 * seq_len // experts
    line = members // 2
    here = lax.axis_index("expert")
    section = lax.axis_index("segment")
    place, side = here // 2, here % 2
    group = here // PARTS_SIZE
    my_expert = section * per_section + group
    experts_here = jnp.arange(sections) * per_section + group

    def along(value, steps):
        pairs = [(j, (j + 2 * steps) % members) for j in range(members)]
        return lax.ppermute(value, "expert", pairs)

    def across(value):
        return lax.ppermute(value, "expert", [(j, j ^ 1) for j in range(members)])

    def deal(value):
        return lax.all_to_all(value, "segment", split_axis=0, concat_axis=0, tiled=True)

    half = line // 2
    chunks = [list(range(1, half + 1)), list(range(half + 1, line)) + [0]]

    lane_ids = lax.all_to_all(
        jnp.broadcast_to(chosen.reshape(1, seq_len * TOP), (members, seq_len * TOP)),
        "expert",
        split_axis=0,
        concat_axis=0,
        tiled=True,
    ).reshape(members, seq_len, TOP)

    def sources(steps):
        spots = (place - jnp.array(steps)) % line
        return jnp.concatenate([2 * spots + side, 2 * spots + 1 - side])

    def packed(table, dense):
        return jnp.einsum(
            "srt,td->srd", table, dense, preferred_element_type=jnp.float32
        ).astype(jnp.bfloat16)

    def unpacked(table, rows):
        return jnp.einsum("srt,srd->td", table, rows, preferred_element_type=jnp.float32)

    order = chunks[0] + chunks[1]
    ids = jnp.take(lane_ids, sources(order), axis=0)
    hits = jnp.any(ids[None] == experts_here[:, None, None, None], axis=-1)
    slots = slot_of(hits.reshape(-1, seq_len)).reshape(hits.shape)
    slots = jnp.where(hits, slots, -1)
    others = jnp.sum(ids, axis=-1)[None] - experts_here[:, None, None]
    at_slot = slots[:, :, None, :] == jnp.arange(capacity)[None, None, :, None]
    slot_other = deal(jnp.sum(jnp.where(at_slot, others[:, :, None, :], 0), axis=-1))
    slot_other = slot_other.reshape(sections, 2, line, capacity)

    cot_dense = {0: upstream}
    for step in range(1, line):
        cot_dense[step] = along(upstream, step)
    tables, cot_rows = {}, {}
    for index in (1, 0):
        chunk = chunks[index]
        count = len(chunk)
        chunk_ids = jnp.take(lane_ids, sources(chunk), axis=0)
        tables[index, 0] = row_table(chunk_ids[:count], experts_here, capacity)
        tables[index, 1] = row_table(chunk_ids[count:], experts_here, capacity)
        dense = jnp.concatenate([cot_dense[step] for step in chunk], axis=0)
        cot_rows[index, 0] = deal(packed(tables[index, 0], dense))
        cot_rows[index, 1] = across(cot_rows[index, 0])

    def branch(row_block):
        return attention_branch(row_block, first_gain, in_projection, out_projection)

    residual, attention_back = jax.vjp(branch, picture)
    normed, norm_back = jax.vjp(partial(layer_norm, gain_vector=second_gain), residual)
    mixed = normed.astype(jnp.bfloat16)
    own_logits = jnp.dot(mixed, router_weight, preferred_element_type=jnp.float32)

    mixed_dense = {0: mixed}
    for step in range(1, line):
        mixed_dense[step] = along(mixed, step)

    def expert_unit(mixed_rows, grads_in, other):
        logits = jnp.dot(mixed_rows, router_weight, preferred_element_type=jnp.float32)
        lanes = jnp.arange(experts)
        mine_logit = jnp.sum(jnp.where(lanes[None, :] == my_expert, logits, 0.0), axis=1)
        other_logit = jnp.sum(jnp.where(lanes[None, :] == other[:, None], logits, 0.0), axis=1)
        gate = (1.0 / (1.0 + jnp.exp(other_logit - mine_logit)))[:, None]
        preact = jnp.dot(mixed_rows, up_local, preferred_element_type=jnp.float32)
        hidden_wide, slope = gelu_parts(preact)
        hidden = hidden_wide.astype(jnp.bfloat16)
        out_rows = (
            jnp.dot(hidden, down_local, preferred_element_type=jnp.float32) * gate
        ).astype(jnp.bfloat16)
        pulled = (
            jnp.einsum("rd,fd->rf", grads_in, down_local, preferred_element_type=jnp.float32)
            * gate
        )
        score = jnp.sum(hidden.astype(jnp.float32) * pulled, axis=1)
        hidden_grad = (pulled * slope).astype(jnp.bfloat16)
        grad_rows = jnp.einsum(
            "rf,df->rd", hidden_grad, up_local, preferred_element_type=jnp.float32
        ).astype(jnp.bfloat16)
        return out_rows, grad_rows, score

    out_dense, grad_dense, scores = {}, {}, {}
    for index in (0, 1):
        chunk = chunks[index]
        count = len(chunk)
        start = 0 if index == 0 else len(chunks[0])
        dense = jnp.concatenate([mixed_dense[step] for step in chunk], axis=0)
        blocks = (dense, across(dense))
        shape = (sections, count * capacity, width)
        outs, grads = {}, {}
        for far in (0, 1):
            rows = deal(packed(tables[index, far], blocks[far])).reshape(-1, width)
            out_rows, grad_rows, score = expert_unit(
                rows,
                cot_rows[index, far].reshape(-1, width),
                slot_other[:, far, start : start + count].reshape(-1),
            )
            scores[index, far] = score.reshape(sections, count, capacity)
            outs[far] = out_rows.reshape(shape)
            grads[far] = unpacked(tables[index, far], deal(grad_rows.reshape(shape)))
        grad_block = grads[0] + across(grads[1].astype(jnp.bfloat16)).astype(jnp.float32)
        summed = (outs[0].astype(jnp.float32) + across(outs[1]).astype(jnp.float32)).astype(
            jnp.bfloat16
        )
        out_block = unpacked(tables[index, 0], deal(summed))
        for spot, step in enumerate(chunk):
            part_out = out_block[spot * seq_len : (spot + 1) * seq_len]
            part_grad = grad_block[spot * seq_len : (spot + 1) * seq_len]
            if step:
                part_out = along(part_out.astype(jnp.bfloat16), -step)
                part_grad = along(part_grad.astype(jnp.bfloat16), -step)
            out_dense[step] = part_out
            grad_dense[step] = part_grad

    expert_total = sum(out_dense[step].astype(jnp.float32) for step in range(line))
    input_total = sum(grad_dense[step].astype(jnp.float32) for step in range(line))
    layer_out = (residual + expert_total).astype(jnp.bfloat16)

    score_table = jnp.stack(
        [jnp.concatenate([scores[0, far], scores[1, far]], axis=1) for far in (0, 1)], axis=1
    )
    spot_of = {step: spot for spot, step in enumerate(order)}
    spots = jnp.array([spot_of[step] for step in range(line)])
    lane_scores = deal(score_table)
    member = jnp.arange(members)
    lane_scores = lane_scores[:, (member % 2 != side).astype(jnp.int32), spots[(place - member // 2) % line]]
    own_scores = lax.all_to_all(
        lane_scores.transpose(1, 0, 2), "expert", split_axis=0, concat_axis=0, tiled=True
    )
    expert_scores = (
        jnp.sum(own_scores.reshape(per_section, PARTS_SIZE, sections, capacity), axis=1)
        .transpose(1, 0, 2)
        .reshape(experts, capacity)
    )
    expert_list = jnp.arange(experts)
    named = chosen[:, :, None] == expert_list
    hits = jnp.any(named, axis=1)
    own_slots = slot_of(hits.T)
    at_slot = (own_slots[:, :, None] == jnp.arange(capacity)) & hits.T[:, :, None]
    token_scores = jnp.sum(jnp.where(at_slot, expert_scores[:, None, :], 0.0), axis=2).T
    picked_logit = jnp.sum(jnp.where(named, own_logits[:, None, :], 0.0), axis=2)
    gate_values = 1.0 / (1.0 + jnp.exp(picked_logit[:, ::-1] - picked_logit))
    gate_spread = jnp.sum(jnp.where(named, gate_values[:, :, None], 0.0), axis=1)
    spread_grad = token_scores - gate_spread * jnp.sum(token_scores, axis=1, keepdims=True)
    mixed_grad = input_total + jnp.einsum(
        "se,de->sd", spread_grad, router_weight.astype(jnp.float32), precision=lax.Precision.HIGHEST
    )
    residual_grad = upstream.astype(jnp.float32) + norm_back(mixed_grad)[0]
    input_grad = attention_back(residual_grad)[0].astype(jnp.bfloat16)
    return (layer_out[None, None], input_grad[None, None])


def solution(mesh):
    placed = (
        P("segment", "expert", None, None),
        P("segment", "expert", None, None),
        P("segment", "expert", None, None),
        P(),
        P(),
        P(),
        P(),
        P(),
        P("segment", "expert", None, None),
        P("segment", "expert", None, None),
    )
    return jax.shard_map(
        shards,
        mesh=mesh,
        in_specs=placed,
        out_specs=(P("segment", "expert", None, None), P("segment", "expert", None, None)),
        check_vma=False,
    )
```

```python
from functools import partial

import jax
import jax.numpy as jnp
from jax import lax
from jax.experimental import pallas as pl
from jax.experimental.pallas import tpu as pltpu
from jax.sharding import PartitionSpec as P

HD = 104
PARTS_SIZE = 4
TOP = 2


EPSILON = 1e-06
ROOT_HALF = 0.7071067811865476
INV_ROOT_TWO_PI = 0.3989422804014327


def layer_norm(row_block, gain_vector):
    center = row_block - jnp.mean(row_block, axis=-1, keepdims=True)
    spread = jnp.mean(center * center, axis=-1, keepdims=True)
    return center * lax.rsqrt(spread + EPSILON) * gain_vector


def gelu_parts(preact):
    half_cdf = 0.5 * (1.0 + lax.erf(preact * ROOT_HALF))
    slope = half_cdf + preact * INV_ROOT_TWO_PI * jnp.exp(-0.5 * preact * preact)
    return preact * half_cdf, slope


def attention_branch(picture, first_gain, in_projection, out_projection):
    seq_len = picture.shape[0]
    head_width = out_projection.shape[0]
    head_count = head_width // HD
    normed = layer_norm(picture, first_gain).astype(jnp.bfloat16)
    joined = jnp.dot(normed, in_projection, preferred_element_type=jnp.float32).astype(jnp.bfloat16)
    queries = joined[:, :head_width].reshape(seq_len, head_count, HD)
    key_rows = joined[:, head_width : 2 * head_width].reshape(seq_len, head_count, HD)
    value_rows = joined[:, 2 * head_width :].reshape(seq_len, head_count, HD)
    scores = jnp.einsum(
        "qhd,khd->hqk", queries, key_rows, preferred_element_type=jnp.float32
    ) * HD ** (-0.5)
    weights = jnp.exp(scores)
    attention = (weights / jnp.sum(weights, axis=-1, keepdims=True)).astype(jnp.bfloat16)
    context = jnp.einsum(
        "hqk,khd->qhd", attention, value_rows, preferred_element_type=jnp.float32
    ).astype(jnp.bfloat16)
    return picture + jnp.dot(
        context.reshape(seq_len, head_width), out_projection, preferred_element_type=jnp.float32
    )


def slot_of(hits):
    seq_len = hits.shape[-1]
    order = jnp.arange(seq_len)
    before = (order[:, None] < order[None, :]).astype(jnp.bfloat16)
    return jnp.dot(
        hits.astype(jnp.bfloat16), before, preferred_element_type=jnp.float32
    ).astype(jnp.int32)


def slot_rows(ids, experts_here, capacity):
    images, seq_len, _ = ids.shape
    hits = jnp.any(ids[None] == experts_here[:, None, None, None], axis=-1)
    slots = slot_of(hits.reshape(-1, seq_len)).reshape(hits.shape)
    rows = slots + jnp.arange(images)[None, :, None] * capacity
    return jnp.where(hits, rows, -1).reshape(hits.shape[0], images * seq_len)


def params():
    return pltpu.CompilerParams(vmem_limit_bytes=48 * 1024 * 1024)


def cost(flops, moved):
    return pl.CostEstimate(flops=int(flops), bytes_accessed=int(moved), transcendentals=0)


def pack_kernel(images, sections, *refs):
    rows_ref = refs[0]
    dense = refs[1 : 1 + images]
    blocks = refs[1 + images :]
    count = blocks[0].shape[0]
    seq_len = dense[0].shape[0]
    for d in range(sections):
        target = rows_ref[d : d + 1, :]
        lanes = lax.broadcasted_iota(jnp.int32, (count, images * seq_len), 0)
        table = jnp.where(lanes == target, 1.0, 0.0).astype(jnp.bfloat16)
        total = None
        for i in range(images):
            part = jnp.dot(
                table[:, i * seq_len : (i + 1) * seq_len],
                dense[i][...],
                preferred_element_type=jnp.float32,
            )
            total = part if total is None else total + part
        blocks[d][...] = total.astype(jnp.bfloat16)


def pack(rows, dense, capacity):
    sections = rows.shape[0]
    seq_len, width = dense[0].shape
    images = len(dense)
    count = images * capacity
    return pl.pallas_call(
        partial(pack_kernel, images, sections),
        out_shape=[jax.ShapeDtypeStruct((count, width), jnp.bfloat16)] * sections,
        compiler_params=params(),
        cost_estimate=cost(
            2 * sections * count * images * seq_len * width,
            2 * width * (images * seq_len + sections * count),
        ),
    )(rows, *dense)


def unpack_kernel(images, sections, extra, *refs):
    rows_ref = refs[0]
    blocks = refs[1 : 1 + sections]
    addend = refs[1 + sections : 1 + sections + extra]
    dense = refs[1 + sections + extra :]
    count = blocks[0].shape[0]
    seq_len = dense[0].shape[0]
    for i in range(images):
        total = None
        for d in range(sections):
            target = rows_ref[i * seq_len : (i + 1) * seq_len, d : d + 1]
            lanes = lax.broadcasted_iota(jnp.int32, (seq_len, count), 1)
            table = jnp.where(lanes == target, 1.0, 0.0).astype(jnp.bfloat16)
            part = jnp.dot(table, blocks[d][...], preferred_element_type=jnp.float32)
            total = part if total is None else total + part
        if extra:
            total = total + addend[i][...].astype(jnp.float32)
        dense[i][...] = total.astype(jnp.bfloat16)


def unpack(rows, blocks, images, addend=()):
    sections = rows.shape[0]
    seq_len = rows.shape[1] // images
    count, width = blocks[0].shape
    return pl.pallas_call(
        partial(unpack_kernel, images, sections, len(addend)),
        out_shape=[jax.ShapeDtypeStruct((seq_len, width), jnp.bfloat16)] * images,
        compiler_params=params(),
        cost_estimate=cost(
            2 * sections * count * images * seq_len * width,
            2 * width * (images * seq_len * 2 + sections * count),
        ),
    )(rows.T, *blocks, *addend)


def expert_kernel(sections, split, *refs):
    expert_ref, other_ref, router_ref = refs[:3]
    mixed_in = refs[3 : 3 + sections]
    grads_in = refs[3 + sections : 3 + 2 * sections]
    up_ref, down_ref = refs[3 + 2 * sections : 5 + 2 * sections]
    outs = refs[5 + 2 * sections :]
    out_parts, grad_parts, score_ref = outs[:split], outs[split : split + sections], outs[split + sections]
    mixed, grads, out_sum, grad_sum, gate_ref = outs[split + sections + 1 :]
    step, last = pl.program_id(0), pl.num_programs(0) - 1
    count = mixed_in[0].shape[0]
    total = count * sections

    @pl.when(step == 0)
    def _():
        for d in range(sections):
            mixed[d * count : (d + 1) * count, :] = mixed_in[d][...]
            grads[d * count : (d + 1) * count, :] = grads_in[d][...]
        logits = jnp.dot(mixed[...], router_ref[...], preferred_element_type=jnp.float32)
        lanes = lax.broadcasted_iota(jnp.int32, logits.shape, 1)
        mine = jnp.sum(jnp.where(lanes == expert_ref[0], logits, 0.0), axis=1, keepdims=True)
        other = jnp.sum(jnp.where(lanes == other_ref[...], logits, 0.0), axis=1, keepdims=True)
        gate_ref[...] = 1.0 / (1.0 + jnp.exp(other - mine))
        out_sum[...] = jnp.zeros_like(out_sum)
        grad_sum[...] = jnp.zeros_like(grad_sum)
        score_ref[...] = jnp.zeros_like(score_ref)

    gate = gate_ref[...]
    preact = jnp.dot(mixed[...], up_ref[...], preferred_element_type=jnp.float32)
    pulled = gate * lax.dot_general(
        grads[...], down_ref[...], (((1,), (1,)), ((), ())), preferred_element_type=jnp.float32
    )
    hidden_wide, slope = gelu_parts(preact)
    hidden = hidden_wide.astype(jnp.bfloat16)
    hidden_grad = (pulled * slope).astype(jnp.bfloat16)
    score_ref[...] += jnp.sum(hidden_wide * pulled, axis=1, keepdims=True)
    out_sum[...] += jnp.dot(hidden, down_ref[...], preferred_element_type=jnp.float32)
    grad_sum[...] += lax.dot_general(
        hidden_grad, up_ref[...], (((1,), (1,)), ((), ())), preferred_element_type=jnp.float32
    )

    @pl.when(step == last)
    def _():
        size = total // split
        for part in range(split):
            rows = slice(part * size, (part + 1) * size)
            out_parts[part][...] = (out_sum[rows, :] * gate[rows, :]).astype(jnp.bfloat16)
        for d in range(sections):
            grad_parts[d][...] = grad_sum[d * count : (d + 1) * count, :].astype(jnp.bfloat16)


def expert_unit(expert, other, router, mixed_in, grads_in, up_local, down_local, split):
    sections = len(mixed_in)
    count, width = mixed_in[0].shape
    total = count * sections
    hidden_units = up_local.shape[1]
    tile = 512 if hidden_units % 512 == 0 else hidden_units

    def whole(shape):
        return pl.BlockSpec(shape, lambda f: (0,) * len(shape))

    block = whole((count, width))
    results = pl.pallas_call(
        partial(expert_kernel, sections, split),
        grid=(hidden_units // tile,),
        in_specs=[
            pl.BlockSpec(memory_space=pltpu.SMEM),
            whole((total, 1)),
            whole(router.shape),
        ]
        + [block] * (2 * sections)
        + [
            pl.BlockSpec((width, tile), lambda f: (0, f)),
            pl.BlockSpec((tile, width), lambda f: (f, 0)),
        ],
        out_specs=[whole((total // split, width))] * split + [block] * sections + [whole((total, 1))],
        out_shape=[jax.ShapeDtypeStruct((total // split, width), jnp.bfloat16)] * split
        + [jax.ShapeDtypeStruct((count, width), jnp.bfloat16)] * sections
        + [jax.ShapeDtypeStruct((total, 1), jnp.float32)],
        scratch_shapes=[
            pltpu.VMEM((total, width), jnp.bfloat16),
            pltpu.VMEM((total, width), jnp.bfloat16),
            pltpu.VMEM((total, width), jnp.float32),
            pltpu.VMEM((total, width), jnp.float32),
            pltpu.VMEM((total, 1), jnp.float32),
        ],
        compiler_params=params(),
        cost_estimate=cost(
            8 * total * width * hidden_units,
            4 * width * hidden_units + 8 * total * width,
        ),
    )(expert, other, router, *mixed_in, *grads_in, up_local, down_local)
    return results[:split], results[split : split + sections], results[split + sections]


def shards(
    tokens,
    route_ids,
    cotangent,
    first_gain,
    in_projection,
    out_projection,
    second_gain,
    router_weight,
    up_weight,
    down_weight,
):
    picture = tokens[0, 0].astype(jnp.float32)
    chosen = route_ids[0, 0]
    upstream = cotangent[0, 0]
    up_local = up_weight[0, 0]
    down_local = down_weight[0, 0]
    seq_len, width = picture.shape
    experts = router_weight.shape[1]
    sections = lax.axis_size("segment")
    members = lax.axis_size("expert")
    per_section = members // PARTS_SIZE
    capacity = 3 * seq_len // experts
    line = members // 2
    here = lax.axis_index("expert")
    section = lax.axis_index("segment")
    place, side = here // 2, here % 2
    group = here // PARTS_SIZE
    my_expert = section * per_section + group
    relative = section ^ jnp.arange(sections)
    experts_here = relative * per_section + group

    def along(value, steps):
        pairs = [(j, (j + 2 * steps) % members) for j in range(members)]
        return lax.ppermute(value, "expert", pairs)

    def across(value):
        return lax.ppermute(value, "expert", [(j, j ^ 1) for j in range(members)])

    def deal(blocks):
        moved = [blocks[0]]
        for d in range(1, sections):
            pairs = [(s, s ^ d) for s in range(sections)]
            moved.append(lax.ppermute(blocks[d], "segment", pairs))
        return moved

    def deal_small(value):
        return lax.all_to_all(
            jnp.take(value, relative, axis=0), "segment", split_axis=0, concat_axis=0, tiled=True
        )

    half = line // 2
    chunks = [list(range(1, half + 1)), list(range(half + 1, line)) + [0]]

    lane_ids = lax.all_to_all(
        jnp.broadcast_to(chosen.reshape(1, seq_len * TOP), (members, seq_len * TOP)),
        "expert",
        split_axis=0,
        concat_axis=0,
        tiled=True,
    ).reshape(members, seq_len, TOP)

    def sources(steps):
        spots = (place - jnp.array(steps)) % line
        return jnp.concatenate([2 * spots + side, 2 * spots + 1 - side])

    order = chunks[0] + chunks[1]
    ids = jnp.take(lane_ids, sources(order), axis=0)
    hits = jnp.any(ids[None] == experts_here[:, None, None, None], axis=-1)
    slots = slot_of(hits.reshape(-1, seq_len)).reshape(hits.shape)
    slots = jnp.where(hits, slots, -1)
    others = jnp.sum(ids, axis=-1)[None] - experts_here[:, None, None]
    at_slot = slots[:, :, None, :] == jnp.arange(capacity)[None, None, :, None]
    slot_other = deal_small(jnp.sum(jnp.where(at_slot, others[:, :, None, :], 0), axis=-1))
    slot_other = jnp.take(slot_other, relative, axis=0).reshape(sections, 2, line, capacity)

    cot_dense = {0: upstream}
    for step in range(1, line):
        cot_dense[step] = along(upstream, step)
    rows, cot_rows = {}, {}
    for index in (1, 0):
        chunk = chunks[index]
        count = len(chunk)
        chunk_ids = jnp.take(lane_ids, sources(chunk), axis=0)
        rows[index, 0] = slot_rows(chunk_ids[:count], experts_here, capacity)
        rows[index, 1] = slot_rows(chunk_ids[count:], experts_here, capacity)
        dense = [cot_dense[step] for step in chunk]
        cot_rows[index, 0] = deal(pack(rows[index, 0], dense, capacity))
        cot_rows[index, 1] = [across(block) for block in cot_rows[index, 0]]

    def branch(row_block):
        return attention_branch(row_block, first_gain, in_projection, out_projection)

    residual, attention_back = jax.vjp(branch, picture)
    normed, norm_back = jax.vjp(partial(layer_norm, gain_vector=second_gain), residual)
    mixed = normed.astype(jnp.bfloat16)
    own_logits = jnp.dot(mixed, router_weight, preferred_element_type=jnp.float32)

    mixed_dense = {0: mixed}
    for step in range(1, line):
        mixed_dense[step] = along(mixed, step)

    expert_id = my_expert.reshape(1).astype(jnp.int32)
    out_dense, grad_dense, scores = {}, {}, {}
    for index in (0, 1):
        chunk = chunks[index]
        count = len(chunk)
        start = 0 if index == 0 else len(chunks[0])
        near = [mixed_dense[step] for step in chunk]
        blocks = (near, [across(block) for block in near])
        outs, grads = {}, {}
        for far in (0, 1):
            outs[far], grads[far], score = expert_unit(
                expert_id,
                slot_other[:, far, start : start + count].reshape(-1, 1),
                router_weight,
                deal(pack(rows[index, far], blocks[far], capacity)),
                cot_rows[index, far],
                up_local,
                down_local,
                1 if far else sections,
            )
            scores[index, far] = score.reshape(sections, count, capacity)
        met = across(outs[1][0])
        size = count * capacity
        summed = [
            (
                outs[0][d].astype(jnp.float32)
                + met[d * size : (d + 1) * size].astype(jnp.float32)
            ).astype(jnp.bfloat16)
            for d in range(sections)
        ]
        out_block = unpack(rows[index, 0], deal(summed), count)
        grad_far = unpack(rows[index, 1], deal(grads[1]), count)
        grad_block = unpack(
            rows[index, 0], deal(grads[0]), count, [across(block) for block in grad_far]
        )
        for spot, step in enumerate(chunk):
            part_out, part_grad = out_block[spot], grad_block[spot]
            out_dense[step] = along(part_out, -step) if step else part_out
            grad_dense[step] = along(part_grad, -step) if step else part_grad

    expert_total = sum(out_dense[step].astype(jnp.float32) for step in range(line))
    input_total = sum(grad_dense[step].astype(jnp.float32) for step in range(line))
    layer_out = (residual + expert_total).astype(jnp.bfloat16)

    score_table = jnp.stack(
        [jnp.concatenate([scores[0, far], scores[1, far]], axis=1) for far in (0, 1)], axis=1
    )
    spot_of = {step: spot for spot, step in enumerate(order)}
    spots = jnp.array([spot_of[step] for step in range(line)])
    lane_scores = deal_small(score_table)
    member = jnp.arange(members)
    lane_scores = lane_scores[:, (member % 2 != side).astype(jnp.int32), spots[(place - member // 2) % line]]
    own_scores = lax.all_to_all(
        lane_scores.transpose(1, 0, 2), "expert", split_axis=0, concat_axis=0, tiled=True
    )
    expert_scores = (
        jnp.sum(own_scores.reshape(per_section, PARTS_SIZE, sections, capacity), axis=1)
        .transpose(1, 0, 2)
        .reshape(experts, capacity)
    )
    expert_list = jnp.arange(experts)
    named = chosen[:, :, None] == expert_list
    hits = jnp.any(named, axis=1)
    own_slots = slot_of(hits.T)
    at_slot = (own_slots[:, :, None] == jnp.arange(capacity)) & hits.T[:, :, None]
    token_scores = jnp.sum(jnp.where(at_slot, expert_scores[:, None, :], 0.0), axis=2).T
    picked_logit = jnp.sum(jnp.where(named, own_logits[:, None, :], 0.0), axis=2)
    gate_values = 1.0 / (1.0 + jnp.exp(picked_logit[:, ::-1] - picked_logit))
    gate_spread = jnp.sum(jnp.where(named, gate_values[:, :, None], 0.0), axis=1)
    spread_grad = token_scores - gate_spread * jnp.sum(token_scores, axis=1, keepdims=True)
    mixed_grad = input_total + jnp.einsum(
        "se,de->sd", spread_grad, router_weight.astype(jnp.float32), precision=lax.Precision.HIGHEST
    )
    residual_grad = upstream.astype(jnp.float32) + norm_back(mixed_grad)[0]
    input_grad = attention_back(residual_grad)[0].astype(jnp.bfloat16)
    return (layer_out[None, None], input_grad[None, None])


def solution(mesh):
    placed = (
        P("segment", "expert", None, None),
        P("segment", "expert", None, None),
        P("segment", "expert", None, None),
        P(),
        P(),
        P(),
        P(),
        P(),
        P("segment", "expert", None, None),
        P("segment", "expert", None, None),
    )
    return jax.shard_map(
        shards,
        mesh=mesh,
        in_specs=placed,
        out_specs=(P("segment", "expert", None, None), P("segment", "expert", None, None)),
        check_vma=False,
    )
```

```python
from functools import partial

import jax
import jax.numpy as jnp
from jax import lax
from jax.experimental import pallas as pl
from jax.experimental.pallas import tpu as pltpu
from jax.sharding import PartitionSpec as P

HD = 104
PARTS_SIZE = 4
TOP = 2


EPSILON = 1e-06
ROOT_HALF = 0.7071067811865476
INV_ROOT_TWO_PI = 0.3989422804014327


def layer_norm(row_block, gain_vector):
    center = row_block - jnp.mean(row_block, axis=-1, keepdims=True)
    spread = jnp.mean(center * center, axis=-1, keepdims=True)
    return center * lax.rsqrt(spread + EPSILON) * gain_vector


def gelu_parts(preact):
    half_cdf = 0.5 * (1.0 + lax.erf(preact * ROOT_HALF))
    slope = half_cdf + preact * INV_ROOT_TWO_PI * jnp.exp(-0.5 * preact * preact)
    return preact * half_cdf, slope


def attention_branch(picture, first_gain, in_projection, out_projection):
    seq_len = picture.shape[0]
    head_width = out_projection.shape[0]
    head_count = head_width // HD
    normed = layer_norm(picture, first_gain).astype(jnp.bfloat16)
    joined = jnp.dot(normed, in_projection, preferred_element_type=jnp.float32).astype(jnp.bfloat16)
    queries = joined[:, :head_width].reshape(seq_len, head_count, HD)
    key_rows = joined[:, head_width : 2 * head_width].reshape(seq_len, head_count, HD)
    value_rows = joined[:, 2 * head_width :].reshape(seq_len, head_count, HD)
    scores = jnp.einsum(
        "qhd,khd->hqk", queries, key_rows, preferred_element_type=jnp.float32
    ) * HD ** (-0.5)
    weights = jnp.exp(scores)
    attention = (weights / jnp.sum(weights, axis=-1, keepdims=True)).astype(jnp.bfloat16)
    context = jnp.einsum(
        "hqk,khd->qhd", attention, value_rows, preferred_element_type=jnp.float32
    ).astype(jnp.bfloat16)
    return picture + jnp.dot(
        context.reshape(seq_len, head_width), out_projection, preferred_element_type=jnp.float32
    )


def params():
    return pltpu.CompilerParams(vmem_limit_bytes=60 * 1024 * 1024)


SMALL = pl.CostEstimate(flops=1000, bytes_accessed=1000, transcendentals=0)
SCALARS = pl.BlockSpec(memory_space=pltpu.SMEM)
UNREAD = pl.BlockSpec(memory_space=pl.ANY)


def slot_table(spots_ref, slots_ref, images, sections, count):
    capacity = count // images
    rows = []
    for d in range(sections):
        columns = []
        for i in range(images):
            slots = slots_ref[spots_ref[i]][d : d + 1, :]
            lanes = lax.broadcasted_iota(jnp.int32, (count, slots.shape[1]), 0)
            hit = (lanes == slots + i * capacity) & (slots >= 0)
            columns.append(jnp.where(hit, 1.0, 0.0))
        rows.append(jnp.concatenate(columns, axis=1))
    return jnp.concatenate(rows, axis=0)


def pack_kernel(images, sections, *refs):
    spots_ref, slots_ref = refs[:2]
    dense = refs[2 : 2 + images]
    joined = refs[-1]
    blocks = refs[-1 - sections : -1]
    count = blocks[0].shape[0]
    seq_len = dense[0].shape[0]
    for i in range(images):
        joined[i * seq_len : (i + 1) * seq_len, :] = dense[i][...]
    table = slot_table(spots_ref, slots_ref, images, sections, count).astype(jnp.bfloat16)
    total = jnp.dot(table, joined[...], preferred_element_type=jnp.float32).astype(jnp.bfloat16)
    for d in range(sections):
        blocks[d][...] = total[d * count : (d + 1) * count, :]


def pack(spots, slots, dense, capacity, after=()):
    sections = slots.shape[1]
    seq_len, width = dense[0].shape
    images = len(dense)
    count = images * capacity
    whole = pl.BlockSpec(memory_space=pltpu.VMEM)
    return pl.pallas_call(
        partial(pack_kernel, images, sections),
        in_specs=[SCALARS] + [whole] * (1 + images) + [UNREAD] * len(after),
        out_specs=[whole] * sections,
        out_shape=[jax.ShapeDtypeStruct((count, width), jnp.bfloat16)] * sections,
        scratch_shapes=[pltpu.VMEM((images * seq_len, width), jnp.bfloat16)],
        compiler_params=params(),
        cost_estimate=SMALL,
    )(spots, slots, *dense, *after)


def unpack_kernel(images, sections, extra, *refs):
    spots_ref, slots_ref = refs[:2]
    blocks = refs[2 : 2 + sections]
    addend = refs[2 + sections : 2 + sections + extra]
    joined = refs[-1]
    dense = refs[-1 - images : -1]
    count = blocks[0].shape[0]
    seq_len = dense[0].shape[0]
    for d in range(sections):
        joined[d * count : (d + 1) * count, :] = blocks[d][...]
    table = slot_table(spots_ref, slots_ref, images, sections, count).T.astype(jnp.bfloat16)
    total = jnp.dot(table, joined[...], preferred_element_type=jnp.float32)
    for i in range(images):
        part = total[i * seq_len : (i + 1) * seq_len, :]
        if extra:
            part = part + addend[i][...].astype(jnp.float32)
        dense[i][...] = part.astype(jnp.bfloat16)


def unpack(spots, slots, blocks, images, addend=(), after=()):
    sections, seq_len = slots.shape[1:]
    count, width = blocks[0].shape
    whole = pl.BlockSpec(memory_space=pltpu.VMEM)
    return pl.pallas_call(
        partial(unpack_kernel, images, sections, len(addend)),
        in_specs=[SCALARS] + [whole] * (1 + sections + len(addend)) + [UNREAD] * len(after),
        out_specs=[whole] * images,
        out_shape=[jax.ShapeDtypeStruct((seq_len, width), jnp.bfloat16)] * images,
        scratch_shapes=[pltpu.VMEM((sections * count, width), jnp.bfloat16)],
        compiler_params=params(),
        cost_estimate=SMALL,
    )(spots, slots, *blocks, *addend, *after)


def expert_kernel(sections, images, split, unread, *refs):
    spots_ref, other_ref, router_ref = refs[:3]
    mixed_in = refs[3 : 3 + sections]
    grads_in = refs[3 + sections : 3 + 2 * sections]
    up_ref, down_ref = refs[3 + 2 * sections : 5 + 2 * sections]
    outs = refs[5 + 2 * sections + unread :]
    out_parts, grad_parts, score_ref = outs[:split], outs[split : split + sections], outs[split + sections]
    mixed, grads, out_sum, grad_sum, gate_ref, score_sum = outs[split + sections + 1 :]
    step, last = pl.program_id(0), pl.num_programs(0) - 1
    count = mixed_in[0].shape[0]
    total = count * sections
    capacity = count // images
    at_row = lax.broadcasted_iota(jnp.int32, (count, capacity), 0)
    at_slot = lax.broadcasted_iota(jnp.int32, (count, capacity), 1)

    @pl.when(step == 0)
    def _():
        others = []
        for d in range(sections):
            mixed[d * count : (d + 1) * count, :] = mixed_in[d][...]
            grads[d * count : (d + 1) * count, :] = grads_in[d][...]
            column = jnp.zeros((count, 1), jnp.int32)
            for i in range(images):
                ids = other_ref[spots_ref[images + 1 + d], pl.ds(spots_ref[i], 1), :]
                own = at_row == at_slot + i * capacity
                column = column + jnp.sum(jnp.where(own, ids, 0), axis=1, keepdims=True)
            others.append(column)
        logits = jnp.dot(mixed[...], router_ref[...], preferred_element_type=jnp.float32)
        lanes = lax.broadcasted_iota(jnp.int32, logits.shape, 1)
        mine = jnp.sum(jnp.where(lanes == spots_ref[images], logits, 0.0), axis=1, keepdims=True)
        is_other = lanes == jnp.concatenate(others, axis=0)
        other = jnp.sum(jnp.where(is_other, logits, 0.0), axis=1, keepdims=True)
        gate_ref[...] = 1.0 / (1.0 + jnp.exp(other - mine))

    gate = gate_ref[...]
    preact = jnp.dot(mixed[...], up_ref[...], preferred_element_type=jnp.float32)
    pulled = gate * lax.dot_general(
        grads[...], down_ref[...], (((1,), (1,)), ((), ())), preferred_element_type=jnp.float32
    )
    hidden_wide, slope = gelu_parts(preact)
    hidden = hidden_wide.astype(jnp.bfloat16)
    hidden_grad = (pulled * slope).astype(jnp.bfloat16)
    score = jnp.sum(hidden_wide * pulled, axis=1, keepdims=True)
    out_add = jnp.dot(hidden, down_ref[...], preferred_element_type=jnp.float32)
    grad_add = lax.dot_general(
        hidden_grad, up_ref[...], (((1,), (1,)), ((), ())), preferred_element_type=jnp.float32
    )

    @pl.when(step == 0)
    def _():
        score_sum[...] = score
        out_sum[...] = out_add
        grad_sum[...] = grad_add

    @pl.when((step > 0) & (step < last))
    def _():
        score_sum[...] += score
        out_sum[...] += out_add
        grad_sum[...] += grad_add

    @pl.when(step == last)
    def _():
        base = jnp.where(last > 0, 1.0, 0.0)
        out_all = ((out_sum[...] * base + out_add) * gate).astype(jnp.bfloat16)
        grad_all = (grad_sum[...] * base + grad_add).astype(jnp.bfloat16)
        score_all = score_sum[...] * base + score
        size = total // split
        for part in range(split):
            out_parts[part][...] = out_all[part * size : (part + 1) * size, :]
        for d in range(sections):
            grad_parts[d][...] = grad_all[d * count : (d + 1) * count, :]
            column = score_all[d * count : (d + 1) * count, :]
            for i in range(images):
                own = at_row == at_slot + i * capacity
                score_ref[d, i : i + 1, :] = jnp.sum(
                    jnp.where(own, column, 0.0), axis=0, keepdims=True
                )


def expert_unit(spots, others, router, mixed_in, grads_in, up_local, down_local, split, after=()):
    sections = len(mixed_in)
    images = spots.shape[0] - 1 - sections
    count, width = mixed_in[0].shape
    total = count * sections
    hidden_units = up_local.shape[1]
    tile = 512
    assert hidden_units // tile >= 2

    def whole(shape):
        return pl.BlockSpec(shape, lambda f: (0,) * len(shape))

    block = whole((count, width))
    score_shape = (sections, images, count // images)
    results = pl.pallas_call(
        partial(expert_kernel, sections, images, split, len(after)),
        grid=(hidden_units // tile,),
        in_specs=[SCALARS, whole(others.shape), whole(router.shape)]
        + [block] * (2 * sections)
        + [
            pl.BlockSpec((width, tile), lambda f: (0, f)),
            pl.BlockSpec((tile, width), lambda f: (f, 0)),
        ]
        + [UNREAD] * len(after),
        out_specs=[whole((total // split, width))] * split + [block] * sections + [whole(score_shape)],
        out_shape=[jax.ShapeDtypeStruct((total // split, width), jnp.bfloat16)] * split
        + [jax.ShapeDtypeStruct((count, width), jnp.bfloat16)] * sections
        + [jax.ShapeDtypeStruct(score_shape, jnp.float32)],
        scratch_shapes=[
            pltpu.VMEM((total, width), jnp.bfloat16),
            pltpu.VMEM((total, width), jnp.bfloat16),
            pltpu.VMEM((total, width), jnp.float32),
            pltpu.VMEM((total, width), jnp.float32),
            pltpu.VMEM((total, 1), jnp.float32),
            pltpu.VMEM((total, 1), jnp.float32),
        ],
        compiler_params=params(),
        cost_estimate=SMALL,
    )(spots, others, router, *mixed_in, *grads_in, up_local, down_local, *after)
    return results[:split], results[split : split + sections], results[split + sections]


def shards(
    tokens,
    route_ids,
    cotangent,
    first_gain,
    in_projection,
    out_projection,
    second_gain,
    router_weight,
    up_weight,
    down_weight,
):
    picture = tokens[0, 0].astype(jnp.float32)
    chosen = route_ids[0, 0]
    upstream = cotangent[0, 0]
    up_local = up_weight[0, 0]
    down_local = down_weight[0, 0]
    seq_len, width = picture.shape
    experts = router_weight.shape[1]
    sections = lax.axis_size("segment")
    members = lax.axis_size("expert")
    per_section = members // PARTS_SIZE
    capacity = 3 * seq_len // experts
    line = members // 2
    here = lax.axis_index("expert")
    section = lax.axis_index("segment")
    place, side = here // 2, here % 2
    group = here // PARTS_SIZE
    my_expert = section * per_section + group
    relative = section ^ jnp.arange(sections)
    experts_here = relative * per_section + group

    def along(value, steps):
        pairs = [(j, (j + 2 * steps) % members) for j in range(members)]
        return lax.ppermute(value, "expert", pairs)

    def across(value):
        return lax.ppermute(value, "expert", [(j, j ^ 1) for j in range(members)])

    def deal(blocks):
        moved = [blocks[0]]
        for d in range(1, sections):
            pairs = [(s, s ^ d) for s in range(sections)]
            moved.append(lax.ppermute(blocks[d], "segment", pairs))
        return moved

    def deal_small(value):
        return lax.all_to_all(
            jnp.take(value, relative, axis=0), "segment", split_axis=0, concat_axis=0, tiled=True
        )

    half = line // 2
    chunks = [list(range(line - 1, half - 1, -1)), list(range(half - 1, -1, -1))]
    order = chunks[0] + chunks[1]

    expert_list = jnp.arange(experts)
    hits = jnp.any(chosen.T[None] == expert_list[:, None, None], axis=1)
    tokens_before = jnp.arange(seq_len)[:, None] < jnp.arange(seq_len)[None, :]
    own_slots = jnp.dot(
        hits.astype(jnp.bfloat16),
        tokens_before.astype(jnp.bfloat16),
        preferred_element_type=jnp.float32,
    ).astype(jnp.int32)
    own_slots = jnp.where(hits, own_slots, -1)
    others = jnp.sum(chosen, axis=1)[None, :] - expert_list[:, None]
    at_slot = own_slots[:, None, :] == jnp.arange(capacity)[None, :, None]
    own_others = jnp.sum(jnp.where(at_slot, others[:, None, :], 0), axis=2)
    wide = jnp.concatenate([own_slots, own_others], axis=1)
    wide = jnp.take(wide.reshape(sections, per_section, -1), relative, axis=0).transpose(1, 0, 2)
    wide = jnp.broadcast_to(
        wide[:, None], (per_section, PARTS_SIZE) + wide.shape[1:]
    ).reshape(members, -1)
    lane = lax.all_to_all(wide, "expert", split_axis=0, concat_axis=0, tiled=True).reshape(
        members, sections, seq_len + capacity
    )
    slots = lane[:, :, :seq_len]
    slot_others = deal_small(lane[:, :, seq_len:].transpose(1, 0, 2))

    def spots_of(index, far):
        places = (place - jnp.array(chunks[index])) % line
        side_of = (1 - side) if far else side
        return jnp.concatenate(
            [2 * places + side_of, my_expert.reshape(1), relative]
        ).astype(jnp.int32)

    spots = {(index, far): spots_of(index, far) for index in (0, 1) for far in (0, 1)}

    cot_dense = {0: upstream, 1: along(upstream, 1)}
    late_upstream, slots = lax.optimization_barrier((upstream, slots))
    for step in range(2, line):
        cot_dense[step] = along(late_upstream, step)
    cot_rows = {}
    for index in (1, 0):
        dense = [cot_dense[step] for step in chunks[index]]
        cot_rows[index, 0] = deal(pack(spots[index, 0], slots, dense, capacity))
        cot_rows[index, 1] = [across(block) for block in cot_rows[index, 0]]

    def branch(row_block):
        return attention_branch(row_block, first_gain, in_projection, out_projection)

    residual, attention_back = jax.vjp(branch, picture)
    normed, norm_back = jax.vjp(partial(layer_norm, gain_vector=second_gain), residual)
    mixed = normed.astype(jnp.bfloat16)
    own_logits = jnp.dot(mixed, router_weight, preferred_element_type=jnp.float32)

    mixed_dense = {0: mixed}
    for step in range(1, line):
        mixed_dense[step] = along(mixed, step)

    blocks, mixed_rows = {}, {}
    for index in (1, 0):
        blocks[index, 0] = [mixed_dense[step] for step in chunks[index]]
        blocks[index, 1] = [across(block) for block in blocks[index, 0]]
    for index, far in ((1, 0), (0, 0), (0, 1), (1, 1)):
        mixed_rows[index, far] = deal(pack(spots[index, far], slots, blocks[index, far], capacity))
    outs, grads, scores = {}, {}, {}
    after = ()
    for index, far in ((1, 0), (0, 0), (0, 1), (1, 1)):
        outs[index, far], grads[index, far], scores[index, far] = expert_unit(
            spots[index, far],
            slot_others,
            router_weight,
            mixed_rows[index, far],
            cot_rows[index, far],
            up_local,
            down_local,
            1 if far else sections,
            after,
        )
        after = (grads[index, far][0],)
    out_dense, grad_dense = {}, {}
    after = ()
    for index in (0, 1):
        chunk = chunks[index]
        count = len(chunk)
        grad_far = unpack(spots[index, 1], slots, deal(grads[index, 1]), count)
        met = across(outs[index, 1][0])
        size = count * capacity
        summed = [
            (
                outs[index, 0][d].astype(jnp.float32)
                + met[d * size : (d + 1) * size].astype(jnp.float32)
            ).astype(jnp.bfloat16)
            for d in range(sections)
        ]
        grad_block = unpack(
            spots[index, 0],
            slots,
            deal(grads[index, 0]),
            count,
            [across(block) for block in grad_far],
            after,
        )
        out_block = unpack(spots[index, 0], slots, deal(summed), count, (), after)
        after = []
        for spot, step in enumerate(chunk):
            part_out, part_grad = out_block[spot], grad_block[spot]
            out_dense[step] = along(part_out, -step) if step else part_out
            grad_dense[step] = along(part_grad, -step) if step else part_grad
            after += [out_dense[step], grad_dense[step]]

    expert_total = sum(out_dense[step].astype(jnp.float32) for step in range(line))
    input_total = sum(grad_dense[step].astype(jnp.float32) for step in range(line))
    layer_out = (residual + expert_total).astype(jnp.bfloat16)

    score_table = jnp.stack(
        [jnp.concatenate([scores[0, far], scores[1, far]], axis=1) for far in (0, 1)], axis=1
    )
    spot_of = {step: spot for spot, step in enumerate(order)}
    spots = jnp.array([spot_of[step] for step in range(line)])
    lane_scores = deal_small(score_table)
    member = jnp.arange(members)
    lane_scores = lane_scores[:, (member % 2 != side).astype(jnp.int32), spots[(place - member // 2) % line]]
    own_scores = lax.all_to_all(
        lane_scores.transpose(1, 0, 2), "expert", split_axis=0, concat_axis=0, tiled=True
    )
    expert_scores = (
        jnp.sum(own_scores.reshape(per_section, PARTS_SIZE, sections, capacity), axis=1)
        .transpose(1, 0, 2)
        .reshape(experts, capacity)
    )
    named = chosen[:, :, None] == expert_list
    at_slot = own_slots.T[:, :, None] == jnp.arange(capacity)
    token_scores = jnp.sum(jnp.where(at_slot, expert_scores[None], 0.0), axis=2)
    picked_logit = jnp.sum(jnp.where(named, own_logits[:, None, :], 0.0), axis=2)
    gate_values = 1.0 / (1.0 + jnp.exp(picked_logit[:, ::-1] - picked_logit))
    gate_spread = jnp.sum(jnp.where(named, gate_values[:, :, None], 0.0), axis=1)
    spread_grad = token_scores - gate_spread * jnp.sum(token_scores, axis=1, keepdims=True)
    mixed_grad = input_total + jnp.einsum(
        "se,de->sd", spread_grad, router_weight.astype(jnp.float32), precision=lax.Precision.HIGHEST
    )
    residual_grad = upstream.astype(jnp.float32) + norm_back(mixed_grad)[0]
    input_grad = attention_back(residual_grad)[0].astype(jnp.bfloat16)
    return (layer_out[None, None], input_grad[None, None])


def solution(mesh):
    placed = (
        P("segment", "expert", None, None),
        P("segment", "expert", None, None),
        P("segment", "expert", None, None),
        P(),
        P(),
        P(),
        P(),
        P(),
        P("segment", "expert", None, None),
        P("segment", "expert", None, None),
    )
    return jax.shard_map(
        shards,
        mesh=mesh,
        in_specs=placed,
        out_specs=(P("segment", "expert", None, None), P("segment", "expert", None, None)),
        check_vma=False,
    )
```

```python
from functools import partial

import jax
import jax.numpy as jnp
from jax import lax
from jax.experimental import pallas as pl
from jax.experimental.pallas import tpu as pltpu
from jax.sharding import PartitionSpec as P

HD = 104
PARTS_SIZE = 4
TOP = 2


EPSILON = 1e-06
ROOT_HALF = 0.7071067811865476
INV_ROOT_TWO_PI = 0.3989422804014327


def layer_norm(row_block, gain_vector):
    center = row_block - jnp.mean(row_block, axis=-1, keepdims=True)
    spread = jnp.mean(center * center, axis=-1, keepdims=True)
    return center * lax.rsqrt(spread + EPSILON) * gain_vector


def gelu_parts(preact):
    half_cdf = 0.5 * (1.0 + lax.erf(preact * ROOT_HALF))
    slope = half_cdf + preact * INV_ROOT_TWO_PI * jnp.exp(-0.5 * preact * preact)
    return preact * half_cdf, slope


def project_in(picture, first_gain, in_projection):
    normed = layer_norm(picture, first_gain).astype(jnp.bfloat16)
    return jnp.dot(normed, in_projection, preferred_element_type=jnp.float32).astype(jnp.bfloat16)


def attend(picture, joined, out_projection):
    seq_len = picture.shape[0]
    head_width = out_projection.shape[0]
    head_count = head_width // HD
    queries = joined[:, :head_width].reshape(seq_len, head_count, HD)
    key_rows = joined[:, head_width : 2 * head_width].reshape(seq_len, head_count, HD)
    value_rows = joined[:, 2 * head_width :].reshape(seq_len, head_count, HD)
    scores = jnp.einsum(
        "qhd,khd->hqk", queries, key_rows, preferred_element_type=jnp.float32
    ) * HD ** (-0.5)
    weights = jnp.exp(scores)
    attention = (weights / jnp.sum(weights, axis=-1, keepdims=True)).astype(jnp.bfloat16)
    context = jnp.einsum(
        "hqk,khd->qhd", attention, value_rows, preferred_element_type=jnp.float32
    ).astype(jnp.bfloat16)
    return picture + jnp.dot(
        context.reshape(seq_len, head_width), out_projection, preferred_element_type=jnp.float32
    )


def params():
    return pltpu.CompilerParams(vmem_limit_bytes=60 * 1024 * 1024)


SMALL = pl.CostEstimate(flops=1000, bytes_accessed=1000, transcendentals=0)
SCALARS = pl.BlockSpec(memory_space=pltpu.SMEM)
UNREAD = pl.BlockSpec(memory_space=pl.ANY)


def slot_table(spots_ref, slots_ref, images, sections, count):
    capacity = count // images
    rows = []
    for d in range(sections):
        columns = []
        for i in range(images):
            slots = slots_ref[spots_ref[i]][d : d + 1, :]
            lanes = lax.broadcasted_iota(jnp.int32, (count, slots.shape[1]), 0)
            hit = (lanes == slots + i * capacity) & (slots >= 0)
            columns.append(jnp.where(hit, 1.0, 0.0))
        rows.append(jnp.concatenate(columns, axis=1))
    return jnp.concatenate(rows, axis=0)


def pack_kernel(images, sections, *refs):
    spots_ref, slots_ref = refs[:2]
    dense = refs[2 : 2 + images]
    joined = refs[-1]
    blocks = refs[-1 - sections : -1]
    count = blocks[0].shape[0]
    seq_len = dense[0].shape[0]
    for i in range(images):
        joined[i * seq_len : (i + 1) * seq_len, :] = dense[i][...]
    table = slot_table(spots_ref, slots_ref, images, sections, count).astype(jnp.bfloat16)
    total = jnp.dot(table, joined[...], preferred_element_type=jnp.float32).astype(jnp.bfloat16)
    for d in range(sections):
        blocks[d][...] = total[d * count : (d + 1) * count, :]


def pack(spots, slots, dense, capacity, after=()):
    sections = slots.shape[1]
    seq_len, width = dense[0].shape
    images = len(dense)
    count = images * capacity
    whole = pl.BlockSpec(memory_space=pltpu.VMEM)
    return pl.pallas_call(
        partial(pack_kernel, images, sections),
        name="pack",
        in_specs=[SCALARS] + [whole] * (1 + images) + [UNREAD] * len(after),
        out_specs=[whole] * sections,
        out_shape=[jax.ShapeDtypeStruct((count, width), jnp.bfloat16)] * sections,
        scratch_shapes=[pltpu.VMEM((images * seq_len, width), jnp.bfloat16)],
        compiler_params=params(),
        cost_estimate=SMALL,
    )(spots, slots, *dense, *after)


EXTRA = 16


def unpack_kernel(images, sections, extra, scored, *refs):
    spots_ref, slots_ref = refs[:2]
    blocks = refs[2 : 2 + sections]
    addend = refs[2 + sections : 2 + sections + extra]
    partners = refs[2 + sections + extra : 2 + sections + extra + scored]
    joined = refs[-1]
    dense = refs[-1 - images : -1]
    count = blocks[0].shape[0]
    seq_len = slots_ref.shape[2]
    for d in range(sections):
        joined[d * count : (d + 1) * count, :] = blocks[d][...]
    table = slot_table(spots_ref, slots_ref, images, sections, count)
    total = jnp.dot(
        table.T.astype(jnp.bfloat16), joined[...], preferred_element_type=jnp.float32
    )
    if scored:
        lines = []
        for d in range(sections):
            product = blocks[d][...].astype(jnp.float32) * partners[d][...].astype(jnp.float32)
            column = jnp.sum(product, axis=1, keepdims=True)
            lines.append(
                jnp.sum(table[d * count : (d + 1) * count, :] * column, axis=0, keepdims=True)
            )
        lines = jnp.concatenate(
            lines + [jnp.zeros((EXTRA - sections, lines[0].shape[1]), jnp.float32)], axis=0
        )
    for i in range(images):
        part = total[i * seq_len : (i + 1) * seq_len, :]
        if extra:
            part = part + addend[i][...].astype(jnp.float32)
        dense[i][:seq_len, :] = part.astype(jnp.bfloat16)
        if scored:
            dense[i][seq_len:, :] = jnp.zeros((EXTRA, total.shape[1]), jnp.bfloat16)
            dense[i][seq_len:, :seq_len] = lines[:, i * seq_len : (i + 1) * seq_len].astype(
                jnp.bfloat16
            )


def unpack(spots, slots, blocks, images, addend=(), partners=(), after=()):
    sections, seq_len = slots.shape[1:]
    count, width = blocks[0].shape
    whole = pl.BlockSpec(memory_space=pltpu.VMEM)
    inputs = sections + len(addend) + len(partners)
    height = seq_len + (EXTRA if partners else 0)
    return pl.pallas_call(
        partial(unpack_kernel, images, sections, len(addend), len(partners)),
        name="unpack",
        in_specs=[SCALARS] + [whole] * (1 + inputs) + [UNREAD] * len(after),
        out_specs=[whole] * images,
        out_shape=[jax.ShapeDtypeStruct((height, width), jnp.bfloat16)] * images,
        scratch_shapes=[pltpu.VMEM((sections * count, width), jnp.bfloat16)],
        compiler_params=params(),
        cost_estimate=SMALL,
    )(spots, slots, *blocks, *addend, *partners, *after)


def expert_kernel(sections, images, split, unread, *refs):
    spots_ref, other_ref, router_ref = refs[:3]
    mixed_in = refs[3 : 3 + sections]
    grads_in = refs[3 + sections : 3 + 2 * sections]
    up_ref, down_ref = refs[3 + 2 * sections : 5 + 2 * sections]
    outs = refs[5 + 2 * sections + unread :]
    out_parts, grad_parts = outs[:split], outs[split : split + sections]
    mixed, grads, out_sum, grad_sum, gate_ref = outs[split + sections :]
    step, last = pl.program_id(0), pl.num_programs(0) - 1
    count = mixed_in[0].shape[0]
    total = count * sections
    capacity = count // images
    at_row = lax.broadcasted_iota(jnp.int32, (count, capacity), 0)
    at_slot = lax.broadcasted_iota(jnp.int32, (count, capacity), 1)

    @pl.when(step == 0)
    def _():
        others = []
        for d in range(sections):
            mixed[d * count : (d + 1) * count, :] = mixed_in[d][...]
            grads[d * count : (d + 1) * count, :] = grads_in[d][...]
            column = jnp.zeros((count, 1), jnp.int32)
            for i in range(images):
                ids = other_ref[spots_ref[images + 1 + d], pl.ds(spots_ref[i], 1), :]
                own = at_row == at_slot + i * capacity
                column = column + jnp.sum(jnp.where(own, ids, 0), axis=1, keepdims=True)
            others.append(column)
        logits = jnp.dot(mixed[...], router_ref[...], preferred_element_type=jnp.float32)
        lanes = lax.broadcasted_iota(jnp.int32, logits.shape, 1)
        mine = jnp.sum(jnp.where(lanes == spots_ref[images], logits, 0.0), axis=1, keepdims=True)
        is_other = lanes == jnp.concatenate(others, axis=0)
        other = jnp.sum(jnp.where(is_other, logits, 0.0), axis=1, keepdims=True)
        gate_ref[...] = 1.0 / (1.0 + jnp.exp(other - mine))
        out_sum[...] = jnp.zeros_like(out_sum)
        grad_sum[...] = jnp.zeros_like(grad_sum)

    gate = gate_ref[...]
    preact = jnp.dot(mixed[...], up_ref[...], preferred_element_type=jnp.float32)
    pulled = gate * lax.dot_general(
        grads[...], down_ref[...], (((1,), (1,)), ((), ())), preferred_element_type=jnp.float32
    )
    hidden_wide, slope = gelu_parts(preact)
    hidden = hidden_wide.astype(jnp.bfloat16)
    hidden_grad = (pulled * slope).astype(jnp.bfloat16)
    out_sum[...] += jnp.dot(hidden, down_ref[...], preferred_element_type=jnp.float32)
    grad_sum[...] += lax.dot_general(
        hidden_grad, up_ref[...], (((1,), (1,)), ((), ())), preferred_element_type=jnp.float32
    )

    @pl.when(step == last)
    def _():
        size = total // split
        for part in range(split):
            rows = slice(part * size, (part + 1) * size)
            out_parts[part][...] = (out_sum[rows, :] * gate[rows, :]).astype(jnp.bfloat16)
        for d in range(sections):
            grad_parts[d][...] = grad_sum[d * count : (d + 1) * count, :].astype(jnp.bfloat16)


def expert_unit(spots, others, router, mixed_in, grads_in, up_local, down_local, split, after=()):
    sections = len(mixed_in)
    images = spots.shape[0] - 1 - sections
    count, width = mixed_in[0].shape
    total = count * sections
    hidden_units = up_local.shape[1]
    tile = 512
    assert hidden_units // tile >= 2

    def whole(shape):
        return pl.BlockSpec(shape, lambda f: (0,) * len(shape))

    block = whole((count, width))
    results = pl.pallas_call(
        partial(expert_kernel, sections, images, split, len(after)),
        name="expert",
        grid=(hidden_units // tile,),
        in_specs=[SCALARS, whole(others.shape), whole(router.shape)]
        + [block] * (2 * sections)
        + [
            pl.BlockSpec((width, tile), lambda f: (0, f)),
            pl.BlockSpec((tile, width), lambda f: (f, 0)),
        ]
        + [UNREAD] * len(after),
        out_specs=[whole((total // split, width))] * split + [block] * sections,
        out_shape=[jax.ShapeDtypeStruct((total // split, width), jnp.bfloat16)] * split
        + [jax.ShapeDtypeStruct((count, width), jnp.bfloat16)] * sections,
        scratch_shapes=[
            pltpu.VMEM((total, width), jnp.bfloat16),
            pltpu.VMEM((total, width), jnp.bfloat16),
            pltpu.VMEM((total, width), jnp.float32),
            pltpu.VMEM((total, width), jnp.float32),
            pltpu.VMEM((total, 1), jnp.float32),
        ],
        compiler_params=params(),
        cost_estimate=SMALL,
    )(spots, others, router, *mixed_in, *grads_in, up_local, down_local, *after)
    return results[:split], results[split:]


def shards(
    tokens,
    route_ids,
    cotangent,
    first_gain,
    in_projection,
    out_projection,
    second_gain,
    router_weight,
    up_weight,
    down_weight,
):
    picture = tokens[0, 0].astype(jnp.float32)
    chosen = route_ids[0, 0]
    upstream = cotangent[0, 0]
    up_local = up_weight[0, 0]
    down_local = down_weight[0, 0]
    seq_len, width = picture.shape
    experts = router_weight.shape[1]
    sections = lax.axis_size("segment")
    members = lax.axis_size("expert")
    per_section = members // PARTS_SIZE
    capacity = 3 * seq_len // experts
    line = members // 2
    here = lax.axis_index("expert")
    section = lax.axis_index("segment")
    place, side = here // 2, here % 2
    group = here // PARTS_SIZE
    my_expert = section * per_section + group
    relative = section ^ jnp.arange(sections)
    experts_here = relative * per_section + group

    def along(value, steps):
        pairs = [(j, (j + 2 * steps) % members) for j in range(members)]
        return lax.ppermute(value, "expert", pairs)

    def across(value):
        return lax.ppermute(value, "expert", [(j, j ^ 1) for j in range(members)])

    def deal(blocks):
        moved = [blocks[0]]
        for d in range(1, sections):
            pairs = [(s, s ^ d) for s in range(sections)]
            moved.append(lax.ppermute(blocks[d], "segment", pairs))
        return moved

    def deal_small(value):
        return lax.all_to_all(
            jnp.take(value, relative, axis=0), "segment", split_axis=0, concat_axis=0, tiled=True
        )

    half = line // 2
    chunks = [list(range(line - 1, half - 1, -1)), list(range(half - 1, -1, -1))]

    expert_list = jnp.arange(experts)
    hits = jnp.any(chosen.T[None] == expert_list[:, None, None], axis=1)
    tokens_before = jnp.arange(seq_len)[:, None] < jnp.arange(seq_len)[None, :]
    own_slots = jnp.dot(
        hits.astype(jnp.bfloat16),
        tokens_before.astype(jnp.bfloat16),
        preferred_element_type=jnp.float32,
    ).astype(jnp.int32)
    own_slots = jnp.where(hits, own_slots, -1)
    others = jnp.sum(chosen, axis=1)[None, :] - expert_list[:, None]
    at_slot = own_slots[:, None, :] == jnp.arange(capacity)[None, :, None]
    own_others = jnp.sum(jnp.where(at_slot, others[:, None, :], 0), axis=2)
    wide = jnp.concatenate([own_slots, own_others], axis=1)
    wide = jnp.take(wide.reshape(sections, per_section, -1), relative, axis=0).transpose(1, 0, 2)
    wide = jnp.broadcast_to(
        wide[:, None], (per_section, PARTS_SIZE) + wide.shape[1:]
    ).reshape(members, -1)
    lane = lax.all_to_all(wide, "expert", split_axis=0, concat_axis=0, tiled=True).reshape(
        members, sections, seq_len + capacity
    )
    slots = lane[:, :, :seq_len]
    slot_others = deal_small(lane[:, :, seq_len:].transpose(1, 0, 2))

    def spots_of(index, far):
        places = (place - jnp.array(chunks[index])) % line
        side_of = (1 - side) if far else side
        return jnp.concatenate(
            [2 * places + side_of, my_expert.reshape(1), relative]
        ).astype(jnp.int32)

    spots = {(index, far): spots_of(index, far) for index in (0, 1) for far in (0, 1)}

    cot_dense = {0: upstream, 1: along(upstream, 1)}
    joined, project_back = jax.vjp(
        partial(project_in, first_gain=first_gain, in_projection=in_projection), picture
    )
    joined, slots, slot_others, cot_dense[1] = lax.optimization_barrier(
        (joined, slots, slot_others, cot_dense[1])
    )
    late_upstream, joined = lax.optimization_barrier((upstream, joined))
    for step in range(2, line):
        cot_dense[step] = along(late_upstream, step)
    residual, attend_back = jax.vjp(partial(attend, out_projection=out_projection), picture, joined)
    normed, norm_back = jax.vjp(partial(layer_norm, gain_vector=second_gain), residual)
    mixed = normed.astype(jnp.bfloat16)
    own_logits = jnp.dot(mixed, router_weight, preferred_element_type=jnp.float32)

    cot_packed, cot_rows = {}, {}
    for index in (1, 0):
        dense = [cot_dense[step] for step in chunks[index]]
        cot_packed[index] = pack(spots[index, 0], slots, dense, capacity)
        cot_rows[index, 0] = deal(cot_packed[index])
        cot_rows[index, 1] = [across(block) for block in cot_rows[index, 0]]

    mixed_dense = {0: mixed}
    for step in range(1, line):
        mixed_dense[step] = along(mixed, step)

    blocks, mixed_rows = {}, {}
    for index in (1, 0):
        blocks[index, 0] = [mixed_dense[step] for step in chunks[index]]
        blocks[index, 1] = [across(block) for block in blocks[index, 0]]
    for index, far in ((1, 0), (0, 0), (0, 1), (1, 1)):
        mixed_rows[index, far] = deal(pack(spots[index, far], slots, blocks[index, far], capacity))
    outs, grads = {}, {}
    after = ()
    for index, far in ((1, 0), (0, 0), (0, 1), (1, 1)):
        outs[index, far], grads[index, far] = expert_unit(
            spots[index, far],
            slot_others,
            router_weight,
            mixed_rows[index, far],
            cot_rows[index, far],
            up_local,
            down_local,
            1 if far else sections,
            after,
        )
        after = (grads[index, far][0],)
    out_dense, grad_dense = {}, {}
    far_out = {index: across(outs[index, 1][0]) for index in (0, 1)}
    last_unit, after = after, ()
    for index in (0, 1):
        chunk = chunks[index]
        count = len(chunk)
        grad_far = unpack(
            spots[index, 1], slots, deal(grads[index, 1]), count, after=last_unit
        )
        met = far_out[index]
        if index == 0:
            met, last_unit = lax.optimization_barrier((met, last_unit))
        size = count * capacity
        summed = [
            (
                outs[index, 0][d].astype(jnp.float32)
                + met[d * size : (d + 1) * size].astype(jnp.float32)
            ).astype(jnp.bfloat16)
            for d in range(sections)
        ]
        out_block = unpack(
            spots[index, 0], slots, deal(summed), count, (), cot_packed[index]
        )
        grad_block = unpack(
            spots[index, 0],
            slots,
            deal(grads[index, 0]),
            count,
            [across(block) for block in grad_far],
            (),
            after,
        )
        after = []
        for spot, step in enumerate(chunk):
            part_out, part_grad = out_block[spot], grad_block[spot]
            out_dense[step] = along(part_out, -step) if step else part_out
            grad_dense[step] = along(part_grad, -step) if step else part_grad
            after += [out_dense[step], grad_dense[step]]

    expert_total = sum(out_dense[step][:seq_len].astype(jnp.float32) for step in range(line))
    input_total = sum(grad_dense[step].astype(jnp.float32) for step in range(line))
    layer_out = (residual + expert_total).astype(jnp.bfloat16)

    named = chosen[:, :, None] == expert_list
    score_lines = jnp.zeros((per_section, sections, seq_len), jnp.float32)
    for step in range(line):
        sender = 2 * ((place + step) % line) // PARTS_SIZE
        lines = out_dense[step][seq_len : seq_len + sections, :seq_len].astype(jnp.float32)
        score_lines += jnp.where((jnp.arange(per_section) == sender)[:, None, None], lines, 0.0)
    token_scores = (
        jnp.take(score_lines, relative, axis=1).transpose(1, 0, 2).reshape(experts, seq_len).T
    )
    picked_logit = jnp.sum(jnp.where(named, own_logits[:, None, :], 0.0), axis=2)
    gate_values = 1.0 / (1.0 + jnp.exp(picked_logit[:, ::-1] - picked_logit))
    gate_spread = jnp.sum(jnp.where(named, gate_values[:, :, None], 0.0), axis=1)
    spread_grad = token_scores - gate_spread * jnp.sum(token_scores, axis=1, keepdims=True)
    mixed_grad = input_total + jnp.einsum(
        "se,de->sd", spread_grad, router_weight.astype(jnp.float32), precision=lax.Precision.HIGHEST
    )
    residual_grad = upstream.astype(jnp.float32) + norm_back(mixed_grad)[0]
    picture_grad, joined_grad = attend_back(residual_grad)
    input_grad = (picture_grad + project_back(joined_grad)[0]).astype(jnp.bfloat16)
    return (layer_out[None, None], input_grad[None, None])


def solution(mesh):
    placed = (
        P("segment", "expert", None, None),
        P("segment", "expert", None, None),
        P("segment", "expert", None, None),
        P(),
        P(),
        P(),
        P(),
        P(),
        P("segment", "expert", None, None),
        P("segment", "expert", None, None),
    )
    return jax.shard_map(
        shards,
        mesh=mesh,
        in_specs=placed,
        out_specs=(P("segment", "expert", None, None), P("segment", "expert", None, None)),
        check_vma=False,
    )
```

```python
from functools import partial

import jax
import jax.numpy as jnp
from jax import lax
from jax.experimental import pallas as pl
from jax.experimental.pallas import tpu as pltpu
from jax.sharding import PartitionSpec as P

HD = 104
PARTS_SIZE = 4
TOP = 2


EPSILON = 1e-06
ROOT_HALF = 0.7071067811865476
INV_ROOT_TWO_PI = 0.3989422804014327


def layer_norm(row_block, gain_vector):
    center = row_block - jnp.mean(row_block, axis=-1, keepdims=True)
    spread = jnp.mean(center * center, axis=-1, keepdims=True)
    return center * lax.rsqrt(spread + EPSILON) * gain_vector


def gelu_parts(preact):
    half_cdf = 0.5 * (1.0 + lax.erf(preact * ROOT_HALF))
    slope = half_cdf + preact * INV_ROOT_TWO_PI * jnp.exp(-0.5 * preact * preact)
    return preact * half_cdf, slope


def project_in(picture, first_gain, in_projection):
    normed = layer_norm(picture, first_gain).astype(jnp.bfloat16)
    return jnp.dot(normed, in_projection, preferred_element_type=jnp.float32).astype(jnp.bfloat16)


def attend(picture, joined, out_projection):
    seq_len = picture.shape[0]
    head_width = out_projection.shape[0]
    head_count = head_width // HD
    queries = joined[:, :head_width].reshape(seq_len, head_count, HD)
    key_rows = joined[:, head_width : 2 * head_width].reshape(seq_len, head_count, HD)
    value_rows = joined[:, 2 * head_width :].reshape(seq_len, head_count, HD)
    scores = jnp.einsum(
        "qhd,khd->hqk", queries, key_rows, preferred_element_type=jnp.float32
    ) * HD ** (-0.5)
    weights = jnp.exp(scores)
    attention = (weights / jnp.sum(weights, axis=-1, keepdims=True)).astype(jnp.bfloat16)
    context = jnp.einsum(
        "hqk,khd->qhd", attention, value_rows, preferred_element_type=jnp.float32
    ).astype(jnp.bfloat16)
    return picture + jnp.dot(
        context.reshape(seq_len, head_width), out_projection, preferred_element_type=jnp.float32
    )


def params():
    return pltpu.CompilerParams(vmem_limit_bytes=60 * 1024 * 1024)


SMALL = pl.CostEstimate(flops=1000, bytes_accessed=1000, transcendentals=0)
SCALARS = pl.BlockSpec(memory_space=pltpu.SMEM)
UNREAD = pl.BlockSpec(memory_space=pl.ANY)


def slot_table(spots_ref, slots_ref, images, sections, count):
    capacity = count // images
    rows = []
    for d in range(sections):
        columns = []
        for i in range(images):
            slots = slots_ref[spots_ref[i]][d : d + 1, :]
            lanes = lax.broadcasted_iota(jnp.int32, (count, slots.shape[1]), 0)
            hit = (lanes == slots + i * capacity) & (slots >= 0)
            columns.append(jnp.where(hit, 1.0, 0.0))
        rows.append(jnp.concatenate(columns, axis=1))
    return jnp.concatenate(rows, axis=0)


def pack_kernel(images, sections, inputs, *refs):
    spots_ref, slots_ref = refs[:2]
    dense = refs[2 : 2 + inputs]
    if inputs > 1:
        joined, blocks = refs[-1], refs[-1 - sections : -1]
        seq_len = dense[0].shape[0]
        for i in range(images):
            joined[i * seq_len : (i + 1) * seq_len, :] = dense[i][...]
    else:
        joined, blocks = dense[0], refs[-sections:]
    count = blocks[0].shape[0]
    table = slot_table(spots_ref, slots_ref, images, sections, count).astype(jnp.bfloat16)
    total = jnp.dot(table, joined[...], preferred_element_type=jnp.float32).astype(jnp.bfloat16)
    for d in range(sections):
        blocks[d][...] = total[d * count : (d + 1) * count, :]


def pack(spots, slots, dense, capacity, after=()):
    sections, seq_len = slots.shape[1:]
    width = dense[0].shape[1]
    inputs = len(dense)
    images = sum(block.shape[0] for block in dense) // seq_len
    count = images * capacity
    whole = pl.BlockSpec(memory_space=pltpu.VMEM)
    shapes = [jax.ShapeDtypeStruct((count, width), jnp.bfloat16)] * sections
    if inputs > 1:
        shapes.append(jax.ShapeDtypeStruct((images * seq_len, width), jnp.bfloat16))
    results = pl.pallas_call(
        partial(pack_kernel, images, sections, inputs),
        name="pack",
        in_specs=[SCALARS] + [whole] * (1 + inputs) + [UNREAD] * len(after),
        out_specs=[whole] * len(shapes),
        out_shape=shapes,
        compiler_params=params(),
        cost_estimate=SMALL,
    )(spots, slots, *dense, *after)
    return results[:sections], results[sections:]


EXTRA = 16


def unpack_kernel(images, sections, extra, scored, *refs):
    spots_ref, slots_ref = refs[:2]
    blocks = refs[2 : 2 + sections]
    addend = refs[2 + sections : 2 + sections + extra]
    partners = refs[2 + sections + extra : 2 + sections + extra + scored]
    joined = refs[-1]
    dense = refs[-1 - (images if extra or scored else 1) : -1]
    count = blocks[0].shape[0]
    seq_len = slots_ref.shape[2]
    for d in range(sections):
        joined[d * count : (d + 1) * count, :] = blocks[d][...]
    table = slot_table(spots_ref, slots_ref, images, sections, count)
    total = jnp.dot(
        table.T.astype(jnp.bfloat16), joined[...], preferred_element_type=jnp.float32
    )
    if scored:
        lines = []
        for d in range(sections):
            product = blocks[d][...].astype(jnp.float32) * partners[d][...].astype(jnp.float32)
            column = jnp.sum(product, axis=1, keepdims=True)
            lines.append(
                jnp.sum(table[d * count : (d + 1) * count, :] * column, axis=0, keepdims=True)
            )
        lines = jnp.concatenate(
            lines + [jnp.zeros((EXTRA - sections, lines[0].shape[1]), jnp.float32)], axis=0
        )
    if not (extra or scored):
        dense[0][...] = total.astype(jnp.bfloat16)
        return
    for i in range(images):
        part = total[i * seq_len : (i + 1) * seq_len, :]
        if extra:
            part = part + addend[0][i * seq_len : (i + 1) * seq_len, :].astype(jnp.float32)
        dense[i][:seq_len, :] = part.astype(jnp.bfloat16)
        if scored:
            dense[i][seq_len:, :] = jnp.zeros((EXTRA, total.shape[1]), jnp.bfloat16)
            dense[i][seq_len:, :seq_len] = lines[:, i * seq_len : (i + 1) * seq_len].astype(
                jnp.bfloat16
            )


def unpack(spots, slots, blocks, images, addend=(), partners=(), after=()):
    sections, seq_len = slots.shape[1:]
    count, width = blocks[0].shape
    whole = pl.BlockSpec(memory_space=pltpu.VMEM)
    inputs = sections + len(addend) + len(partners)
    height = seq_len + (EXTRA if partners else 0)
    parts = images if addend or partners else 1
    if parts == 1:
        height = images * seq_len
    return pl.pallas_call(
        partial(unpack_kernel, images, sections, len(addend), len(partners)),
        name="unpack",
        in_specs=[SCALARS] + [whole] * (1 + inputs) + [UNREAD] * len(after),
        out_specs=[whole] * parts,
        out_shape=[jax.ShapeDtypeStruct((height, width), jnp.bfloat16)] * parts,
        scratch_shapes=[pltpu.VMEM((sections * count, width), jnp.bfloat16)],
        compiler_params=params(),
        cost_estimate=SMALL,
    )(spots, slots, *blocks, *addend, *partners, *after)


def merge_kernel(sections, *refs):
    met = refs[sections]
    merged = refs[-sections:]
    count = merged[0].shape[0]
    for d in range(sections):
        total = refs[d][...].astype(jnp.float32)
        total = total + met[d * count : (d + 1) * count, :].astype(jnp.float32)
        merged[d][...] = total.astype(jnp.bfloat16)


def merge(blocks, met, after=()):
    sections = len(blocks)
    whole = pl.BlockSpec(memory_space=pltpu.VMEM)
    return pl.pallas_call(
        partial(merge_kernel, sections),
        name="merge",
        in_specs=[whole] * (sections + 1) + [UNREAD] * len(after),
        out_specs=[whole] * sections,
        out_shape=[jax.ShapeDtypeStruct(blocks[0].shape, jnp.bfloat16)] * sections,
        compiler_params=params(),
        cost_estimate=SMALL,
    )(*blocks, met, *after)


def expert_kernel(sections, images, split, unread, *refs):
    spots_ref, other_ref, router_ref = refs[:3]
    mixed_in = refs[3 : 3 + sections]
    pulls = 1 if split == 1 else sections
    grads_in = refs[3 + sections : 3 + sections + pulls]
    up_ref, down_ref = refs[3 + sections + pulls : 5 + sections + pulls]
    outs = refs[5 + sections + pulls + unread :]
    out_parts, grad_parts = outs[:split], outs[split : split + sections]
    mixed, grads, out_sum, grad_sum, gate_ref = outs[split + sections :]
    step, last = pl.program_id(0), pl.num_programs(0) - 1
    count = mixed_in[0].shape[0]
    total = count * sections
    capacity = count // images
    at_row = lax.broadcasted_iota(jnp.int32, (count, capacity), 0)
    at_slot = lax.broadcasted_iota(jnp.int32, (count, capacity), 1)

    @pl.when(step == 0)
    def _():
        others = []
        for d in range(sections):
            mixed[d * count : (d + 1) * count, :] = mixed_in[d][...]
            if split > 1:
                grads[d * count : (d + 1) * count, :] = grads_in[d][...]
            column = jnp.zeros((count, 1), jnp.int32)
            for i in range(images):
                ids = other_ref[spots_ref[images + 1 + d], pl.ds(spots_ref[i], 1), :]
                own = at_row == at_slot + i * capacity
                column = column + jnp.sum(jnp.where(own, ids, 0), axis=1, keepdims=True)
            others.append(column)
        if split == 1:
            grads[...] = grads_in[0][...]
        logits = jnp.dot(mixed[...], router_ref[...], preferred_element_type=jnp.float32)
        lanes = lax.broadcasted_iota(jnp.int32, logits.shape, 1)
        mine = jnp.sum(jnp.where(lanes == spots_ref[images], logits, 0.0), axis=1, keepdims=True)
        is_other = lanes == jnp.concatenate(others, axis=0)
        other = jnp.sum(jnp.where(is_other, logits, 0.0), axis=1, keepdims=True)
        gate_ref[...] = 1.0 / (1.0 + jnp.exp(other - mine))
        out_sum[...] = jnp.zeros_like(out_sum)
        grad_sum[...] = jnp.zeros_like(grad_sum)

    gate = gate_ref[...]
    preact = jnp.dot(mixed[...], up_ref[...], preferred_element_type=jnp.float32)
    pulled = gate * lax.dot_general(
        grads[...], down_ref[...], (((1,), (1,)), ((), ())), preferred_element_type=jnp.float32
    )
    hidden_wide, slope = gelu_parts(preact)
    hidden = hidden_wide.astype(jnp.bfloat16)
    hidden_grad = (pulled * slope).astype(jnp.bfloat16)
    out_sum[...] += jnp.dot(hidden, down_ref[...], preferred_element_type=jnp.float32)
    grad_sum[...] += lax.dot_general(
        hidden_grad, up_ref[...], (((1,), (1,)), ((), ())), preferred_element_type=jnp.float32
    )

    @pl.when(step == last)
    def _():
        size = total // split
        for part in range(split):
            rows = slice(part * size, (part + 1) * size)
            out_parts[part][...] = (out_sum[rows, :] * gate[rows, :]).astype(jnp.bfloat16)
        for d in range(sections):
            grad_parts[d][...] = grad_sum[d * count : (d + 1) * count, :].astype(jnp.bfloat16)


def expert_unit(spots, others, router, mixed_in, grads_in, up_local, down_local, split, after=()):
    sections = len(mixed_in)
    images = spots.shape[0] - 1 - sections
    count, width = mixed_in[0].shape
    total = count * sections
    hidden_units = up_local.shape[1]
    tile = 512
    assert hidden_units // tile >= 2

    def whole(shape):
        return pl.BlockSpec(shape, lambda f: (0,) * len(shape))

    block = whole((count, width))
    results = pl.pallas_call(
        partial(expert_kernel, sections, images, split, len(after)),
        name="expert",
        grid=(hidden_units // tile,),
        in_specs=[SCALARS, whole(others.shape), whole(router.shape)]
        + [block] * sections
        + [whole(block_in.shape) for block_in in grads_in]
        + [
            pl.BlockSpec((width, tile), lambda f: (0, f)),
            pl.BlockSpec((tile, width), lambda f: (f, 0)),
        ]
        + [UNREAD] * len(after),
        out_specs=[whole((total // split, width))] * split + [block] * sections,
        out_shape=[jax.ShapeDtypeStruct((total // split, width), jnp.bfloat16)] * split
        + [jax.ShapeDtypeStruct((count, width), jnp.bfloat16)] * sections,
        scratch_shapes=[
            pltpu.VMEM((total, width), jnp.bfloat16),
            pltpu.VMEM((total, width), jnp.bfloat16),
            pltpu.VMEM((total, width), jnp.float32),
            pltpu.VMEM((total, width), jnp.float32),
            pltpu.VMEM((total, 1), jnp.float32),
        ],
        compiler_params=params(),
        cost_estimate=SMALL,
    )(spots, others, router, *mixed_in, *grads_in, up_local, down_local, *after)
    return results[:split], results[split:]


def shards(
    tokens,
    route_ids,
    cotangent,
    first_gain,
    in_projection,
    out_projection,
    second_gain,
    router_weight,
    up_weight,
    down_weight,
):
    picture = tokens[0, 0].astype(jnp.float32)
    chosen = route_ids[0, 0]
    upstream = cotangent[0, 0]
    up_local = up_weight[0, 0]
    down_local = down_weight[0, 0]
    seq_len, width = picture.shape
    experts = router_weight.shape[1]
    sections = lax.axis_size("segment")
    members = lax.axis_size("expert")
    per_section = members // PARTS_SIZE
    capacity = 3 * seq_len // experts
    line = members // 2
    here = lax.axis_index("expert")
    section = lax.axis_index("segment")
    place, side = here // 2, here % 2
    group = here // PARTS_SIZE
    my_expert = section * per_section + group
    relative = section ^ jnp.arange(sections)
    experts_here = relative * per_section + group

    def along(value, steps):
        pairs = [(j, (j + 2 * steps) % members) for j in range(members)]
        return lax.ppermute(value, "expert", pairs)

    def across(value):
        return lax.ppermute(value, "expert", [(j, j ^ 1) for j in range(members)])

    def deal(blocks):
        moved = [blocks[0]]
        for d in range(1, sections):
            pairs = [(s, s ^ d) for s in range(sections)]
            moved.append(lax.ppermute(blocks[d], "segment", pairs))
        return moved

    def deal_small(value):
        return lax.all_to_all(
            jnp.take(value, relative, axis=0), "segment", split_axis=0, concat_axis=0, tiled=True
        )

    half = line // 2
    chunks = [list(range(line - 1, half - 1, -1)), list(range(half - 1, -1, -1))]

    expert_list = jnp.arange(experts)
    hits = jnp.any(chosen.T[None] == expert_list[:, None, None], axis=1)
    tokens_before = jnp.arange(seq_len)[:, None] < jnp.arange(seq_len)[None, :]
    own_slots = jnp.dot(
        hits.astype(jnp.bfloat16),
        tokens_before.astype(jnp.bfloat16),
        preferred_element_type=jnp.float32,
    ).astype(jnp.int32)
    own_slots = jnp.where(hits, own_slots, -1)
    others = jnp.sum(chosen, axis=1)[None, :] - expert_list[:, None]
    at_slot = own_slots[:, None, :] == jnp.arange(capacity)[None, :, None]
    own_others = jnp.sum(jnp.where(at_slot, others[:, None, :], 0), axis=2)
    wide = jnp.concatenate([own_slots, own_others], axis=1)
    wide = jnp.take(wide.reshape(sections, per_section, -1), relative, axis=0).transpose(1, 0, 2)
    wide = jnp.broadcast_to(
        wide[:, None], (per_section, PARTS_SIZE) + wide.shape[1:]
    ).reshape(members, -1)
    lane = lax.all_to_all(wide, "expert", split_axis=0, concat_axis=0, tiled=True).reshape(
        members, sections, seq_len + capacity
    )
    slots = lane[:, :, :seq_len]
    slot_others = deal_small(lane[:, :, seq_len:].transpose(1, 0, 2))

    def spots_of(index, far):
        places = (place - jnp.array(chunks[index])) % line
        side_of = (1 - side) if far else side
        return jnp.concatenate(
            [2 * places + side_of, my_expert.reshape(1), relative]
        ).astype(jnp.int32)

    spots = {(index, far): spots_of(index, far) for index in (0, 1) for far in (0, 1)}

    cot_dense = {0: upstream, 1: along(upstream, 1)}
    slots, late_upstream = lax.optimization_barrier((slots, upstream))
    for step in range(2, line):
        cot_dense[step] = along(late_upstream, step)

    def cot_pack(index):
        dense = [cot_dense[step] for step in chunks[index]]
        return pack(spots[index, 0], slots, dense, capacity)[0]

    joined, project_back = jax.vjp(
        partial(project_in, first_gain=first_gain, in_projection=in_projection), picture
    )
    cot_packed, cot_rows = {}, {}
    cot_packed[1] = cot_pack(1)
    joined, cot_packed[1] = lax.optimization_barrier((joined, cot_packed[1]))
    cot_rows[1, 0] = deal(cot_packed[1])
    residual, attend_back = jax.vjp(partial(attend, out_projection=out_projection), picture, joined)
    residual, cot_rows[1, 0], slot_others = lax.optimization_barrier(
        (residual, cot_rows[1, 0], slot_others)
    )
    normed, norm_back = jax.vjp(partial(layer_norm, gain_vector=second_gain), residual)
    mixed = normed.astype(jnp.bfloat16)
    own_logits = jnp.dot(mixed, router_weight, preferred_element_type=jnp.float32)

    mixed_dense = {0: mixed}
    for step in range(1, line):
        mixed_dense[step] = along(mixed, step)

    cot_rows[1, 1] = [across(jnp.concatenate(cot_rows[1, 0], axis=0))]
    cot_packed[0] = cot_pack(0)
    cot_rows[0, 0] = deal(cot_packed[0])

    mixed_rows, far_dense = {}, {}

    def mixed_pack(index, after):
        dense = [mixed_dense[step] for step in chunks[index]]
        blocks, joined_dense = pack(spots[index, 0], slots, dense, capacity, after)
        far_dense[index] = across(joined_dense[0])
        mixed_rows[index, 0] = deal(blocks)
        return (blocks[0],)

    def far_pack(index, after):
        blocks, _ = pack(spots[index, 1], slots, [far_dense[index]], capacity, after)
        mixed_rows[index, 1] = deal(blocks)
        return (blocks[0],)

    outs, grads = {}, {}

    def unit(index, far, after):
        outs[index, far], grads[index, far] = expert_unit(
            spots[index, far],
            slot_others,
            router_weight,
            mixed_rows[index, far],
            cot_rows[index, far],
            up_local,
            down_local,
            1 if far else sections,
            after,
        )
        done = (grads[index, far][0],)
        grads[index, far] = deal(grads[index, far])
        return done

    done = mixed_pack(1, (cot_packed[0][0],))
    done = mixed_pack(0, done + tuple(cot_rows[1, 1]))
    cot_rows[0, 1] = [across(jnp.concatenate(cot_rows[0, 0], axis=0))]
    done = far_pack(1, done)
    done = unit(1, 0, done)
    done = far_pack(0, done)
    done = unit(0, 0, done)
    done = unit(1, 1, done + tuple(grads[1, 0][1:]))
    met = {1: across(outs[1, 1][0])}
    done = unit(0, 1, done + tuple(grads[0, 0][1:]))
    met[0] = across(outs[0, 1][0])

    grad_far, out_back, out_dense, grad_dense = {}, {}, {}, {}
    for index in (1, 0):
        count = len(chunks[index])
        grad_far[index] = unpack(spots[index, 1], slots, grads[index, 1], count, after=done)[0]
        done = (grad_far[index],)
        grad_far[index] = across(grad_far[index])
        merged = merge(outs[index, 0], met[index], done)
        done = (merged[0],)
        out_back[index] = deal(merged)
    for index in (1, 0):
        chunk = chunks[index]
        count = len(chunk)
        out_block = unpack(
            spots[index, 0], slots, out_back[index], count, (), cot_packed[index], done
        )
        done = (out_block[0],)
        grad_block = unpack(
            spots[index, 0], slots, grads[index, 0], count, (grad_far[index],), (), done
        )
        done = (grad_block[0],)
        for spot, step in enumerate(chunk):
            part_out, part_grad = out_block[spot], grad_block[spot]
            out_dense[step] = along(part_out, -step) if step else part_out
            grad_dense[step] = along(part_grad, -step) if step else part_grad
        done += tuple(out_dense[step] for step in chunk if step)

    expert_total = sum(out_dense[step][:seq_len].astype(jnp.float32) for step in range(line))
    input_total = sum(grad_dense[step].astype(jnp.float32) for step in range(line))
    layer_out = (residual + expert_total).astype(jnp.bfloat16)

    named = chosen[:, :, None] == expert_list
    score_lines = jnp.zeros((per_section, sections, seq_len), jnp.float32)
    for step in range(line):
        sender = 2 * ((place + step) % line) // PARTS_SIZE
        lines = out_dense[step][seq_len : seq_len + sections, :seq_len].astype(jnp.float32)
        score_lines += jnp.where((jnp.arange(per_section) == sender)[:, None, None], lines, 0.0)
    token_scores = (
        jnp.take(score_lines, relative, axis=1).transpose(1, 0, 2).reshape(experts, seq_len).T
    )
    picked_logit = jnp.sum(jnp.where(named, own_logits[:, None, :], 0.0), axis=2)
    gate_values = 1.0 / (1.0 + jnp.exp(picked_logit[:, ::-1] - picked_logit))
    gate_spread = jnp.sum(jnp.where(named, gate_values[:, :, None], 0.0), axis=1)
    spread_grad = token_scores - gate_spread * jnp.sum(token_scores, axis=1, keepdims=True)
    mixed_grad = input_total + jnp.einsum(
        "se,de->sd", spread_grad, router_weight.astype(jnp.float32), precision=lax.Precision.HIGHEST
    )
    residual_grad = upstream.astype(jnp.float32) + norm_back(mixed_grad)[0]
    picture_grad, joined_grad = attend_back(residual_grad)
    input_grad = (picture_grad + project_back(joined_grad)[0]).astype(jnp.bfloat16)
    return (layer_out[None, None], input_grad[None, None])


def solution(mesh):
    placed = (
        P("segment", "expert", None, None),
        P("segment", "expert", None, None),
        P("segment", "expert", None, None),
        P(),
        P(),
        P(),
        P(),
        P(),
        P("segment", "expert", None, None),
        P("segment", "expert", None, None),
    )
    return jax.shard_map(
        shards,
        mesh=mesh,
        in_specs=placed,
        out_specs=(P("segment", "expert", None, None), P("segment", "expert", None, None)),
        check_vma=False,
    )
```

```python
from functools import partial

import jax
import jax.numpy as jnp
from jax import lax
from jax.experimental import pallas as pl
from jax.experimental.pallas import tpu as pltpu
from jax.sharding import PartitionSpec as P

HD = 104
PARTS_SIZE = 4
TOP = 2


EPSILON = 1e-06
ROOT_HALF = 0.7071067811865476
INV_ROOT_TWO_PI = 0.3989422804014327


def layer_norm(row_block, gain_vector):
    center = row_block - jnp.mean(row_block, axis=-1, keepdims=True)
    spread = jnp.mean(center * center, axis=-1, keepdims=True)
    return center * lax.rsqrt(spread + EPSILON) * gain_vector


def gelu_parts(preact):
    half_cdf = 0.5 * (1.0 + lax.erf(preact * ROOT_HALF))
    slope = half_cdf + preact * INV_ROOT_TWO_PI * jnp.exp(-0.5 * preact * preact)
    return preact * half_cdf, slope


def project_in(picture, first_gain, in_projection):
    normed = layer_norm(picture, first_gain).astype(jnp.bfloat16)
    return jnp.dot(normed, in_projection, preferred_element_type=jnp.float32).astype(jnp.bfloat16)


def attend(picture, joined, out_projection):
    seq_len = picture.shape[0]
    head_width = out_projection.shape[0]
    head_count = head_width // HD
    queries = joined[:, :head_width].reshape(seq_len, head_count, HD)
    key_rows = joined[:, head_width : 2 * head_width].reshape(seq_len, head_count, HD)
    value_rows = joined[:, 2 * head_width :].reshape(seq_len, head_count, HD)
    scores = jnp.einsum(
        "qhd,khd->hqk", queries, key_rows, preferred_element_type=jnp.float32
    ) * HD ** (-0.5)
    weights = jnp.exp(scores)
    attention = (weights / jnp.sum(weights, axis=-1, keepdims=True)).astype(jnp.bfloat16)
    context = jnp.einsum(
        "hqk,khd->qhd", attention, value_rows, preferred_element_type=jnp.float32
    ).astype(jnp.bfloat16)
    return picture + jnp.dot(
        context.reshape(seq_len, head_width), out_projection, preferred_element_type=jnp.float32
    )


def params():
    return pltpu.CompilerParams(vmem_limit_bytes=60 * 1024 * 1024)


SMALL = pl.CostEstimate(flops=1000, bytes_accessed=1000, transcendentals=0)
SCALARS = pl.BlockSpec(memory_space=pltpu.SMEM)
UNREAD = pl.BlockSpec(memory_space=pl.ANY)


def slot_table(spots_ref, slots_ref, images, sections, count):
    capacity = count // images
    rows = []
    for d in range(sections):
        columns = []
        for i in range(images):
            slots = slots_ref[spots_ref[i]][d : d + 1, :]
            lanes = lax.broadcasted_iota(jnp.int32, (count, slots.shape[1]), 0)
            hit = (lanes == slots + i * capacity) & (slots >= 0)
            columns.append(jnp.where(hit, 1.0, 0.0))
        rows.append(jnp.concatenate(columns, axis=1))
    return jnp.concatenate(rows, axis=0)


def pack_kernel(images, sections, inputs, *refs):
    spots_ref, slots_ref = refs[:2]
    dense = refs[2 : 2 + inputs]
    if inputs > 1:
        joined, blocks = refs[-1], refs[-1 - sections : -1]
        seq_len = dense[0].shape[0]
        for i in range(images):
            joined[i * seq_len : (i + 1) * seq_len, :] = dense[i][...]
    else:
        joined, blocks = dense[0], refs[-sections:]
    count = blocks[0].shape[0]
    table = slot_table(spots_ref, slots_ref, images, sections, count).astype(jnp.bfloat16)
    total = jnp.dot(table, joined[...], preferred_element_type=jnp.float32).astype(jnp.bfloat16)
    for d in range(sections):
        blocks[d][...] = total[d * count : (d + 1) * count, :]


def pack(spots, slots, dense, capacity, after=()):
    sections, seq_len = slots.shape[1:]
    width = dense[0].shape[1]
    inputs = len(dense)
    images = sum(block.shape[0] for block in dense) // seq_len
    count = images * capacity
    whole = pl.BlockSpec(memory_space=pltpu.VMEM)
    shapes = [jax.ShapeDtypeStruct((count, width), jnp.bfloat16)] * sections
    if inputs > 1:
        shapes.append(jax.ShapeDtypeStruct((images * seq_len, width), jnp.bfloat16))
    results = pl.pallas_call(
        partial(pack_kernel, images, sections, inputs),
        name="pack",
        in_specs=[SCALARS] + [whole] * (1 + inputs) + [UNREAD] * len(after),
        out_specs=[whole] * len(shapes),
        out_shape=shapes,
        compiler_params=params(),
        cost_estimate=SMALL,
    )(spots, slots, *dense, *after)
    return results[:sections], results[sections:]


EXTRA = 16


def unpack_kernel(images, sections, extra, scored, *refs):
    spots_ref, slots_ref = refs[:2]
    blocks = refs[2 : 2 + sections]
    addend = refs[2 + sections : 2 + sections + extra]
    partners = refs[2 + sections + extra : 2 + sections + extra + scored]
    joined = refs[-1]
    dense = refs[-1 - (images if extra or scored else 1) : -1]
    count = blocks[0].shape[0]
    seq_len = slots_ref.shape[2]
    for d in range(sections):
        joined[d * count : (d + 1) * count, :] = blocks[d][...]
    table = slot_table(spots_ref, slots_ref, images, sections, count)
    total = jnp.dot(
        table.T.astype(jnp.bfloat16), joined[...], preferred_element_type=jnp.float32
    )
    if scored:
        lines = []
        for d in range(sections):
            product = blocks[d][...].astype(jnp.float32) * partners[d][...].astype(jnp.float32)
            column = jnp.sum(product, axis=1, keepdims=True)
            lines.append(
                jnp.sum(table[d * count : (d + 1) * count, :] * column, axis=0, keepdims=True)
            )
        lines = jnp.concatenate(
            lines + [jnp.zeros((EXTRA - sections, lines[0].shape[1]), jnp.float32)], axis=0
        )
    if not (extra or scored):
        dense[0][...] = total.astype(jnp.bfloat16)
        return
    for i in range(images):
        part = total[i * seq_len : (i + 1) * seq_len, :]
        if extra:
            part = part + addend[0][i * seq_len : (i + 1) * seq_len, :].astype(jnp.float32)
        dense[i][:seq_len, :] = part.astype(jnp.bfloat16)
        if scored:
            dense[i][seq_len:, :] = jnp.zeros((EXTRA, total.shape[1]), jnp.bfloat16)
            dense[i][seq_len:, :seq_len] = lines[:, i * seq_len : (i + 1) * seq_len].astype(
                jnp.bfloat16
            )


def unpack(spots, slots, blocks, images, addend=(), partners=(), after=()):
    sections, seq_len = slots.shape[1:]
    count, width = blocks[0].shape
    whole = pl.BlockSpec(memory_space=pltpu.VMEM)
    inputs = sections + len(addend) + len(partners)
    height = seq_len + (EXTRA if partners else 0)
    parts = images if addend or partners else 1
    if parts == 1:
        height = images * seq_len
    return pl.pallas_call(
        partial(unpack_kernel, images, sections, len(addend), len(partners)),
        name="unpack",
        in_specs=[SCALARS] + [whole] * (1 + inputs) + [UNREAD] * len(after),
        out_specs=[whole] * parts,
        out_shape=[jax.ShapeDtypeStruct((height, width), jnp.bfloat16)] * parts,
        scratch_shapes=[pltpu.VMEM((sections * count, width), jnp.bfloat16)],
        compiler_params=params(),
        cost_estimate=SMALL,
    )(spots, slots, *blocks, *addend, *partners, *after)


def merge_kernel(sections, *refs):
    met = refs[sections]
    merged = refs[-sections:]
    count = merged[0].shape[0]
    for d in range(sections):
        total = refs[d][...].astype(jnp.float32)
        total = total + met[d * count : (d + 1) * count, :].astype(jnp.float32)
        merged[d][...] = total.astype(jnp.bfloat16)


def merge(blocks, met, after=()):
    sections = len(blocks)
    whole = pl.BlockSpec(memory_space=pltpu.VMEM)
    return pl.pallas_call(
        partial(merge_kernel, sections),
        name="merge",
        in_specs=[whole] * (sections + 1) + [UNREAD] * len(after),
        out_specs=[whole] * sections,
        out_shape=[jax.ShapeDtypeStruct(blocks[0].shape, jnp.bfloat16)] * sections,
        compiler_params=params(),
        cost_estimate=SMALL,
    )(*blocks, met, *after)


def expert_kernel(sections, images, split, unread, *refs):
    spots_ref, other_ref, router_ref = refs[:3]
    mixed_in = refs[3 : 3 + sections]
    pulls = len(refs) - unread - 10 - 2 * sections - split
    grads_in = refs[3 + sections : 3 + sections + pulls]
    up_ref, down_ref = refs[3 + sections + pulls : 5 + sections + pulls]
    outs = refs[5 + sections + pulls + unread :]
    out_parts, grad_parts = outs[:split], outs[split : split + sections]
    mixed, grads, out_sum, grad_sum, gate_ref = outs[split + sections :]
    step, last = pl.program_id(0), pl.num_programs(0) - 1
    count = mixed_in[0].shape[0]
    total = count * sections
    capacity = count // images
    at_row = lax.broadcasted_iota(jnp.int32, (count, capacity), 0)
    at_slot = lax.broadcasted_iota(jnp.int32, (count, capacity), 1)

    @pl.when(step == 0)
    def _():
        others = []
        for d in range(sections):
            mixed[d * count : (d + 1) * count, :] = mixed_in[d][...]
            if pulls > 1:
                grads[d * count : (d + 1) * count, :] = grads_in[d][...]
            column = jnp.zeros((count, 1), jnp.int32)
            for i in range(images):
                ids = other_ref[spots_ref[images + 1 + d], pl.ds(spots_ref[i], 1), :]
                own = at_row == at_slot + i * capacity
                column = column + jnp.sum(jnp.where(own, ids, 0), axis=1, keepdims=True)
            others.append(column)
        if pulls == 1:
            grads[...] = grads_in[0][...]
        logits = jnp.dot(mixed[...], router_ref[...], preferred_element_type=jnp.float32)
        lanes = lax.broadcasted_iota(jnp.int32, logits.shape, 1)
        mine = jnp.sum(jnp.where(lanes == spots_ref[images], logits, 0.0), axis=1, keepdims=True)
        is_other = lanes == jnp.concatenate(others, axis=0)
        other = jnp.sum(jnp.where(is_other, logits, 0.0), axis=1, keepdims=True)
        gate_ref[...] = 1.0 / (1.0 + jnp.exp(other - mine))
        out_sum[...] = jnp.zeros_like(out_sum)
        grad_sum[...] = jnp.zeros_like(grad_sum)

    gate = gate_ref[...]
    preact = jnp.dot(mixed[...], up_ref[...], preferred_element_type=jnp.float32)
    pulled = gate * lax.dot_general(
        grads[...], down_ref[...], (((1,), (1,)), ((), ())), preferred_element_type=jnp.float32
    )
    hidden_wide, slope = gelu_parts(preact)
    hidden = hidden_wide.astype(jnp.bfloat16)
    hidden_grad = (pulled * slope).astype(jnp.bfloat16)
    out_sum[...] += jnp.dot(hidden, down_ref[...], preferred_element_type=jnp.float32)
    grad_sum[...] += lax.dot_general(
        hidden_grad, up_ref[...], (((1,), (1,)), ((), ())), preferred_element_type=jnp.float32
    )

    @pl.when(step == last)
    def _():
        size = total // split
        for part in range(split):
            rows = slice(part * size, (part + 1) * size)
            out_parts[part][...] = (out_sum[rows, :] * gate[rows, :]).astype(jnp.bfloat16)
        for d in range(sections):
            grad_parts[d][...] = grad_sum[d * count : (d + 1) * count, :].astype(jnp.bfloat16)


def expert_unit(spots, others, router, mixed_in, grads_in, up_local, down_local, split, after=()):
    sections = len(mixed_in)
    images = spots.shape[0] - 1 - sections
    count, width = mixed_in[0].shape
    total = count * sections
    hidden_units = up_local.shape[1]
    tile = 512
    assert hidden_units // tile >= 2

    def whole(shape):
        return pl.BlockSpec(shape, lambda f: (0,) * len(shape))

    block = whole((count, width))
    results = pl.pallas_call(
        partial(expert_kernel, sections, images, split, len(after)),
        name="expert",
        grid=(hidden_units // tile,),
        in_specs=[SCALARS, whole(others.shape), whole(router.shape)]
        + [block] * sections
        + [whole(block_in.shape) for block_in in grads_in]
        + [
            pl.BlockSpec((width, tile), lambda f: (0, f)),
            pl.BlockSpec((tile, width), lambda f: (f, 0)),
        ]
        + [UNREAD] * len(after),
        out_specs=[whole((total // split, width))] * split + [block] * sections,
        out_shape=[jax.ShapeDtypeStruct((total // split, width), jnp.bfloat16)] * split
        + [jax.ShapeDtypeStruct((count, width), jnp.bfloat16)] * sections,
        scratch_shapes=[
            pltpu.VMEM((total, width), jnp.bfloat16),
            pltpu.VMEM((total, width), jnp.bfloat16),
            pltpu.VMEM((total, width), jnp.float32),
            pltpu.VMEM((total, width), jnp.float32),
            pltpu.VMEM((total, 1), jnp.float32),
        ],
        compiler_params=params(),
        cost_estimate=SMALL,
    )(spots, others, router, *mixed_in, *grads_in, up_local, down_local, *after)
    return results[:split], results[split:]


def shards(
    tokens,
    route_ids,
    cotangent,
    first_gain,
    in_projection,
    out_projection,
    second_gain,
    router_weight,
    up_weight,
    down_weight,
):
    picture = tokens[0, 0].astype(jnp.float32)
    chosen = route_ids[0, 0]
    upstream = cotangent[0, 0]
    up_local = up_weight[0, 0]
    down_local = down_weight[0, 0]
    seq_len, width = picture.shape
    experts = router_weight.shape[1]
    sections = lax.axis_size("segment")
    members = lax.axis_size("expert")
    per_section = members // PARTS_SIZE
    capacity = 3 * seq_len // experts
    line = members // 2
    here = lax.axis_index("expert")
    section = lax.axis_index("segment")
    place, side = here // 2, here % 2
    group = here // PARTS_SIZE
    my_expert = section * per_section + group
    relative = section ^ jnp.arange(sections)
    experts_here = relative * per_section + group

    def along(value, steps):
        pairs = [(j, (j + 2 * steps) % members) for j in range(members)]
        return lax.ppermute(value, "expert", pairs)

    def across(value):
        return lax.ppermute(value, "expert", [(j, j ^ 1) for j in range(members)])

    def deal(blocks):
        moved = [blocks[0]]
        for d in range(1, sections):
            pairs = [(s, s ^ d) for s in range(sections)]
            moved.append(lax.ppermute(blocks[d], "segment", pairs))
        return moved

    def deal_small(value):
        return lax.all_to_all(
            jnp.take(value, relative, axis=0), "segment", split_axis=0, concat_axis=0, tiled=True
        )

    half = line // 2
    chunks = [list(range(line - 1, half - 1, -1)), list(range(half - 1, -1, -1))]

    expert_list = jnp.arange(experts)
    hits = jnp.any(chosen.T[None] == expert_list[:, None, None], axis=1)
    tokens_before = jnp.arange(seq_len)[:, None] < jnp.arange(seq_len)[None, :]
    own_slots = jnp.dot(
        hits.astype(jnp.bfloat16),
        tokens_before.astype(jnp.bfloat16),
        preferred_element_type=jnp.float32,
    ).astype(jnp.int32)
    own_slots = jnp.where(hits, own_slots, -1)
    others = jnp.sum(chosen, axis=1)[None, :] - expert_list[:, None]
    at_slot = own_slots[:, None, :] == jnp.arange(capacity)[None, :, None]
    own_others = jnp.sum(jnp.where(at_slot, others[:, None, :], 0), axis=2)
    wide = jnp.concatenate([own_slots, own_others], axis=1)
    wide = jnp.take(wide.reshape(sections, per_section, -1), relative, axis=0).transpose(1, 0, 2)
    wide = jnp.broadcast_to(
        wide[:, None], (per_section, PARTS_SIZE) + wide.shape[1:]
    ).reshape(members, -1)
    lane = lax.all_to_all(wide, "expert", split_axis=0, concat_axis=0, tiled=True).reshape(
        members, sections, seq_len + capacity
    )
    slots = lane[:, :, :seq_len]
    slot_others = deal_small(lane[:, :, seq_len:].transpose(1, 0, 2))

    def spots_of(index, far):
        places = (place - jnp.array(chunks[index])) % line
        side_of = (1 - side) if far else side
        return jnp.concatenate(
            [2 * places + side_of, my_expert.reshape(1), relative]
        ).astype(jnp.int32)

    spots = {(index, far): spots_of(index, far) for index in (0, 1) for far in (0, 1)}

    cot_dense = {0: upstream, 1: along(upstream, 1)}
    cot_far = {0: across(upstream)}
    slots, late_upstream = lax.optimization_barrier((slots, upstream))
    for step in range(2, line):
        cot_dense[step] = along(late_upstream, step)

    def cot_pack(index):
        dense = [cot_dense[step] for step in chunks[index]]
        return pack(spots[index, 0], slots, dense, capacity)[0]

    joined, project_back = jax.vjp(
        partial(project_in, first_gain=first_gain, in_projection=in_projection), picture
    )
    cot_packed, cot_rows = {}, {}
    cot_packed[1] = cot_pack(1)
    joined, cot_packed[1] = lax.optimization_barrier((joined, cot_packed[1]))
    for step in chunks[1]:
        if step:
            cot_far[step] = across(cot_dense[step])
    cot_rows[1, 0] = deal(cot_packed[1])
    residual, attend_back = jax.vjp(partial(attend, out_projection=out_projection), picture, joined)
    far_packed, _ = pack(spots[1, 1], slots, [cot_far[step] for step in chunks[1]], capacity)
    residual, far_packed, slot_others = lax.optimization_barrier(
        (residual, far_packed, slot_others)
    )
    cot_rows[1, 1] = deal(far_packed)
    normed, norm_back = jax.vjp(partial(layer_norm, gain_vector=second_gain), residual)
    mixed = normed.astype(jnp.bfloat16)
    own_logits = jnp.dot(mixed, router_weight, preferred_element_type=jnp.float32)

    mixed_dense = {0: mixed}
    for step in range(1, line):
        mixed_dense[step] = along(mixed, step)

    cot_packed[0] = cot_pack(0)
    cot_rows[0, 0] = deal(cot_packed[0])

    mixed_rows, far_dense = {}, {}

    def mixed_pack(index, after):
        dense = [mixed_dense[step] for step in chunks[index]]
        blocks, joined_dense = pack(spots[index, 0], slots, dense, capacity, after)
        far_dense[index] = across(joined_dense[0])
        mixed_rows[index, 0] = deal(blocks)
        return (blocks[0],)

    def far_pack(index, after):
        blocks, _ = pack(spots[index, 1], slots, [far_dense[index]], capacity, after)
        mixed_rows[index, 1] = deal(blocks)
        return (blocks[0],)

    outs, grads = {}, {}

    def unit(index, far, after):
        outs[index, far], grads[index, far] = expert_unit(
            spots[index, far],
            slot_others,
            router_weight,
            mixed_rows[index, far],
            cot_rows[index, far],
            up_local,
            down_local,
            1 if far else sections,
            after,
        )
        done = (grads[index, far][0],)
        grads[index, far] = deal(grads[index, far])
        return done

    done = mixed_pack(1, (cot_packed[0][0],))
    done = mixed_pack(0, done + tuple(cot_rows[1, 1][1:]))
    cot_rows[0, 1] = [across(jnp.concatenate(cot_rows[0, 0], axis=0))]
    done = far_pack(1, done)
    done = unit(1, 0, done)
    done = far_pack(0, done)
    done = unit(0, 0, done)
    done = unit(1, 1, done)
    met = {1: across(outs[1, 1][0])}

    grad_far, out_back, out_dense, grad_dense = {}, {}, {}, {}

    def unpack_far(index, after):
        count = len(chunks[index])
        block = unpack(spots[index, 1], slots, grads[index, 1], count, after=after)[0]
        grad_far[index] = across(block)
        return (block,)

    def merge_out(index, after):
        merged = merge(outs[index, 0], met[index], after)
        out_back[index] = deal(merged)
        return (merged[0],)

    done = unpack_far(1, done)
    done = unit(0, 1, done)
    met[0] = across(outs[0, 1][0])
    done = merge_out(1, done + tuple(grads[1, 0][1:]))
    done = unpack_far(0, done)
    done = merge_out(0, done + tuple(grads[0, 0][1:]))
    for index in (1, 0):
        chunk = chunks[index]
        count = len(chunk)
        out_block = unpack(
            spots[index, 0], slots, out_back[index], count, (), cot_packed[index], done
        )
        done = (out_block[0],)
        if index == 1:
            done += tuple(out_back[0][1:]) + (grad_far[0],)
        grad_block = unpack(
            spots[index, 0], slots, grads[index, 0], count, (grad_far[index],), (), done
        )
        done = (grad_block[0],)
        for spot, step in enumerate(chunk):
            part_out, part_grad = out_block[spot], grad_block[spot]
            out_dense[step] = along(part_out, -step) if step else part_out
            grad_dense[step] = along(part_grad, -step) if step else part_grad
        done += tuple(out_dense[step] for step in chunk if step)

    expert_total = sum(out_dense[step][:seq_len].astype(jnp.float32) for step in range(line))
    input_total = sum(grad_dense[step].astype(jnp.float32) for step in range(line))
    layer_out = (residual + expert_total).astype(jnp.bfloat16)

    named = chosen[:, :, None] == expert_list
    score_lines = jnp.zeros((per_section, sections, seq_len), jnp.float32)
    for step in range(line):
        sender = 2 * ((place + step) % line) // PARTS_SIZE
        lines = out_dense[step][seq_len : seq_len + sections, :seq_len].astype(jnp.float32)
        score_lines += jnp.where((jnp.arange(per_section) == sender)[:, None, None], lines, 0.0)
    token_scores = (
        jnp.take(score_lines, relative, axis=1).transpose(1, 0, 2).reshape(experts, seq_len).T
    )
    picked_logit = jnp.sum(jnp.where(named, own_logits[:, None, :], 0.0), axis=2)
    gate_values = 1.0 / (1.0 + jnp.exp(picked_logit[:, ::-1] - picked_logit))
    gate_spread = jnp.sum(jnp.where(named, gate_values[:, :, None], 0.0), axis=1)
    spread_grad = token_scores - gate_spread * jnp.sum(token_scores, axis=1, keepdims=True)
    mixed_grad = input_total + jnp.einsum(
        "se,de->sd", spread_grad, router_weight.astype(jnp.float32), precision=lax.Precision.HIGHEST
    )
    residual_grad = upstream.astype(jnp.float32) + norm_back(mixed_grad)[0]
    picture_grad, joined_grad = attend_back(residual_grad)
    input_grad = (picture_grad + project_back(joined_grad)[0]).astype(jnp.bfloat16)
    return (layer_out[None, None], input_grad[None, None])


def solution(mesh):
    placed = (
        P("segment", "expert", None, None),
        P("segment", "expert", None, None),
        P("segment", "expert", None, None),
        P(),
        P(),
        P(),
        P(),
        P(),
        P("segment", "expert", None, None),
        P("segment", "expert", None, None),
    )
    return jax.shard_map(
        shards,
        mesh=mesh,
        in_specs=placed,
        out_specs=(P("segment", "expert", None, None), P("segment", "expert", None, None)),
        check_vma=False,
    )
```

```python
from functools import partial

import jax
import jax.numpy as jnp
from jax import lax
from jax.experimental import pallas as pl
from jax.experimental.pallas import tpu as pltpu
from jax.sharding import PartitionSpec as P

HD = 104
PARTS_SIZE = 4
TOP = 2


EPSILON = 1e-06
ROOT_HALF = 0.7071067811865476
INV_ROOT_TWO_PI = 0.3989422804014327


def layer_norm(row_block, gain_vector):
    center = row_block - jnp.mean(row_block, axis=-1, keepdims=True)
    spread = jnp.mean(center * center, axis=-1, keepdims=True)
    return center * lax.rsqrt(spread + EPSILON) * gain_vector


def gelu_parts(preact):
    half_cdf = 0.5 * (1.0 + lax.erf(preact * ROOT_HALF))
    slope = half_cdf + preact * INV_ROOT_TWO_PI * jnp.exp(-0.5 * preact * preact)
    return preact * half_cdf, slope


def project_in(picture, first_gain, in_projection):
    normed = layer_norm(picture, first_gain).astype(jnp.bfloat16)
    return jnp.dot(normed, in_projection, preferred_element_type=jnp.float32).astype(jnp.bfloat16)


def attend(picture, joined, out_projection):
    seq_len = picture.shape[0]
    head_width = out_projection.shape[0]
    head_count = head_width // HD
    queries = joined[:, :head_width].reshape(seq_len, head_count, HD)
    key_rows = joined[:, head_width : 2 * head_width].reshape(seq_len, head_count, HD)
    value_rows = joined[:, 2 * head_width :].reshape(seq_len, head_count, HD)
    scores = jnp.einsum(
        "qhd,khd->hqk", queries, key_rows, preferred_element_type=jnp.float32
    ) * HD ** (-0.5)
    weights = jnp.exp(scores)
    attention = (weights / jnp.sum(weights, axis=-1, keepdims=True)).astype(jnp.bfloat16)
    context = jnp.einsum(
        "hqk,khd->qhd", attention, value_rows, preferred_element_type=jnp.float32
    ).astype(jnp.bfloat16)
    return picture + jnp.dot(
        context.reshape(seq_len, head_width), out_projection, preferred_element_type=jnp.float32
    )


def params():
    return pltpu.CompilerParams(vmem_limit_bytes=60 * 1024 * 1024)


SMALL = pl.CostEstimate(flops=1000, bytes_accessed=1000, transcendentals=0)
SCALARS = pl.BlockSpec(memory_space=pltpu.SMEM)
UNREAD = pl.BlockSpec(memory_space=pl.ANY)


def slot_table(spots_ref, slots_ref, images, sections, count):
    capacity = count // images
    rows = []
    for d in range(sections):
        columns = []
        for i in range(images):
            slots = slots_ref[spots_ref[i]][d : d + 1, :]
            lanes = lax.broadcasted_iota(jnp.int32, (count, slots.shape[1]), 0)
            hit = (lanes == slots + i * capacity) & (slots >= 0)
            columns.append(jnp.where(hit, 1.0, 0.0))
        rows.append(jnp.concatenate(columns, axis=1))
    return jnp.concatenate(rows, axis=0)


def pack_kernel(images, sections, inputs, together, *refs):
    spots_ref, slots_ref = refs[:2]
    dense = refs[2 : 2 + inputs]
    parts = 1 if together else sections
    if inputs > 1:
        joined, blocks = refs[-1], refs[-1 - parts : -1]
        seq_len = dense[0].shape[0]
        for i in range(images):
            joined[i * seq_len : (i + 1) * seq_len, :] = dense[i][...]
    else:
        joined, blocks = dense[0], refs[-parts:]
    count = blocks[0].shape[-2]
    table = slot_table(spots_ref, slots_ref, images, sections, count).astype(jnp.bfloat16)
    total = jnp.dot(table, joined[...], preferred_element_type=jnp.float32).astype(jnp.bfloat16)
    for d in range(sections):
        block = total[d * count : (d + 1) * count, :]
        if together:
            blocks[0][spots_ref[images + 1 + d]] = block
        else:
            blocks[d][...] = block


def pack(spots, slots, dense, capacity, after=(), together=False):
    sections, seq_len = slots.shape[1:]
    width = dense[0].shape[1]
    inputs = len(dense)
    images = sum(block.shape[0] for block in dense) // seq_len
    count = images * capacity
    whole = pl.BlockSpec(memory_space=pltpu.VMEM)
    if together:
        shapes = [jax.ShapeDtypeStruct((sections, count, width), jnp.bfloat16)]
    else:
        shapes = [jax.ShapeDtypeStruct((count, width), jnp.bfloat16)] * sections
    parts = len(shapes)
    if inputs > 1:
        shapes.append(jax.ShapeDtypeStruct((images * seq_len, width), jnp.bfloat16))
    results = pl.pallas_call(
        partial(pack_kernel, images, sections, inputs, together),
        name="pack",
        in_specs=[SCALARS] + [whole] * (1 + inputs) + [UNREAD] * len(after),
        out_specs=[whole] * len(shapes),
        out_shape=shapes,
        compiler_params=params(),
        cost_estimate=SMALL,
    )(spots, slots, *dense, *after)
    return results[:parts], results[parts:]


EXTRA = 16


def unpack_kernel(images, sections, parts, extra, scored, *refs):
    spots_ref, slots_ref = refs[:2]
    blocks = refs[2 : 2 + parts]
    addend = refs[2 + parts : 2 + parts + extra]
    partners = refs[2 + parts + extra : 2 + parts + extra + scored]
    joined = refs[-1]
    dense = refs[-1 - (images if extra or scored else 1) : -1]
    count = blocks[0].shape[-2]
    seq_len = slots_ref.shape[2]
    for d in range(sections):
        block = blocks[d][...] if parts > 1 else blocks[0][spots_ref[images + 1 + d]]
        joined[d * count : (d + 1) * count, :] = block
    table = slot_table(spots_ref, slots_ref, images, sections, count)
    total = jnp.dot(
        table.T.astype(jnp.bfloat16), joined[...], preferred_element_type=jnp.float32
    )
    if scored:
        lines = []
        for d in range(sections):
            product = joined[d * count : (d + 1) * count, :].astype(jnp.float32)
            product = product * partners[0][spots_ref[images + 1 + d]].astype(jnp.float32)
            column = jnp.sum(product, axis=1, keepdims=True)
            lines.append(
                jnp.sum(table[d * count : (d + 1) * count, :] * column, axis=0, keepdims=True)
            )
        lines = jnp.concatenate(
            lines + [jnp.zeros((EXTRA - sections, lines[0].shape[1]), jnp.float32)], axis=0
        )
    if not (extra or scored):
        dense[0][...] = total.astype(jnp.bfloat16)
        return
    for i in range(images):
        part = total[i * seq_len : (i + 1) * seq_len, :]
        if extra:
            part = part + addend[0][i * seq_len : (i + 1) * seq_len, :].astype(jnp.float32)
        dense[i][:seq_len, :] = part.astype(jnp.bfloat16)
        if scored:
            dense[i][seq_len:, :] = jnp.zeros((EXTRA, total.shape[1]), jnp.bfloat16)
            dense[i][seq_len:, :seq_len] = lines[:, i * seq_len : (i + 1) * seq_len].astype(
                jnp.bfloat16
            )


def unpack(spots, slots, blocks, images, addend=(), partners=(), after=()):
    sections, seq_len = slots.shape[1:]
    count, width = blocks[0].shape[-2:]
    whole = pl.BlockSpec(memory_space=pltpu.VMEM)
    inputs = len(blocks) + len(addend) + len(partners)
    height = seq_len + (EXTRA if partners else 0)
    parts = images if addend or partners else 1
    if parts == 1:
        height = images * seq_len
    return pl.pallas_call(
        partial(unpack_kernel, images, sections, len(blocks), len(addend), len(partners)),
        name="unpack",
        in_specs=[SCALARS] + [whole] * (1 + inputs) + [UNREAD] * len(after),
        out_specs=[whole] * parts,
        out_shape=[jax.ShapeDtypeStruct((height, width), jnp.bfloat16)] * parts,
        scratch_shapes=[pltpu.VMEM((sections * count, width), jnp.bfloat16)],
        compiler_params=params(),
        cost_estimate=SMALL,
    )(spots, slots, *blocks, *addend, *partners, *after)


def merge_kernel(sections, spots_ref, *refs):
    met, merged = refs[sections], refs[-1]
    count = merged.shape[1]
    first = spots_ref.shape[0] - sections
    for d in range(sections):
        total = refs[d][...].astype(jnp.float32)
        total = total + met[d * count : (d + 1) * count, :].astype(jnp.float32)
        merged[spots_ref[first + d]] = total.astype(jnp.bfloat16)


def merge(spots, blocks, met, after=()):
    sections = len(blocks)
    whole = pl.BlockSpec(memory_space=pltpu.VMEM)
    return pl.pallas_call(
        partial(merge_kernel, sections),
        name="merge",
        in_specs=[SCALARS] + [whole] * (sections + 1) + [UNREAD] * len(after),
        out_specs=whole,
        out_shape=jax.ShapeDtypeStruct((sections,) + blocks[0].shape, jnp.bfloat16),
        compiler_params=params(),
        cost_estimate=SMALL,
    )(spots, *blocks, met, *after)


def expert_kernel(sections, images, split, unread, *refs):
    spots_ref, other_ref, router_ref = refs[:3]
    mixed_in = refs[3 : 3 + sections]
    grads_in, up_ref, down_ref = refs[3 + sections : 6 + sections]
    outs = refs[6 + sections + unread :]
    mixed, grads, out_sum, grad_sum, gate_ref = outs[-5:]
    out_parts, grad_parts = outs[:split], outs[split:-5]
    step, last = pl.program_id(0), pl.num_programs(0) - 1
    count = mixed_in[0].shape[0]
    total = count * sections
    capacity = count // images
    at_row = lax.broadcasted_iota(jnp.int32, (count, capacity), 0)
    at_slot = lax.broadcasted_iota(jnp.int32, (count, capacity), 1)

    @pl.when(step == 0)
    def _():
        others = []
        for d in range(sections):
            mixed[d * count : (d + 1) * count, :] = mixed_in[d][...]
            grads[d * count : (d + 1) * count, :] = grads_in[spots_ref[images + 1 + d]]
            column = jnp.zeros((count, 1), jnp.int32)
            for i in range(images):
                ids = other_ref[spots_ref[images + 1 + d], pl.ds(spots_ref[i], 1), :]
                own = at_row == at_slot + i * capacity
                column = column + jnp.sum(jnp.where(own, ids, 0), axis=1, keepdims=True)
            others.append(column)
        logits = jnp.dot(mixed[...], router_ref[...], preferred_element_type=jnp.float32)
        lanes = lax.broadcasted_iota(jnp.int32, logits.shape, 1)
        mine = jnp.sum(jnp.where(lanes == spots_ref[images], logits, 0.0), axis=1, keepdims=True)
        is_other = lanes == jnp.concatenate(others, axis=0)
        other = jnp.sum(jnp.where(is_other, logits, 0.0), axis=1, keepdims=True)
        gate_ref[...] = 1.0 / (1.0 + jnp.exp(other - mine))
        out_sum[...] = jnp.zeros_like(out_sum)
        grad_sum[...] = jnp.zeros_like(grad_sum)

    gate = gate_ref[...]
    preact = jnp.dot(mixed[...], up_ref[...], preferred_element_type=jnp.float32)
    pulled = gate * lax.dot_general(
        grads[...], down_ref[...], (((1,), (1,)), ((), ())), preferred_element_type=jnp.float32
    )
    hidden_wide, slope = gelu_parts(preact)
    hidden = hidden_wide.astype(jnp.bfloat16)
    hidden_grad = (pulled * slope).astype(jnp.bfloat16)
    out_sum[...] += jnp.dot(hidden, down_ref[...], preferred_element_type=jnp.float32)
    grad_sum[...] += lax.dot_general(
        hidden_grad, up_ref[...], (((1,), (1,)), ((), ())), preferred_element_type=jnp.float32
    )

    @pl.when(step == last)
    def _():
        size = total // split
        for part in range(split):
            rows = slice(part * size, (part + 1) * size)
            out_parts[part][...] = (out_sum[rows, :] * gate[rows, :]).astype(jnp.bfloat16)
        for d in range(sections):
            block = grad_sum[d * count : (d + 1) * count, :].astype(jnp.bfloat16)
            if split > 1:
                grad_parts[0][spots_ref[images + 1 + d]] = block
            else:
                grad_parts[d][...] = block


def expert_unit(spots, others, router, mixed_in, grads_in, up_local, down_local, split, after=()):
    sections = len(mixed_in)
    images = spots.shape[0] - 1 - sections
    count, width = mixed_in[0].shape
    total = count * sections
    hidden_units = up_local.shape[1]
    tile = 512
    assert hidden_units // tile >= 2

    def whole(shape):
        return pl.BlockSpec(shape, lambda f: (0,) * len(shape))

    block = whole((count, width))
    shapes = [(total // split, width)] * split
    shapes += [(sections, count, width)] if split > 1 else [(count, width)] * sections
    results = pl.pallas_call(
        partial(expert_kernel, sections, images, split, len(after)),
        name="expert",
        grid=(hidden_units // tile,),
        in_specs=[SCALARS, whole(others.shape), whole(router.shape)]
        + [block] * sections
        + [whole(grads_in.shape)]
        + [
            pl.BlockSpec((width, tile), lambda f: (0, f)),
            pl.BlockSpec((tile, width), lambda f: (f, 0)),
        ]
        + [UNREAD] * len(after),
        out_specs=[whole(shape) for shape in shapes],
        out_shape=[jax.ShapeDtypeStruct(shape, jnp.bfloat16) for shape in shapes],
        scratch_shapes=[
            pltpu.VMEM((total, width), jnp.bfloat16),
            pltpu.VMEM((total, width), jnp.bfloat16),
            pltpu.VMEM((total, width), jnp.float32),
            pltpu.VMEM((total, width), jnp.float32),
            pltpu.VMEM((total, 1), jnp.float32),
        ],
        compiler_params=params(),
        cost_estimate=SMALL,
    )(spots, others, router, *mixed_in, grads_in, up_local, down_local, *after)
    return results[:split], results[split:]


def shards(
    tokens,
    route_ids,
    cotangent,
    first_gain,
    in_projection,
    out_projection,
    second_gain,
    router_weight,
    up_weight,
    down_weight,
):
    picture = tokens[0, 0].astype(jnp.float32)
    chosen = route_ids[0, 0]
    upstream = cotangent[0, 0]
    up_local = up_weight[0, 0]
    down_local = down_weight[0, 0]
    seq_len, width = picture.shape
    experts = router_weight.shape[1]
    sections = lax.axis_size("segment")
    members = lax.axis_size("expert")
    per_section = members // PARTS_SIZE
    capacity = 3 * seq_len // experts
    line = members // 2
    here = lax.axis_index("expert")
    section = lax.axis_index("segment")
    place, side = here // 2, here % 2
    group = here // PARTS_SIZE
    my_expert = section * per_section + group
    relative = section ^ jnp.arange(sections)
    experts_here = relative * per_section + group

    def along(value, steps):
        pairs = [(j, (j + 2 * steps) % members) for j in range(members)]
        return lax.ppermute(value, "expert", pairs)

    def across(value):
        return lax.ppermute(value, "expert", [(j, j ^ 1) for j in range(members)])

    def deal(blocks):
        moved = [blocks[0]]
        for d in range(1, sections):
            pairs = [(s, s ^ d) for s in range(sections)]
            moved.append(lax.ppermute(blocks[d], "segment", pairs))
        return moved

    def deal_whole(value):
        return lax.all_to_all(value, "segment", split_axis=0, concat_axis=0, tiled=True)

    def deal_small(value):
        return lax.all_to_all(
            jnp.take(value, relative, axis=0), "segment", split_axis=0, concat_axis=0, tiled=True
        )

    chunks = [list(range(line - 2, -1, -2)), list(range(line - 1, 0, -2))]

    expert_list = jnp.arange(experts)
    hits = jnp.any(chosen.T[None] == expert_list[:, None, None], axis=1)
    tokens_before = jnp.arange(seq_len)[:, None] < jnp.arange(seq_len)[None, :]
    own_slots = jnp.dot(
        hits.astype(jnp.bfloat16),
        tokens_before.astype(jnp.bfloat16),
        preferred_element_type=jnp.float32,
    ).astype(jnp.int32)
    own_slots = jnp.where(hits, own_slots, -1)
    others = jnp.sum(chosen, axis=1)[None, :] - expert_list[:, None]
    at_slot = own_slots[:, None, :] == jnp.arange(capacity)[None, :, None]
    own_others = jnp.sum(jnp.where(at_slot, others[:, None, :], 0), axis=2)
    wide = jnp.concatenate([own_slots, own_others], axis=1)
    wide = jnp.take(wide.reshape(sections, per_section, -1), relative, axis=0).transpose(1, 0, 2)
    wide = jnp.broadcast_to(
        wide[:, None], (per_section, PARTS_SIZE) + wide.shape[1:]
    ).reshape(members, -1)
    lane = lax.all_to_all(wide, "expert", split_axis=0, concat_axis=0, tiled=True).reshape(
        members, sections, seq_len + capacity
    )
    slots = lane[:, :, :seq_len]
    slot_others = deal_small(lane[:, :, seq_len:].transpose(1, 0, 2))

    def spots_of(index, far):
        places = (place - jnp.array(chunks[index])) % line
        side_of = (1 - side) if far else side
        return jnp.concatenate(
            [2 * places + side_of, my_expert.reshape(1), relative]
        ).astype(jnp.int32)

    spots = {(index, far): spots_of(index, far) for index in (0, 1) for far in (0, 1)}

    early = {1, line - 1}
    cot_dense = {0: upstream}
    for step in sorted(early):
        cot_dense[step] = along(upstream, step)
    slots, late_upstream = lax.optimization_barrier((slots, upstream))
    for step in range(1, line):
        if step not in early:
            cot_dense[step] = along(late_upstream, step)

    def cot_pack(index):
        dense = [cot_dense[step] for step in chunks[index]]
        return pack(spots[index, 0], slots, dense, capacity, together=True)[0][0]

    joined, project_back = jax.vjp(
        partial(project_in, first_gain=first_gain, in_projection=in_projection), picture
    )
    cot_packed, cot_rows = {}, {}
    cot_packed[1] = cot_pack(1)
    joined, cot_packed[1] = lax.optimization_barrier((joined, cot_packed[1]))
    cot_rows[1, 0] = deal_whole(cot_packed[1])
    residual, attend_back = jax.vjp(partial(attend, out_projection=out_projection), picture, joined)
    residual, slot_others = lax.optimization_barrier((residual, slot_others))
    normed, norm_back = jax.vjp(partial(layer_norm, gain_vector=second_gain), residual)
    mixed = normed.astype(jnp.bfloat16)
    own_logits = jnp.dot(mixed, router_weight, preferred_element_type=jnp.float32)

    mixed_dense = {0: mixed}
    for step in range(1, line):
        mixed_dense[step] = along(mixed, step)

    cot_rows[1, 1] = across(cot_rows[1, 0])
    cot_packed[0] = cot_pack(0)
    cot_rows[0, 0] = deal_whole(cot_packed[0])

    mixed_rows, far_dense = {}, {}

    def mixed_pack(index, after):
        dense = [mixed_dense[step] for step in chunks[index]]
        blocks, joined_dense = pack(spots[index, 0], slots, dense, capacity, after)
        far_dense[index] = across(joined_dense[0])
        mixed_rows[index, 0] = deal(blocks)
        return (blocks[0],)

    def far_pack(index, after):
        blocks, _ = pack(spots[index, 1], slots, [far_dense[index]], capacity, after)
        mixed_rows[index, 1] = deal(blocks)
        return (blocks[0],)

    outs, grads = {}, {}

    def unit(index, far, after):
        outs[index, far], grads[index, far] = expert_unit(
            spots[index, far],
            slot_others,
            router_weight,
            mixed_rows[index, far],
            cot_rows[index, far],
            up_local,
            down_local,
            1 if far else sections,
            after,
        )
        done = (grads[index, far][0],)
        if far:
            grads[index, far] = deal(grads[index, far])
        else:
            grads[index, far] = [deal_whole(grads[index, far][0])]
        return done

    done = mixed_pack(1, (cot_packed[0],))
    done = mixed_pack(0, done + (cot_rows[1, 1],))
    cot_rows[0, 1] = across(cot_rows[0, 0])
    done = far_pack(1, done)
    done = far_pack(0, done)
    done = unit(1, 0, done + tuple(mixed_rows[1, 1][1:]))
    done = unit(0, 0, done + tuple(mixed_rows[0, 1][1:]))
    done = unit(1, 1, done)
    met = {1: across(outs[1, 1][0])}
    done = unit(0, 1, done + tuple(grads[1, 0]))
    met[0] = across(outs[0, 1][0])

    grad_far, out_back, out_dense, grad_dense = {}, {}, {}, {}
    for index in (1, 0):
        count = len(chunks[index])
        if index == 0:
            done += tuple(grads[0, 0])
        grad_far[index] = unpack(spots[index, 1], slots, grads[index, 1], count, after=done)[0]
        done = (grad_far[index],)
        grad_far[index] = across(grad_far[index])
        merged = merge(spots[index, 0], outs[index, 0], met[index], done)
        done = (merged,)
        out_back[index] = deal_whole(merged)
    for index in (1, 0):
        chunk = chunks[index]
        count = len(chunk)
        out_block = unpack(
            spots[index, 0], slots, [out_back[index]], count, (), [cot_packed[index]], done
        )
        done = (out_block[0],)
        grad_block = unpack(
            spots[index, 0], slots, grads[index, 0], count, (grad_far[index],), (), done
        )
        done = (grad_block[0],)
        for spot, step in enumerate(chunk):
            part_out, part_grad = out_block[spot], grad_block[spot]
            out_dense[step] = along(part_out, -step) if step else part_out
            grad_dense[step] = along(part_grad, -step) if step else part_grad
        done += tuple(out_dense[step] for step in chunk if step)

    expert_total = sum(out_dense[step][:seq_len].astype(jnp.float32) for step in range(line))
    input_total = sum(grad_dense[step].astype(jnp.float32) for step in range(line))
    layer_out = (residual + expert_total).astype(jnp.bfloat16)

    named = chosen[:, :, None] == expert_list
    score_lines = jnp.zeros((per_section, sections, seq_len), jnp.float32)
    for step in range(line):
        sender = 2 * ((place + step) % line) // PARTS_SIZE
        lines = out_dense[step][seq_len : seq_len + sections, :seq_len].astype(jnp.float32)
        score_lines += jnp.where((jnp.arange(per_section) == sender)[:, None, None], lines, 0.0)
    token_scores = (
        jnp.take(score_lines, relative, axis=1).transpose(1, 0, 2).reshape(experts, seq_len).T
    )
    picked_logit = jnp.sum(jnp.where(named, own_logits[:, None, :], 0.0), axis=2)
    gate_values = 1.0 / (1.0 + jnp.exp(picked_logit[:, ::-1] - picked_logit))
    gate_spread = jnp.sum(jnp.where(named, gate_values[:, :, None], 0.0), axis=1)
    spread_grad = token_scores - gate_spread * jnp.sum(token_scores, axis=1, keepdims=True)
    mixed_grad = input_total + jnp.einsum(
        "se,de->sd", spread_grad, router_weight.astype(jnp.float32), precision=lax.Precision.HIGHEST
    )
    residual_grad = upstream.astype(jnp.float32) + norm_back(mixed_grad)[0]
    picture_grad, joined_grad = attend_back(residual_grad)
    input_grad = (picture_grad + project_back(joined_grad)[0]).astype(jnp.bfloat16)
    return (layer_out[None, None], input_grad[None, None])


def solution(mesh):
    placed = (
        P("segment", "expert", None, None),
        P("segment", "expert", None, None),
        P("segment", "expert", None, None),
        P(),
        P(),
        P(),
        P(),
        P(),
        P("segment", "expert", None, None),
        P("segment", "expert", None, None),
    )
    return jax.shard_map(
        shards,
        mesh=mesh,
        in_specs=placed,
        out_specs=(P("segment", "expert", None, None), P("segment", "expert", None, None)),
        check_vma=False,
    )
```

```python
from functools import partial

import jax
import jax.numpy as jnp
from jax import lax
from jax.experimental import pallas as pl
from jax.experimental.pallas import tpu as pltpu
from jax.sharding import PartitionSpec as P

HD = 104
PARTS_SIZE = 4
TOP = 2


EPSILON = 1e-06
ROOT_HALF = 0.7071067811865476
INV_ROOT_TWO_PI = 0.3989422804014327


def layer_norm(row_block, gain_vector):
    center = row_block - jnp.mean(row_block, axis=-1, keepdims=True)
    spread = jnp.mean(center * center, axis=-1, keepdims=True)
    return center * lax.rsqrt(spread + EPSILON) * gain_vector


def gelu_parts(preact):
    half_cdf = 0.5 * (1.0 + lax.erf(preact * ROOT_HALF))
    slope = half_cdf + preact * INV_ROOT_TWO_PI * jnp.exp(-0.5 * preact * preact)
    return preact * half_cdf, slope


def project_in(picture, first_gain, in_projection):
    normed = layer_norm(picture, first_gain).astype(jnp.bfloat16)
    return jnp.dot(normed, in_projection, preferred_element_type=jnp.float32).astype(jnp.bfloat16)


def attend(picture, joined, out_projection):
    seq_len = picture.shape[0]
    head_width = out_projection.shape[0]
    head_count = head_width // HD
    queries = joined[:, :head_width].reshape(seq_len, head_count, HD)
    key_rows = joined[:, head_width : 2 * head_width].reshape(seq_len, head_count, HD)
    value_rows = joined[:, 2 * head_width :].reshape(seq_len, head_count, HD)
    scores = jnp.einsum(
        "qhd,khd->hqk", queries, key_rows, preferred_element_type=jnp.float32
    ) * HD ** (-0.5)
    weights = jnp.exp(scores)
    attention = (weights / jnp.sum(weights, axis=-1, keepdims=True)).astype(jnp.bfloat16)
    context = jnp.einsum(
        "hqk,khd->qhd", attention, value_rows, preferred_element_type=jnp.float32
    ).astype(jnp.bfloat16)
    return picture + jnp.dot(
        context.reshape(seq_len, head_width), out_projection, preferred_element_type=jnp.float32
    )


def params():
    return pltpu.CompilerParams(vmem_limit_bytes=60 * 1024 * 1024)


SMALL = pl.CostEstimate(flops=1000, bytes_accessed=1000, transcendentals=0)
SCALARS = pl.BlockSpec(memory_space=pltpu.SMEM)
UNREAD = pl.BlockSpec(memory_space=pl.ANY)


def slot_table(spots_ref, slots_ref, images, sections, count):
    capacity = count // images
    rows = []
    for d in range(sections):
        columns = []
        for i in range(images):
            slots = slots_ref[spots_ref[i]][d : d + 1, :]
            lanes = lax.broadcasted_iota(jnp.int32, (count, slots.shape[1]), 0)
            hit = (lanes == slots + i * capacity) & (slots >= 0)
            columns.append(jnp.where(hit, 1.0, 0.0))
        rows.append(jnp.concatenate(columns, axis=1))
    return jnp.concatenate(rows, axis=0)


def pack_kernel(images, sections, inputs, together, *refs):
    spots_ref, slots_ref = refs[:2]
    dense = refs[2 : 2 + inputs]
    parts = 1 if together else sections
    if inputs > 1:
        joined, blocks = refs[-1], refs[-1 - parts : -1]
        seq_len = dense[0].shape[0]
        for i in range(images):
            joined[i * seq_len : (i + 1) * seq_len, :] = dense[i][...]
    else:
        joined, blocks = dense[0], refs[-parts:]
    count = blocks[0].shape[-2]
    table = slot_table(spots_ref, slots_ref, images, sections, count).astype(jnp.bfloat16)
    total = jnp.dot(table, joined[...], preferred_element_type=jnp.float32).astype(jnp.bfloat16)
    for d in range(sections):
        block = total[d * count : (d + 1) * count, :]
        if together:
            blocks[0][spots_ref[images + 1 + d]] = block
        else:
            blocks[d][...] = block


def pack(spots, slots, dense, capacity, after=(), together=False):
    sections, seq_len = slots.shape[1:]
    width = dense[0].shape[1]
    inputs = len(dense)
    images = sum(block.shape[0] for block in dense) // seq_len
    count = images * capacity
    whole = pl.BlockSpec(memory_space=pltpu.VMEM)
    if together:
        shapes = [jax.ShapeDtypeStruct((sections, count, width), jnp.bfloat16)]
    else:
        shapes = [jax.ShapeDtypeStruct((count, width), jnp.bfloat16)] * sections
    parts = len(shapes)
    if inputs > 1:
        shapes.append(jax.ShapeDtypeStruct((images * seq_len, width), jnp.bfloat16))
    results = pl.pallas_call(
        partial(pack_kernel, images, sections, inputs, together),
        name="pack",
        in_specs=[SCALARS] + [whole] * (1 + inputs) + [UNREAD] * len(after),
        out_specs=[whole] * len(shapes),
        out_shape=shapes,
        compiler_params=params(),
        cost_estimate=SMALL,
    )(spots, slots, *dense, *after)
    return results[:parts], results[parts:]


EXTRA = 16


def unpack_kernel(images, sections, parts, extra, scored, *refs):
    spots_ref, slots_ref = refs[:2]
    blocks = refs[2 : 2 + parts]
    addend = refs[2 + parts : 2 + parts + extra]
    partners = refs[2 + parts + extra : 2 + parts + extra + scored]
    joined = refs[-1]
    dense = refs[-1 - (images if extra or scored else 1) : -1]
    count = blocks[0].shape[-2]
    seq_len = slots_ref.shape[2]
    for d in range(sections):
        block = blocks[d][...] if parts > 1 else blocks[0][spots_ref[images + 1 + d]]
        joined[d * count : (d + 1) * count, :] = block
    table = slot_table(spots_ref, slots_ref, images, sections, count)
    total = jnp.dot(
        table.T.astype(jnp.bfloat16), joined[...], preferred_element_type=jnp.float32
    )
    if scored:
        lines = []
        for d in range(sections):
            product = joined[d * count : (d + 1) * count, :].astype(jnp.float32)
            product = product * partners[0][spots_ref[images + 1 + d]].astype(jnp.float32)
            column = jnp.sum(product, axis=1, keepdims=True)
            lines.append(
                jnp.sum(table[d * count : (d + 1) * count, :] * column, axis=0, keepdims=True)
            )
        lines = jnp.concatenate(
            lines + [jnp.zeros((EXTRA - sections, lines[0].shape[1]), jnp.float32)], axis=0
        )
    if not (extra or scored):
        dense[0][...] = total.astype(jnp.bfloat16)
        return
    for i in range(images):
        part = total[i * seq_len : (i + 1) * seq_len, :]
        if extra:
            part = part + addend[0][i * seq_len : (i + 1) * seq_len, :].astype(jnp.float32)
        dense[i][:seq_len, :] = part.astype(jnp.bfloat16)
        if scored:
            dense[i][seq_len:, :] = jnp.zeros((EXTRA, total.shape[1]), jnp.bfloat16)
            dense[i][seq_len:, :seq_len] = lines[:, i * seq_len : (i + 1) * seq_len].astype(
                jnp.bfloat16
            )


def unpack(spots, slots, blocks, images, addend=(), partners=(), after=()):
    sections, seq_len = slots.shape[1:]
    count, width = blocks[0].shape[-2:]
    whole = pl.BlockSpec(memory_space=pltpu.VMEM)
    inputs = len(blocks) + len(addend) + len(partners)
    height = seq_len + (EXTRA if partners else 0)
    parts = images if addend or partners else 1
    if parts == 1:
        height = images * seq_len
    return pl.pallas_call(
        partial(unpack_kernel, images, sections, len(blocks), len(addend), len(partners)),
        name="unpack",
        in_specs=[SCALARS] + [whole] * (1 + inputs) + [UNREAD] * len(after),
        out_specs=[whole] * parts,
        out_shape=[jax.ShapeDtypeStruct((height, width), jnp.bfloat16)] * parts,
        scratch_shapes=[pltpu.VMEM((sections * count, width), jnp.bfloat16)],
        compiler_params=params(),
        cost_estimate=SMALL,
    )(spots, slots, *blocks, *addend, *partners, *after)


def merge_kernel(sections, spots_ref, *refs):
    met, merged = refs[sections], refs[-1]
    count = merged.shape[1]
    first = spots_ref.shape[0] - sections
    for d in range(sections):
        total = refs[d][...].astype(jnp.float32)
        total = total + met[d * count : (d + 1) * count, :].astype(jnp.float32)
        merged[spots_ref[first + d]] = total.astype(jnp.bfloat16)


def merge(spots, blocks, met, after=()):
    sections = len(blocks)
    whole = pl.BlockSpec(memory_space=pltpu.VMEM)
    return pl.pallas_call(
        partial(merge_kernel, sections),
        name="merge",
        in_specs=[SCALARS] + [whole] * (sections + 1) + [UNREAD] * len(after),
        out_specs=whole,
        out_shape=jax.ShapeDtypeStruct((sections,) + blocks[0].shape, jnp.bfloat16),
        compiler_params=params(),
        cost_estimate=SMALL,
    )(spots, *blocks, met, *after)


def expert_kernel(sections, images, split, unread, *refs):
    spots_ref, other_ref, router_ref = refs[:3]
    mixed_in = refs[3 : 3 + sections]
    grads_in, up_ref, down_ref = refs[3 + sections : 6 + sections]
    outs = refs[6 + sections + unread :]
    mixed, grads, out_sum, grad_sum, gate_ref = outs[-5:]
    out_parts, grad_parts = outs[:split], outs[split:-5]
    step, last = pl.program_id(0), pl.num_programs(0) - 1
    count = mixed_in[0].shape[0]
    total = count * sections
    capacity = count // images
    at_row = lax.broadcasted_iota(jnp.int32, (count, capacity), 0)
    at_slot = lax.broadcasted_iota(jnp.int32, (count, capacity), 1)

    @pl.when(step == 0)
    def _():
        others = []
        for d in range(sections):
            mixed[d * count : (d + 1) * count, :] = mixed_in[d][...]
            grads[d * count : (d + 1) * count, :] = grads_in[spots_ref[images + 1 + d]]
            column = jnp.zeros((count, 1), jnp.int32)
            for i in range(images):
                ids = other_ref[spots_ref[images + 1 + d], pl.ds(spots_ref[i], 1), :]
                own = at_row == at_slot + i * capacity
                column = column + jnp.sum(jnp.where(own, ids, 0), axis=1, keepdims=True)
            others.append(column)
        logits = jnp.dot(mixed[...], router_ref[...], preferred_element_type=jnp.float32)
        lanes = lax.broadcasted_iota(jnp.int32, logits.shape, 1)
        mine = jnp.sum(jnp.where(lanes == spots_ref[images], logits, 0.0), axis=1, keepdims=True)
        is_other = lanes == jnp.concatenate(others, axis=0)
        other = jnp.sum(jnp.where(is_other, logits, 0.0), axis=1, keepdims=True)
        gate_ref[...] = 1.0 / (1.0 + jnp.exp(other - mine))
        out_sum[...] = jnp.zeros_like(out_sum)
        grad_sum[...] = jnp.zeros_like(grad_sum)

    gate = gate_ref[...]
    preact = jnp.dot(mixed[...], up_ref[...], preferred_element_type=jnp.float32)
    pulled = gate * lax.dot_general(
        grads[...], down_ref[...], (((1,), (1,)), ((), ())), preferred_element_type=jnp.float32
    )
    hidden_wide, slope = gelu_parts(preact)
    hidden = hidden_wide.astype(jnp.bfloat16)
    hidden_grad = (pulled * slope).astype(jnp.bfloat16)
    out_sum[...] += jnp.dot(hidden, down_ref[...], preferred_element_type=jnp.float32)
    grad_sum[...] += lax.dot_general(
        hidden_grad, up_ref[...], (((1,), (1,)), ((), ())), preferred_element_type=jnp.float32
    )

    @pl.when(step == last)
    def _():
        size = total // split
        for part in range(split):
            rows = slice(part * size, (part + 1) * size)
            out_parts[part][...] = (out_sum[rows, :] * gate[rows, :]).astype(jnp.bfloat16)
        for d in range(sections):
            block = grad_sum[d * count : (d + 1) * count, :].astype(jnp.bfloat16)
            if split > 1:
                grad_parts[0][spots_ref[images + 1 + d]] = block
            else:
                grad_parts[d][...] = block


def expert_unit(spots, others, router, mixed_in, grads_in, up_local, down_local, split, after=()):
    sections = len(mixed_in)
    images = spots.shape[0] - 1 - sections
    count, width = mixed_in[0].shape
    total = count * sections
    hidden_units = up_local.shape[1]
    tile = 512
    assert hidden_units // tile >= 2

    def whole(shape):
        return pl.BlockSpec(shape, lambda f: (0,) * len(shape))

    block = whole((count, width))
    shapes = [(total // split, width)] * split
    shapes += [(sections, count, width)] if split > 1 else [(count, width)] * sections
    results = pl.pallas_call(
        partial(expert_kernel, sections, images, split, len(after)),
        name="expert",
        grid=(hidden_units // tile,),
        in_specs=[SCALARS, whole(others.shape), whole(router.shape)]
        + [block] * sections
        + [whole(grads_in.shape)]
        + [
            pl.BlockSpec((width, tile), lambda f: (0, f)),
            pl.BlockSpec((tile, width), lambda f: (f, 0)),
        ]
        + [UNREAD] * len(after),
        out_specs=[whole(shape) for shape in shapes],
        out_shape=[jax.ShapeDtypeStruct(shape, jnp.bfloat16) for shape in shapes],
        scratch_shapes=[
            pltpu.VMEM((total, width), jnp.bfloat16),
            pltpu.VMEM((total, width), jnp.bfloat16),
            pltpu.VMEM((total, width), jnp.float32),
            pltpu.VMEM((total, width), jnp.float32),
            pltpu.VMEM((total, 1), jnp.float32),
        ],
        compiler_params=params(),
        cost_estimate=SMALL,
    )(spots, others, router, *mixed_in, grads_in, up_local, down_local, *after)
    return results[:split], results[split:]


def shards(
    tokens,
    route_ids,
    cotangent,
    first_gain,
    in_projection,
    out_projection,
    second_gain,
    router_weight,
    up_weight,
    down_weight,
):
    picture = tokens[0, 0].astype(jnp.float32)
    chosen = route_ids[0, 0]
    upstream = cotangent[0, 0]
    up_local = up_weight[0, 0]
    down_local = down_weight[0, 0]
    seq_len, width = picture.shape
    experts = router_weight.shape[1]
    sections = lax.axis_size("segment")
    members = lax.axis_size("expert")
    per_section = members // PARTS_SIZE
    capacity = 3 * seq_len // experts
    line = members // 2
    here = lax.axis_index("expert")
    section = lax.axis_index("segment")
    place, side = here // 2, here % 2
    group = here // PARTS_SIZE
    my_expert = section * per_section + group
    relative = section ^ jnp.arange(sections)
    experts_here = relative * per_section + group

    def along(value, steps):
        pairs = [(j, (j + 2 * steps) % members) for j in range(members)]
        return lax.ppermute(value, "expert", pairs)

    def across(value):
        return lax.ppermute(value, "expert", [(j, j ^ 1) for j in range(members)])

    def deal(blocks):
        moved = [blocks[0]]
        for d in range(1, sections):
            pairs = [(s, s ^ d) for s in range(sections)]
            moved.append(lax.ppermute(blocks[d], "segment", pairs))
        return moved

    def deal_whole(value):
        return lax.all_to_all(value, "segment", split_axis=0, concat_axis=0, tiled=True)

    def deal_small(value):
        return lax.all_to_all(
            jnp.take(value, relative, axis=0), "segment", split_axis=0, concat_axis=0, tiled=True
        )

    half = line // 2
    chunks = [list(range(line - 1, half - 1, -1)), list(range(half - 1, -1, -1))]

    expert_list = jnp.arange(experts)
    hits = jnp.any(chosen.T[None] == expert_list[:, None, None], axis=1)
    tokens_before = jnp.arange(seq_len)[:, None] < jnp.arange(seq_len)[None, :]
    own_slots = jnp.dot(
        hits.astype(jnp.bfloat16),
        tokens_before.astype(jnp.bfloat16),
        preferred_element_type=jnp.float32,
    ).astype(jnp.int32)
    own_slots = jnp.where(hits, own_slots, -1)
    others = jnp.sum(chosen, axis=1)[None, :] - expert_list[:, None]
    at_slot = own_slots[:, None, :] == jnp.arange(capacity)[None, :, None]
    own_others = jnp.sum(jnp.where(at_slot, others[:, None, :], 0), axis=2)
    wide = jnp.concatenate([own_slots, own_others], axis=1)
    wide = jnp.take(wide.reshape(sections, per_section, -1), relative, axis=0).transpose(1, 0, 2)
    wide = jnp.broadcast_to(
        wide[:, None], (per_section, PARTS_SIZE) + wide.shape[1:]
    ).reshape(members, -1)
    lane = lax.all_to_all(wide, "expert", split_axis=0, concat_axis=0, tiled=True).reshape(
        members, sections, seq_len + capacity
    )
    slots = lane[:, :, :seq_len]
    slot_others = deal_small(lane[:, :, seq_len:].transpose(1, 0, 2))

    def spots_of(index, far):
        places = (place - jnp.array(chunks[index])) % line
        side_of = (1 - side) if far else side
        return jnp.concatenate(
            [2 * places + side_of, my_expert.reshape(1), relative]
        ).astype(jnp.int32)

    spots = {(index, far): spots_of(index, far) for index in (0, 1) for far in (0, 1)}

    early = {1}
    cot_dense = {0: upstream}
    for step in sorted(early):
        cot_dense[step] = along(upstream, step)
    slots, late_upstream = lax.optimization_barrier((slots, upstream))
    for step in range(1, line):
        if step not in early:
            cot_dense[step] = along(late_upstream, step)

    def cot_pack(index):
        dense = [cot_dense[step] for step in chunks[index]]
        return pack(spots[index, 0], slots, dense, capacity, together=True)[0][0]

    joined, project_back = jax.vjp(
        partial(project_in, first_gain=first_gain, in_projection=in_projection), picture
    )
    cot_packed, cot_rows = {}, {}
    cot_packed[1] = cot_pack(1)
    joined, cot_packed[1] = lax.optimization_barrier((joined, cot_packed[1]))
    cot_rows[1, 0] = deal_whole(cot_packed[1])
    residual, attend_back = jax.vjp(partial(attend, out_projection=out_projection), picture, joined)
    residual, slot_others = lax.optimization_barrier((residual, slot_others))
    normed, norm_back = jax.vjp(partial(layer_norm, gain_vector=second_gain), residual)
    mixed = normed.astype(jnp.bfloat16)
    own_logits = jnp.dot(mixed, router_weight, preferred_element_type=jnp.float32)

    mixed_dense = {0: mixed}
    for step in range(1, line):
        mixed_dense[step] = along(mixed, step)

    cot_rows[1, 1] = across(cot_rows[1, 0])
    cot_packed[0] = cot_pack(0)
    cot_rows[0, 0] = deal_whole(cot_packed[0])

    mixed_rows, far_dense = {}, {}

    def mixed_pack(index, after):
        dense = [mixed_dense[step] for step in chunks[index]]
        blocks, joined_dense = pack(spots[index, 0], slots, dense, capacity, after)
        far_dense[index] = joined_dense[0]
        mixed_rows[index, 0] = deal(blocks)
        return (blocks[0],)

    def far_pack(index, after):
        blocks, _ = pack(spots[index, 1], slots, [far_dense[index]], capacity, after)
        mixed_rows[index, 1] = deal(blocks)
        return (blocks[0],)

    outs, grads = {}, {}

    def unit(index, far, after):
        outs[index, far], grads[index, far] = expert_unit(
            spots[index, far],
            slot_others,
            router_weight,
            mixed_rows[index, far],
            cot_rows[index, far],
            up_local,
            down_local,
            1 if far else sections,
            after,
        )
        done = (grads[index, far][0],)
        if far:
            grads[index, far] = deal(grads[index, far])
        else:
            grads[index, far] = [deal_whole(grads[index, far][0])]
        return done

    done = mixed_pack(0, (cot_rows[1, 1], cot_rows[0, 0], mixed_dense[1]))
    far_dense[0] = across(far_dense[0])
    done = mixed_pack(1, done)
    cot_rows[0, 1] = across(cot_rows[0, 0])
    done = far_pack(0, done)
    done = unit(0, 0, done)
    far_dense[1], cot_rows[0, 1] = lax.optimization_barrier((far_dense[1], cot_rows[0, 1]))
    far_dense[1] = across(far_dense[1])
    done = unit(0, 1, done)
    met = {0: across(outs[0, 1][0])}
    done = unit(1, 0, done)
    done = far_pack(1, done)

    grad_far, out_back, out_dense, grad_dense = {}, {}, {}, {}

    def unpack_far(index, after):
        count = len(chunks[index])
        block = unpack(spots[index, 1], slots, grads[index, 1], count, after=after)[0]
        grad_far[index] = across(block)
        return (block,)

    def merge_out(index, after):
        merged = merge(spots[index, 0], outs[index, 0], met[index], after)
        out_back[index] = deal_whole(merged)
        return (merged,)

    def unpack_near(index, after):
        chunk = chunks[index]
        count = len(chunk)
        out_block = unpack(
            spots[index, 0], slots, [out_back[index]], count, (), [cot_packed[index]], after
        )
        grad_block = unpack(
            spots[index, 0],
            slots,
            grads[index, 0],
            count,
            (grad_far[index],),
            (),
            (out_block[0],),
        )
        for spot, step in enumerate(chunk):
            part_out, part_grad = out_block[spot], grad_block[spot]
            out_dense[step] = along(part_out, -step) if step else part_out
            grad_dense[step] = along(part_grad, -step) if step else part_grad
        return (grad_block[0],)

    done = unpack_far(0, done)
    done = unit(1, 1, done)
    met[1] = across(outs[1, 1][0])
    done = merge_out(0, done)
    done = unpack_far(1, done)
    done = unpack_near(0, done)
    done = merge_out(1, done)
    done = unpack_near(1, done)

    expert_total = sum(out_dense[step][:seq_len].astype(jnp.float32) for step in range(line))
    input_total = sum(grad_dense[step].astype(jnp.float32) for step in range(line))
    layer_out = (residual + expert_total).astype(jnp.bfloat16)

    named = chosen[:, :, None] == expert_list
    score_lines = jnp.zeros((per_section, sections, seq_len), jnp.float32)
    for step in range(line):
        sender = 2 * ((place + step) % line) // PARTS_SIZE
        lines = out_dense[step][seq_len : seq_len + sections, :seq_len].astype(jnp.float32)
        score_lines += jnp.where((jnp.arange(per_section) == sender)[:, None, None], lines, 0.0)
    token_scores = (
        jnp.take(score_lines, relative, axis=1).transpose(1, 0, 2).reshape(experts, seq_len).T
    )
    picked_logit = jnp.sum(jnp.where(named, own_logits[:, None, :], 0.0), axis=2)
    gate_values = 1.0 / (1.0 + jnp.exp(picked_logit[:, ::-1] - picked_logit))
    gate_spread = jnp.sum(jnp.where(named, gate_values[:, :, None], 0.0), axis=1)
    spread_grad = token_scores - gate_spread * jnp.sum(token_scores, axis=1, keepdims=True)
    mixed_grad = input_total + jnp.einsum(
        "se,de->sd", spread_grad, router_weight.astype(jnp.float32), precision=lax.Precision.HIGHEST
    )
    residual_grad = upstream.astype(jnp.float32) + norm_back(mixed_grad)[0]
    picture_grad, joined_grad = attend_back(residual_grad)
    input_grad = (picture_grad + project_back(joined_grad)[0]).astype(jnp.bfloat16)
    return (layer_out[None, None], input_grad[None, None])


def solution(mesh):
    placed = (
        P("segment", "expert", None, None),
        P("segment", "expert", None, None),
        P("segment", "expert", None, None),
        P(),
        P(),
        P(),
        P(),
        P(),
        P("segment", "expert", None, None),
        P("segment", "expert", None, None),
    )
    return jax.shard_map(
        shards,
        mesh=mesh,
        in_specs=placed,
        out_specs=(P("segment", "expert", None, None), P("segment", "expert", None, None)),
        check_vma=False,
    )
```

```python
from functools import partial

import jax
import jax.numpy as jnp
from jax import lax
from jax.experimental import pallas as pl
from jax.experimental.pallas import tpu as pltpu
from jax.sharding import PartitionSpec as P

HD = 104
PARTS_SIZE = 4
TOP = 2


EPSILON = 1e-06
ROOT_HALF = 0.7071067811865476
INV_ROOT_TWO_PI = 0.3989422804014327


def layer_norm(row_block, gain_vector):
    center = row_block - jnp.mean(row_block, axis=-1, keepdims=True)
    spread = jnp.mean(center * center, axis=-1, keepdims=True)
    return center * lax.rsqrt(spread + EPSILON) * gain_vector


def gelu_parts(preact):
    half_cdf = 0.5 * (1.0 + lax.erf(preact * ROOT_HALF))
    slope = half_cdf + preact * INV_ROOT_TWO_PI * jnp.exp(-0.5 * preact * preact)
    return preact * half_cdf, slope


def project_in(picture, first_gain, in_projection):
    normed = layer_norm(picture, first_gain).astype(jnp.bfloat16)
    return jnp.dot(normed, in_projection, preferred_element_type=jnp.float32).astype(jnp.bfloat16)


def attend(picture, joined, out_projection):
    seq_len = picture.shape[0]
    head_width = out_projection.shape[0]
    head_count = head_width // HD
    queries = joined[:, :head_width].reshape(seq_len, head_count, HD)
    key_rows = joined[:, head_width : 2 * head_width].reshape(seq_len, head_count, HD)
    value_rows = joined[:, 2 * head_width :].reshape(seq_len, head_count, HD)
    scores = jnp.einsum(
        "qhd,khd->hqk", queries, key_rows, preferred_element_type=jnp.float32
    ) * HD ** (-0.5)
    weights = jnp.exp(scores)
    attention = (weights / jnp.sum(weights, axis=-1, keepdims=True)).astype(jnp.bfloat16)
    context = jnp.einsum(
        "hqk,khd->qhd", attention, value_rows, preferred_element_type=jnp.float32
    ).astype(jnp.bfloat16)
    return picture + jnp.dot(
        context.reshape(seq_len, head_width), out_projection, preferred_element_type=jnp.float32
    )


def params():
    return pltpu.CompilerParams(vmem_limit_bytes=60 * 1024 * 1024)


SMALL = pl.CostEstimate(flops=1000, bytes_accessed=1000, transcendentals=0)
SCALARS = pl.BlockSpec(memory_space=pltpu.SMEM)
UNREAD = pl.BlockSpec(memory_space=pl.ANY)


def slot_table(spots_ref, slots_ref, images, sections, count):
    capacity = count // images
    rows = []
    for d in range(sections):
        columns = []
        for i in range(images):
            slots = slots_ref[spots_ref[i]][d : d + 1, :]
            lanes = lax.broadcasted_iota(jnp.int32, (count, slots.shape[1]), 0)
            hit = (lanes == slots + i * capacity) & (slots >= 0)
            columns.append(jnp.where(hit, 1.0, 0.0))
        rows.append(jnp.concatenate(columns, axis=1))
    return jnp.concatenate(rows, axis=0)


def pack_kernel(images, sections, inputs, *refs):
    spots_ref, slots_ref = refs[:2]
    dense = refs[2 : 2 + inputs]
    if inputs > 1:
        joined, blocks = refs[-1], refs[-1 - sections : -1]
        seq_len = dense[0].shape[0]
        for i in range(images):
            joined[i * seq_len : (i + 1) * seq_len, :] = dense[i][...]
    else:
        joined, blocks = dense[0], refs[-sections:]
    count = blocks[0].shape[0]
    table = slot_table(spots_ref, slots_ref, images, sections, count).astype(jnp.bfloat16)
    total = jnp.dot(table, joined[...], preferred_element_type=jnp.float32).astype(jnp.bfloat16)
    for d in range(sections):
        blocks[d][...] = total[d * count : (d + 1) * count, :]


def pack(spots, slots, dense, capacity, after=()):
    sections, seq_len = slots.shape[1:]
    width = dense[0].shape[1]
    inputs = len(dense)
    images = sum(block.shape[0] for block in dense) // seq_len
    count = images * capacity
    whole = pl.BlockSpec(memory_space=pltpu.VMEM)
    shapes = [jax.ShapeDtypeStruct((count, width), jnp.bfloat16)] * sections
    if inputs > 1:
        shapes.append(jax.ShapeDtypeStruct((images * seq_len, width), jnp.bfloat16))
    results = pl.pallas_call(
        partial(pack_kernel, images, sections, inputs),
        name="pack",
        in_specs=[SCALARS] + [whole] * (1 + inputs) + [UNREAD] * len(after),
        out_specs=[whole] * len(shapes),
        out_shape=shapes,
        compiler_params=params(),
        cost_estimate=SMALL,
    )(spots, slots, *dense, *after)
    return results[:sections], results[sections:]


EXTRA = 16


def unpack_kernel(images, sections, extra, scored, *refs):
    spots_ref, slots_ref = refs[:2]
    blocks = refs[2 : 2 + sections]
    addend = refs[2 + sections : 2 + sections + extra]
    partners = refs[2 + sections + extra : 2 + sections + extra + scored]
    joined = refs[-1]
    dense = refs[-1 - (images if extra or scored else 1) : -1]
    count = blocks[0].shape[0]
    seq_len = slots_ref.shape[2]
    for d in range(sections):
        joined[d * count : (d + 1) * count, :] = blocks[d][...]
    table = slot_table(spots_ref, slots_ref, images, sections, count)
    total = jnp.dot(
        table.T.astype(jnp.bfloat16), joined[...], preferred_element_type=jnp.float32
    )
    if scored:
        lines = []
        for d in range(sections):
            product = blocks[d][...].astype(jnp.float32) * partners[d][...].astype(jnp.float32)
            column = jnp.sum(product, axis=1, keepdims=True)
            lines.append(
                jnp.sum(table[d * count : (d + 1) * count, :] * column, axis=0, keepdims=True)
            )
        lines = jnp.concatenate(
            lines + [jnp.zeros((EXTRA - sections, lines[0].shape[1]), jnp.float32)], axis=0
        )
    if not (extra or scored):
        dense[0][...] = total.astype(jnp.bfloat16)
        return
    for i in range(images):
        part = total[i * seq_len : (i + 1) * seq_len, :]
        if extra:
            part = part + addend[0][i * seq_len : (i + 1) * seq_len, :].astype(jnp.float32)
        dense[i][:seq_len, :] = part.astype(jnp.bfloat16)
        if scored:
            dense[i][seq_len:, :] = jnp.zeros((EXTRA, total.shape[1]), jnp.bfloat16)
            dense[i][seq_len:, :seq_len] = lines[:, i * seq_len : (i + 1) * seq_len].astype(
                jnp.bfloat16
            )


def unpack(spots, slots, blocks, images, addend=(), partners=(), after=()):
    sections, seq_len = slots.shape[1:]
    count, width = blocks[0].shape
    whole = pl.BlockSpec(memory_space=pltpu.VMEM)
    inputs = sections + len(addend) + len(partners)
    height = seq_len + (EXTRA if partners else 0)
    parts = images if addend or partners else 1
    if parts == 1:
        height = images * seq_len
    return pl.pallas_call(
        partial(unpack_kernel, images, sections, len(addend), len(partners)),
        name="unpack",
        in_specs=[SCALARS] + [whole] * (1 + inputs) + [UNREAD] * len(after),
        out_specs=[whole] * parts,
        out_shape=[jax.ShapeDtypeStruct((height, width), jnp.bfloat16)] * parts,
        scratch_shapes=[pltpu.VMEM((sections * count, width), jnp.bfloat16)],
        compiler_params=params(),
        cost_estimate=SMALL,
    )(spots, slots, *blocks, *addend, *partners, *after)


def merge_kernel(sections, *refs):
    met = refs[sections]
    merged = refs[-sections:]
    count = merged[0].shape[0]
    for d in range(sections):
        total = refs[d][...].astype(jnp.float32)
        total = total + met[d * count : (d + 1) * count, :].astype(jnp.float32)
        merged[d][...] = total.astype(jnp.bfloat16)


def merge(blocks, met, after=()):
    sections = len(blocks)
    whole = pl.BlockSpec(memory_space=pltpu.VMEM)
    return pl.pallas_call(
        partial(merge_kernel, sections),
        name="merge",
        in_specs=[whole] * (sections + 1) + [UNREAD] * len(after),
        out_specs=[whole] * sections,
        out_shape=[jax.ShapeDtypeStruct(blocks[0].shape, jnp.bfloat16)] * sections,
        compiler_params=params(),
        cost_estimate=SMALL,
    )(*blocks, met, *after)


def expert_kernel(sections, images, split, unread, *refs):
    spots_ref, other_ref, router_ref = refs[:3]
    mixed_in = refs[3 : 3 + sections]
    pulls = 1 if split == 1 else sections
    grads_in = refs[3 + sections : 3 + sections + pulls]
    up_ref, down_ref = refs[3 + sections + pulls : 5 + sections + pulls]
    outs = refs[5 + sections + pulls + unread :]
    out_parts, grad_parts = outs[:split], outs[split : split + sections]
    mixed, grads, out_sum, grad_sum, gate_ref = outs[split + sections :]
    step, last = pl.program_id(0), pl.num_programs(0) - 1
    count = mixed_in[0].shape[0]
    total = count * sections
    capacity = count // images
    at_row = lax.broadcasted_iota(jnp.int32, (count, capacity), 0)
    at_slot = lax.broadcasted_iota(jnp.int32, (count, capacity), 1)

    @pl.when(step == 0)
    def _():
        others = []
        for d in range(sections):
            mixed[d * count : (d + 1) * count, :] = mixed_in[d][...]
            if split > 1:
                grads[d * count : (d + 1) * count, :] = grads_in[d][...]
            column = jnp.zeros((count, 1), jnp.int32)
            for i in range(images):
                ids = other_ref[spots_ref[images + 1 + d], pl.ds(spots_ref[i], 1), :]
                own = at_row == at_slot + i * capacity
                column = column + jnp.sum(jnp.where(own, ids, 0), axis=1, keepdims=True)
            others.append(column)
        if split == 1:
            grads[...] = grads_in[0][...]
        logits = jnp.dot(mixed[...], router_ref[...], preferred_element_type=jnp.float32)
        lanes = lax.broadcasted_iota(jnp.int32, logits.shape, 1)
        mine = jnp.sum(jnp.where(lanes == spots_ref[images], logits, 0.0), axis=1, keepdims=True)
        is_other = lanes == jnp.concatenate(others, axis=0)
        other = jnp.sum(jnp.where(is_other, logits, 0.0), axis=1, keepdims=True)
        gate_ref[...] = 1.0 / (1.0 + jnp.exp(other - mine))
        out_sum[...] = jnp.zeros_like(out_sum)
        grad_sum[...] = jnp.zeros_like(grad_sum)

    gate = gate_ref[...]
    preact = jnp.dot(mixed[...], up_ref[...], preferred_element_type=jnp.float32)
    pulled = gate * lax.dot_general(
        grads[...], down_ref[...], (((1,), (1,)), ((), ())), preferred_element_type=jnp.float32
    )
    hidden_wide, slope = gelu_parts(preact)
    hidden = hidden_wide.astype(jnp.bfloat16)
    hidden_grad = (pulled * slope).astype(jnp.bfloat16)
    out_sum[...] += jnp.dot(hidden, down_ref[...], preferred_element_type=jnp.float32)
    grad_sum[...] += lax.dot_general(
        hidden_grad, up_ref[...], (((1,), (1,)), ((), ())), preferred_element_type=jnp.float32
    )

    @pl.when(step == last)
    def _():
        size = total // split
        for part in range(split):
            rows = slice(part * size, (part + 1) * size)
            out_parts[part][...] = (out_sum[rows, :] * gate[rows, :]).astype(jnp.bfloat16)
        for d in range(sections):
            grad_parts[d][...] = grad_sum[d * count : (d + 1) * count, :].astype(jnp.bfloat16)


def expert_unit(spots, others, router, mixed_in, grads_in, up_local, down_local, split, after=()):
    sections = len(mixed_in)
    images = spots.shape[0] - 1 - sections
    count, width = mixed_in[0].shape
    total = count * sections
    hidden_units = up_local.shape[1]
    tile = 512
    assert hidden_units // tile >= 2

    def whole(shape):
        return pl.BlockSpec(shape, lambda f: (0,) * len(shape))

    block = whole((count, width))
    results = pl.pallas_call(
        partial(expert_kernel, sections, images, split, len(after)),
        name="expert",
        grid=(hidden_units // tile,),
        in_specs=[SCALARS, whole(others.shape), whole(router.shape)]
        + [block] * sections
        + [whole(block_in.shape) for block_in in grads_in]
        + [
            pl.BlockSpec((width, tile), lambda f: (0, f)),
            pl.BlockSpec((tile, width), lambda f: (f, 0)),
        ]
        + [UNREAD] * len(after),
        out_specs=[whole((total // split, width))] * split + [block] * sections,
        out_shape=[jax.ShapeDtypeStruct((total // split, width), jnp.bfloat16)] * split
        + [jax.ShapeDtypeStruct((count, width), jnp.bfloat16)] * sections,
        scratch_shapes=[
            pltpu.VMEM((total, width), jnp.bfloat16),
            pltpu.VMEM((total, width), jnp.bfloat16),
            pltpu.VMEM((total, width), jnp.float32),
            pltpu.VMEM((total, width), jnp.float32),
            pltpu.VMEM((total, 1), jnp.float32),
        ],
        compiler_params=params(),
        cost_estimate=SMALL,
    )(spots, others, router, *mixed_in, *grads_in, up_local, down_local, *after)
    return results[:split], results[split:]


def shards(
    tokens,
    route_ids,
    cotangent,
    first_gain,
    in_projection,
    out_projection,
    second_gain,
    router_weight,
    up_weight,
    down_weight,
):
    picture = tokens[0, 0].astype(jnp.float32)
    chosen = route_ids[0, 0]
    upstream = cotangent[0, 0]
    up_local = up_weight[0, 0]
    down_local = down_weight[0, 0]
    seq_len, width = picture.shape
    experts = router_weight.shape[1]
    sections = lax.axis_size("segment")
    members = lax.axis_size("expert")
    per_section = members // PARTS_SIZE
    capacity = 3 * seq_len // experts
    line = members // 2
    here = lax.axis_index("expert")
    section = lax.axis_index("segment")
    place, side = here // 2, here % 2
    group = here // PARTS_SIZE
    my_expert = section * per_section + group
    relative = section ^ jnp.arange(sections)
    experts_here = relative * per_section + group

    def along(value, steps):
        pairs = [(j, (j + 2 * steps) % members) for j in range(members)]
        return lax.ppermute(value, "expert", pairs)

    def across(value):
        return lax.ppermute(value, "expert", [(j, j ^ 1) for j in range(members)])

    def deal(blocks):
        moved = [blocks[0]]
        for d in range(1, sections):
            pairs = [(s, s ^ d) for s in range(sections)]
            moved.append(lax.ppermute(blocks[d], "segment", pairs))
        return moved

    def deal_small(value):
        return lax.all_to_all(
            jnp.take(value, relative, axis=0), "segment", split_axis=0, concat_axis=0, tiled=True
        )

    half = line // 2
    chunks = [list(range(line - 1, half - 1, -1)), list(range(half - 1, -1, -1))]

    expert_list = jnp.arange(experts)
    hits = jnp.any(chosen.T[None] == expert_list[:, None, None], axis=1)
    tokens_before = jnp.arange(seq_len)[:, None] < jnp.arange(seq_len)[None, :]
    own_slots = jnp.dot(
        hits.astype(jnp.bfloat16),
        tokens_before.astype(jnp.bfloat16),
        preferred_element_type=jnp.float32,
    ).astype(jnp.int32)
    own_slots = jnp.where(hits, own_slots, -1)
    others = jnp.sum(chosen, axis=1)[None, :] - expert_list[:, None]
    at_slot = own_slots[:, None, :] == jnp.arange(capacity)[None, :, None]
    own_others = jnp.sum(jnp.where(at_slot, others[:, None, :], 0), axis=2)
    wide = jnp.concatenate([own_slots, own_others], axis=1)
    wide = jnp.take(wide.reshape(sections, per_section, -1), relative, axis=0).transpose(1, 0, 2)
    wide = jnp.broadcast_to(
        wide[:, None], (per_section, PARTS_SIZE) + wide.shape[1:]
    ).reshape(members, -1)
    lane = lax.all_to_all(wide, "expert", split_axis=0, concat_axis=0, tiled=True).reshape(
        members, sections, seq_len + capacity
    )
    slots = lane[:, :, :seq_len]
    slot_others = deal_small(lane[:, :, seq_len:].transpose(1, 0, 2))

    def spots_of(index, far):
        places = (place - jnp.array(chunks[index])) % line
        side_of = (1 - side) if far else side
        return jnp.concatenate(
            [2 * places + side_of, my_expert.reshape(1), relative]
        ).astype(jnp.int32)

    spots = {(index, far): spots_of(index, far) for index in (0, 1) for far in (0, 1)}

    cot_dense = {0: upstream, 1: along(upstream, 1)}
    slots, late_upstream = lax.optimization_barrier((slots, upstream))
    for step in range(2, line):
        cot_dense[step] = along(late_upstream, step)

    def cot_pack(index):
        dense = [cot_dense[step] for step in chunks[index]]
        return pack(spots[index, 0], slots, dense, capacity)[0]

    joined, project_back = jax.vjp(
        partial(project_in, first_gain=first_gain, in_projection=in_projection), picture
    )
    cot_packed, cot_rows = {}, {}
    cot_packed[1] = cot_pack(1)
    joined, cot_packed[1] = lax.optimization_barrier((joined, cot_packed[1]))
    cot_rows[1, 0] = deal(cot_packed[1])
    residual, attend_back = jax.vjp(partial(attend, out_projection=out_projection), picture, joined)
    residual, slot_others = lax.optimization_barrier((residual, slot_others))
    normed, norm_back = jax.vjp(partial(layer_norm, gain_vector=second_gain), residual)
    mixed = normed.astype(jnp.bfloat16)
    own_logits = jnp.dot(mixed, router_weight, preferred_element_type=jnp.float32)

    mixed_dense = {0: mixed}
    for step in range(1, line):
        mixed_dense[step] = along(mixed, step)

    cot_rows[1, 1] = [across(jnp.concatenate(cot_rows[1, 0], axis=0))]
    cot_packed[0] = cot_pack(0)
    cot_rows[0, 0] = deal(cot_packed[0])

    mixed_rows, far_dense = {}, {}

    def mixed_pack(index, after):
        dense = [mixed_dense[step] for step in chunks[index]]
        blocks, joined_dense = pack(spots[index, 0], slots, dense, capacity, after)
        far_dense[index] = across(joined_dense[0])
        mixed_rows[index, 0] = deal(blocks)
        return (blocks[0],)

    def far_pack(index, after):
        blocks, _ = pack(spots[index, 1], slots, [far_dense[index]], capacity, after)
        mixed_rows[index, 1] = deal(blocks)
        return (blocks[0],)

    outs, grads = {}, {}

    def unit(index, far, after):
        outs[index, far], grads[index, far] = expert_unit(
            spots[index, far],
            slot_others,
            router_weight,
            mixed_rows[index, far],
            cot_rows[index, far],
            up_local,
            down_local,
            1 if far else sections,
            after,
        )
        done = (grads[index, far][0],)
        if far:
            grads[index, far] = deal(grads[index, far])
        return done

    done = mixed_pack(1, (cot_packed[0][0],))
    done = mixed_pack(0, done + tuple(cot_rows[1, 1]))
    cot_rows[0, 1] = [across(jnp.concatenate(cot_rows[0, 0], axis=0))]
    done = far_pack(1, done)
    done = unit(1, 0, done)
    done = unit(0, 0, done)
    done = far_pack(0, done)
    done = unit(1, 1, done)
    met = {1: across(outs[1, 1][0])}
    done = unit(0, 1, done)
    met[0] = across(outs[0, 1][0])
    for index in (1, 0):
        held, _ = lax.optimization_barrier((grads[index, 0], done))
        grads[index, 0] = deal(held)

    grad_far, out_back, out_dense, grad_dense = {}, {}, {}, {}
    for index in (1, 0):
        count = len(chunks[index])
        grad_far[index] = unpack(spots[index, 1], slots, grads[index, 1], count, after=done)[0]
        done = (grad_far[index],)
        grad_far[index] = across(grad_far[index])
        merged = merge(outs[index, 0], met[index], done)
        done = (merged[0],)
        out_back[index] = deal(merged)
    for index in (1, 0):
        chunk = chunks[index]
        out_block = unpack(
            spots[index, 0], slots, out_back[index], len(chunk), (), cot_packed[index], done
        )
        done = (out_block[0],)
        for spot, step in enumerate(chunk):
            out_dense[step] = along(out_block[spot], -step) if step else out_block[spot]
    for index in (1, 0):
        chunk = chunks[index]
        grad_block = unpack(
            spots[index, 0], slots, grads[index, 0], len(chunk), (grad_far[index],), (), done
        )
        done = (grad_block[0],)
        for spot, step in enumerate(chunk):
            grad_dense[step] = along(grad_block[spot], -step) if step else grad_block[spot]

    expert_total = sum(out_dense[step][:seq_len].astype(jnp.float32) for step in range(line))
    input_total = sum(grad_dense[step].astype(jnp.float32) for step in range(line))
    layer_out = (residual + expert_total).astype(jnp.bfloat16)

    named = chosen[:, :, None] == expert_list
    score_lines = jnp.zeros((per_section, sections, seq_len), jnp.float32)
    for step in range(line):
        sender = 2 * ((place + step) % line) // PARTS_SIZE
        lines = out_dense[step][seq_len : seq_len + sections, :seq_len].astype(jnp.float32)
        score_lines += jnp.where((jnp.arange(per_section) == sender)[:, None, None], lines, 0.0)
    token_scores = (
        jnp.take(score_lines, relative, axis=1).transpose(1, 0, 2).reshape(experts, seq_len).T
    )
    picked_logit = jnp.sum(jnp.where(named, own_logits[:, None, :], 0.0), axis=2)
    gate_values = 1.0 / (1.0 + jnp.exp(picked_logit[:, ::-1] - picked_logit))
    gate_spread = jnp.sum(jnp.where(named, gate_values[:, :, None], 0.0), axis=1)
    spread_grad = token_scores - gate_spread * jnp.sum(token_scores, axis=1, keepdims=True)
    mixed_grad = input_total + jnp.einsum(
        "se,de->sd", spread_grad, router_weight.astype(jnp.float32), precision=lax.Precision.HIGHEST
    )
    residual_grad = upstream.astype(jnp.float32) + norm_back(mixed_grad)[0]
    picture_grad, joined_grad = attend_back(residual_grad)
    input_grad = (picture_grad + project_back(joined_grad)[0]).astype(jnp.bfloat16)
    return (layer_out[None, None], input_grad[None, None])


def solution(mesh):
    placed = (
        P("segment", "expert", None, None),
        P("segment", "expert", None, None),
        P("segment", "expert", None, None),
        P(),
        P(),
        P(),
        P(),
        P(),
        P("segment", "expert", None, None),
        P("segment", "expert", None, None),
    )
    return jax.shard_map(
        shards,
        mesh=mesh,
        in_specs=placed,
        out_specs=(P("segment", "expert", None, None), P("segment", "expert", None, None)),
        check_vma=False,
    )
```

```python
from functools import partial

import jax
import jax.numpy as jnp
from jax import lax
from jax.experimental import pallas as pl
from jax.experimental.pallas import tpu as pltpu
from jax.sharding import PartitionSpec as P

HD = 104
PARTS_SIZE = 4
TOP = 2


EPSILON = 1e-06
ROOT_HALF = 0.7071067811865476
INV_ROOT_TWO_PI = 0.3989422804014327


def layer_norm(row_block, gain_vector):
    center = row_block - jnp.mean(row_block, axis=-1, keepdims=True)
    spread = jnp.mean(center * center, axis=-1, keepdims=True)
    return center * lax.rsqrt(spread + EPSILON) * gain_vector


def gelu_parts(preact):
    half_cdf = 0.5 * (1.0 + lax.erf(preact * ROOT_HALF))
    slope = half_cdf + preact * INV_ROOT_TWO_PI * jnp.exp(-0.5 * preact * preact)
    return preact * half_cdf, slope


def project_in(picture, first_gain, in_projection):
    normed = layer_norm(picture, first_gain).astype(jnp.bfloat16)
    return jnp.dot(normed, in_projection, preferred_element_type=jnp.float32).astype(jnp.bfloat16)


def attend(picture, joined, out_projection):
    seq_len = picture.shape[0]
    head_width = out_projection.shape[0]
    head_count = head_width // HD
    queries = joined[:, :head_width].reshape(seq_len, head_count, HD)
    key_rows = joined[:, head_width : 2 * head_width].reshape(seq_len, head_count, HD)
    value_rows = joined[:, 2 * head_width :].reshape(seq_len, head_count, HD)
    scores = jnp.einsum(
        "qhd,khd->hqk", queries, key_rows, preferred_element_type=jnp.float32
    ) * HD ** (-0.5)
    weights = jnp.exp(scores)
    attention = (weights / jnp.sum(weights, axis=-1, keepdims=True)).astype(jnp.bfloat16)
    context = jnp.einsum(
        "hqk,khd->qhd", attention, value_rows, preferred_element_type=jnp.float32
    ).astype(jnp.bfloat16)
    return picture + jnp.dot(
        context.reshape(seq_len, head_width), out_projection, preferred_element_type=jnp.float32
    )


def params():
    return pltpu.CompilerParams(vmem_limit_bytes=60 * 1024 * 1024)


SMALL = pl.CostEstimate(flops=1000, bytes_accessed=1000, transcendentals=0)
SCALARS = pl.BlockSpec(memory_space=pltpu.SMEM)
UNREAD = pl.BlockSpec(memory_space=pl.ANY)


def slot_table(spots_ref, slots_ref, images, sections, count):
    capacity = count // images
    rows = []
    for d in range(sections):
        columns = []
        for i in range(images):
            slots = slots_ref[spots_ref[i]][d : d + 1, :]
            lanes = lax.broadcasted_iota(jnp.int32, (count, slots.shape[1]), 0)
            hit = (lanes == slots + i * capacity) & (slots >= 0)
            columns.append(jnp.where(hit, 1.0, 0.0))
        rows.append(jnp.concatenate(columns, axis=1))
    return jnp.concatenate(rows, axis=0)


def pack_kernel(images, sections, inputs, *refs):
    spots_ref, slots_ref = refs[:2]
    dense = refs[2 : 2 + inputs]
    if inputs > 1:
        joined, blocks = refs[-1], refs[-1 - sections : -1]
        seq_len = dense[0].shape[0]
        for i in range(images):
            joined[i * seq_len : (i + 1) * seq_len, :] = dense[i][...]
    else:
        joined, blocks = dense[0], refs[-sections:]
    count = blocks[0].shape[0]
    table = slot_table(spots_ref, slots_ref, images, sections, count).astype(jnp.bfloat16)
    total = jnp.dot(table, joined[...], preferred_element_type=jnp.float32).astype(jnp.bfloat16)
    for d in range(sections):
        blocks[d][...] = total[d * count : (d + 1) * count, :]


def pack(spots, slots, dense, capacity, after=()):
    sections, seq_len = slots.shape[1:]
    width = dense[0].shape[1]
    inputs = len(dense)
    images = sum(block.shape[0] for block in dense) // seq_len
    count = images * capacity
    whole = pl.BlockSpec(memory_space=pltpu.VMEM)
    shapes = [jax.ShapeDtypeStruct((count, width), jnp.bfloat16)] * sections
    if inputs > 1:
        shapes.append(jax.ShapeDtypeStruct((images * seq_len, width), jnp.bfloat16))
    results = pl.pallas_call(
        partial(pack_kernel, images, sections, inputs),
        name="pack",
        in_specs=[SCALARS] + [whole] * (1 + inputs) + [UNREAD] * len(after),
        out_specs=[whole] * len(shapes),
        out_shape=shapes,
        compiler_params=params(),
        cost_estimate=SMALL,
    )(spots, slots, *dense, *after)
    return results[:sections], results[sections:]


EXTRA = 16


def unpack_kernel(images, sections, extra, scored, *refs):
    spots_ref, slots_ref = refs[:2]
    blocks = refs[2 : 2 + sections]
    addend = refs[2 + sections : 2 + sections + extra]
    partners = refs[2 + sections + extra : 2 + sections + extra + scored]
    joined = refs[-1]
    dense = refs[-1 - (images if extra or scored else 1) : -1]
    count = blocks[0].shape[0]
    seq_len = slots_ref.shape[2]
    for d in range(sections):
        joined[d * count : (d + 1) * count, :] = blocks[d][...]
    table = slot_table(spots_ref, slots_ref, images, sections, count)
    total = jnp.dot(
        table.T.astype(jnp.bfloat16), joined[...], preferred_element_type=jnp.float32
    )
    if scored:
        lines = []
        for d in range(sections):
            product = blocks[d][...].astype(jnp.float32) * partners[d][...].astype(jnp.float32)
            column = jnp.sum(product, axis=1, keepdims=True)
            lines.append(
                jnp.sum(table[d * count : (d + 1) * count, :] * column, axis=0, keepdims=True)
            )
        lines = jnp.concatenate(
            lines + [jnp.zeros((EXTRA - sections, lines[0].shape[1]), jnp.float32)], axis=0
        )
    if not (extra or scored):
        dense[0][...] = total.astype(jnp.bfloat16)
        return
    for i in range(images):
        part = total[i * seq_len : (i + 1) * seq_len, :]
        if extra:
            part = part + addend[0][i * seq_len : (i + 1) * seq_len, :].astype(jnp.float32)
        dense[i][:seq_len, :] = part.astype(jnp.bfloat16)
        if scored:
            dense[i][seq_len:, :] = jnp.zeros((EXTRA, total.shape[1]), jnp.bfloat16)
            dense[i][seq_len:, :seq_len] = lines[:, i * seq_len : (i + 1) * seq_len].astype(
                jnp.bfloat16
            )


def unpack(spots, slots, blocks, images, addend=(), partners=(), after=()):
    sections, seq_len = slots.shape[1:]
    count, width = blocks[0].shape
    whole = pl.BlockSpec(memory_space=pltpu.VMEM)
    inputs = sections + len(addend) + len(partners)
    height = seq_len + (EXTRA if partners else 0)
    parts = images if addend or partners else 1
    if parts == 1:
        height = images * seq_len
    return pl.pallas_call(
        partial(unpack_kernel, images, sections, len(addend), len(partners)),
        name="unpack",
        in_specs=[SCALARS] + [whole] * (1 + inputs) + [UNREAD] * len(after),
        out_specs=[whole] * parts,
        out_shape=[jax.ShapeDtypeStruct((height, width), jnp.bfloat16)] * parts,
        scratch_shapes=[pltpu.VMEM((sections * count, width), jnp.bfloat16)],
        compiler_params=params(),
        cost_estimate=SMALL,
    )(spots, slots, *blocks, *addend, *partners, *after)


def merge_kernel(sections, *refs):
    met = refs[sections]
    merged = refs[-sections:]
    count = merged[0].shape[0]
    for d in range(sections):
        total = refs[d][...].astype(jnp.float32)
        total = total + met[d * count : (d + 1) * count, :].astype(jnp.float32)
        merged[d][...] = total.astype(jnp.bfloat16)


def merge(blocks, met, after=()):
    sections = len(blocks)
    whole = pl.BlockSpec(memory_space=pltpu.VMEM)
    return pl.pallas_call(
        partial(merge_kernel, sections),
        name="merge",
        in_specs=[whole] * (sections + 1) + [UNREAD] * len(after),
        out_specs=[whole] * sections,
        out_shape=[jax.ShapeDtypeStruct(blocks[0].shape, jnp.bfloat16)] * sections,
        compiler_params=params(),
        cost_estimate=SMALL,
    )(*blocks, met, *after)


def expert_kernel(sections, images, split, unread, *refs):
    spots_ref, other_ref, router_ref = refs[:3]
    mixed_in = refs[3 : 3 + sections]
    pulls = 1 if split == 1 else sections
    grads_in = refs[3 + sections : 3 + sections + pulls]
    up_ref, down_ref = refs[3 + sections + pulls : 5 + sections + pulls]
    outs = refs[5 + sections + pulls + unread :]
    out_parts, grad_parts = outs[:split], outs[split : split + sections]
    mixed, grads, out_sum, grad_sum, gate_ref = outs[split + sections :]
    step, last = pl.program_id(0), pl.num_programs(0) - 1
    count = mixed_in[0].shape[0]
    total = count * sections
    capacity = count // images
    at_row = lax.broadcasted_iota(jnp.int32, (count, capacity), 0)
    at_slot = lax.broadcasted_iota(jnp.int32, (count, capacity), 1)

    @pl.when(step == 0)
    def _():
        others = []
        for d in range(sections):
            mixed[d * count : (d + 1) * count, :] = mixed_in[d][...]
            if split > 1:
                grads[d * count : (d + 1) * count, :] = grads_in[d][...]
            column = jnp.zeros((count, 1), jnp.int32)
            for i in range(images):
                ids = other_ref[spots_ref[images + 1 + d], pl.ds(spots_ref[i], 1), :]
                own = at_row == at_slot + i * capacity
                column = column + jnp.sum(jnp.where(own, ids, 0), axis=1, keepdims=True)
            others.append(column)
        if split == 1:
            grads[...] = grads_in[0][...]
        logits = jnp.dot(mixed[...], router_ref[...], preferred_element_type=jnp.float32)
        lanes = lax.broadcasted_iota(jnp.int32, logits.shape, 1)
        mine = jnp.sum(jnp.where(lanes == spots_ref[images], logits, 0.0), axis=1, keepdims=True)
        is_other = lanes == jnp.concatenate(others, axis=0)
        other = jnp.sum(jnp.where(is_other, logits, 0.0), axis=1, keepdims=True)
        gate_ref[...] = 1.0 / (1.0 + jnp.exp(other - mine))
        out_sum[...] = jnp.zeros_like(out_sum)
        grad_sum[...] = jnp.zeros_like(grad_sum)

    gate = gate_ref[...]
    preact = jnp.dot(mixed[...], up_ref[...], preferred_element_type=jnp.float32)
    pulled = gate * lax.dot_general(
        grads[...], down_ref[...], (((1,), (1,)), ((), ())), preferred_element_type=jnp.float32
    )
    hidden_wide, slope = gelu_parts(preact)
    hidden = hidden_wide.astype(jnp.bfloat16)
    hidden_grad = (pulled * slope).astype(jnp.bfloat16)
    out_sum[...] += jnp.dot(hidden, down_ref[...], preferred_element_type=jnp.float32)
    grad_sum[...] += lax.dot_general(
        hidden_grad, up_ref[...], (((1,), (1,)), ((), ())), preferred_element_type=jnp.float32
    )

    @pl.when(step == last)
    def _():
        size = total // split
        for part in range(split):
            rows = slice(part * size, (part + 1) * size)
            out_parts[part][...] = (out_sum[rows, :] * gate[rows, :]).astype(jnp.bfloat16)
        for d in range(sections):
            grad_parts[d][...] = grad_sum[d * count : (d + 1) * count, :].astype(jnp.bfloat16)


def expert_unit(spots, others, router, mixed_in, grads_in, up_local, down_local, split, after=()):
    sections = len(mixed_in)
    images = spots.shape[0] - 1 - sections
    count, width = mixed_in[0].shape
    total = count * sections
    hidden_units = up_local.shape[1]
    tile = 512
    assert hidden_units // tile >= 2

    def whole(shape):
        return pl.BlockSpec(shape, lambda f: (0,) * len(shape))

    block = whole((count, width))
    results = pl.pallas_call(
        partial(expert_kernel, sections, images, split, len(after)),
        name="expert",
        grid=(hidden_units // tile,),
        in_specs=[SCALARS, whole(others.shape), whole(router.shape)]
        + [block] * sections
        + [whole(block_in.shape) for block_in in grads_in]
        + [
            pl.BlockSpec((width, tile), lambda f: (0, f)),
            pl.BlockSpec((tile, width), lambda f: (f, 0)),
        ]
        + [UNREAD] * len(after),
        out_specs=[whole((total // split, width))] * split + [block] * sections,
        out_shape=[jax.ShapeDtypeStruct((total // split, width), jnp.bfloat16)] * split
        + [jax.ShapeDtypeStruct((count, width), jnp.bfloat16)] * sections,
        scratch_shapes=[
            pltpu.VMEM((total, width), jnp.bfloat16),
            pltpu.VMEM((total, width), jnp.bfloat16),
            pltpu.VMEM((total, width), jnp.float32),
            pltpu.VMEM((total, width), jnp.float32),
            pltpu.VMEM((total, 1), jnp.float32),
        ],
        compiler_params=params(),
        cost_estimate=SMALL,
    )(spots, others, router, *mixed_in, *grads_in, up_local, down_local, *after)
    return results[:split], results[split:]


def shards(
    tokens,
    route_ids,
    cotangent,
    first_gain,
    in_projection,
    out_projection,
    second_gain,
    router_weight,
    up_weight,
    down_weight,
):
    picture = tokens[0, 0].astype(jnp.float32)
    chosen = route_ids[0, 0]
    upstream = cotangent[0, 0]
    up_local = up_weight[0, 0]
    down_local = down_weight[0, 0]
    seq_len, width = picture.shape
    experts = router_weight.shape[1]
    sections = lax.axis_size("segment")
    members = lax.axis_size("expert")
    per_section = members // PARTS_SIZE
    capacity = 3 * seq_len // experts
    line = members // 2
    here = lax.axis_index("expert")
    section = lax.axis_index("segment")
    place, side = here // 2, here % 2
    group = here // PARTS_SIZE
    my_expert = section * per_section + group
    relative = section ^ jnp.arange(sections)
    experts_here = relative * per_section + group

    def along(value, steps):
        pairs = [(j, (j + 2 * steps) % members) for j in range(members)]
        return lax.ppermute(value, "expert", pairs)

    def across(value):
        return lax.ppermute(value, "expert", [(j, j ^ 1) for j in range(members)])

    def deal(blocks):
        moved = [blocks[0]]
        for d in range(1, sections):
            pairs = [(s, s ^ d) for s in range(sections)]
            moved.append(lax.ppermute(blocks[d], "segment", pairs))
        return moved

    def deal_small(value):
        return lax.all_to_all(
            jnp.take(value, relative, axis=0), "segment", split_axis=0, concat_axis=0, tiled=True
        )

    half = line // 2
    chunks = [list(range(line - 1, half - 1, -1)), list(range(half - 1, -1, -1))]

    expert_list = jnp.arange(experts)
    hits = jnp.any(chosen.T[None] == expert_list[:, None, None], axis=1)
    tokens_before = jnp.arange(seq_len)[:, None] < jnp.arange(seq_len)[None, :]
    own_slots = jnp.dot(
        hits.astype(jnp.bfloat16),
        tokens_before.astype(jnp.bfloat16),
        preferred_element_type=jnp.float32,
    ).astype(jnp.int32)
    own_slots = jnp.where(hits, own_slots, -1)
    others = jnp.sum(chosen, axis=1)[None, :] - expert_list[:, None]
    at_slot = own_slots[:, None, :] == jnp.arange(capacity)[None, :, None]
    own_others = jnp.sum(jnp.where(at_slot, others[:, None, :], 0), axis=2)
    wide = jnp.concatenate([own_slots, own_others], axis=1)
    wide = jnp.take(wide.reshape(sections, per_section, -1), relative, axis=0).transpose(1, 0, 2)
    wide = jnp.broadcast_to(
        wide[:, None], (per_section, PARTS_SIZE) + wide.shape[1:]
    ).reshape(members, -1)
    lane = lax.all_to_all(wide, "expert", split_axis=0, concat_axis=0, tiled=True).reshape(
        members, sections, seq_len + capacity
    )
    slots = lane[:, :, :seq_len]
    slot_others = deal_small(lane[:, :, seq_len:].transpose(1, 0, 2))

    def spots_of(index, far):
        places = (place - jnp.array(chunks[index])) % line
        side_of = (1 - side) if far else side
        return jnp.concatenate(
            [2 * places + side_of, my_expert.reshape(1), relative]
        ).astype(jnp.int32)

    spots = {(index, far): spots_of(index, far) for index in (0, 1) for far in (0, 1)}

    cot_dense = {0: upstream, 1: along(upstream, 1)}
    slots, late_upstream = lax.optimization_barrier((slots, upstream))
    for step in range(2, line):
        cot_dense[step] = along(late_upstream, step)

    def cot_pack(index):
        dense = [cot_dense[step] for step in chunks[index]]
        return pack(spots[index, 0], slots, dense, capacity)[0]

    joined, project_back = jax.vjp(
        partial(project_in, first_gain=first_gain, in_projection=in_projection), picture
    )
    cot_packed, cot_rows = {}, {}
    cot_packed[1] = cot_pack(1)
    joined, cot_packed[1] = lax.optimization_barrier((joined, cot_packed[1]))
    cot_rows[1, 0] = deal(cot_packed[1])
    residual, attend_back = jax.vjp(partial(attend, out_projection=out_projection), picture, joined)
    residual, slot_others = lax.optimization_barrier((residual, slot_others))
    normed, norm_back = jax.vjp(partial(layer_norm, gain_vector=second_gain), residual)
    mixed = normed.astype(jnp.bfloat16)
    own_logits = jnp.dot(mixed, router_weight, preferred_element_type=jnp.float32)

    mixed_dense = {0: mixed}
    for step in range(1, line):
        mixed_dense[step] = along(mixed, step)

    cot_rows[1, 1] = [across(jnp.concatenate(cot_rows[1, 0], axis=0))]
    cot_packed[0] = cot_pack(0)
    cot_rows[0, 0] = deal(cot_packed[0])

    mixed_rows, far_dense = {}, {}

    def mixed_pack(index, after):
        dense = [mixed_dense[step] for step in chunks[index]]
        blocks, joined_dense = pack(spots[index, 0], slots, dense, capacity, after)
        far_dense[index] = across(joined_dense[0])
        mixed_rows[index, 0] = deal(blocks)
        return (blocks[0],)

    def far_pack(index, after):
        blocks, _ = pack(spots[index, 1], slots, [far_dense[index]], capacity, after)
        mixed_rows[index, 1] = deal(blocks)
        return (blocks[0],)

    outs, grads = {}, {}

    def unit(index, far, after):
        outs[index, far], grads[index, far] = expert_unit(
            spots[index, far],
            slot_others,
            router_weight,
            mixed_rows[index, far],
            cot_rows[index, far],
            up_local,
            down_local,
            1 if far else sections,
            after,
        )
        done = (grads[index, far][0],)
        if far:
            grads[index, far] = deal(grads[index, far])
        return done

    done = mixed_pack(1, (cot_packed[0][0],))
    done = mixed_pack(0, done + tuple(cot_rows[1, 1]))
    cot_rows[0, 1] = [across(jnp.concatenate(cot_rows[0, 0], axis=0))]
    done = far_pack(1, done)
    done = unit(1, 0, done)
    done = far_pack(0, done)
    done = unit(0, 0, done)
    done = unit(1, 1, done)
    met = {1: across(outs[1, 1][0])}
    done = unit(0, 1, done)
    met[0] = across(outs[0, 1][0])
    for index in (0, 1):
        held, _ = lax.optimization_barrier((grads[index, 0], done))
        grads[index, 0] = deal(held)

    grad_far, out_back, out_dense, grad_dense = {}, {}, {}, {}

    def unpack_far(index, after):
        count = len(chunks[index])
        block = unpack(spots[index, 1], slots, grads[index, 1], count, after=after)[0]
        grad_far[index] = across(block)
        return (block,)

    def merge_out(index, after):
        merged = merge(outs[index, 0], met[index], after)
        out_back[index] = deal(merged)
        return (merged[0],)

    def unpack_out(index, after):
        chunk = chunks[index]
        blocks = unpack(
            spots[index, 0], slots, out_back[index], len(chunk), (), cot_packed[index], after
        )
        for spot, step in enumerate(chunk):
            out_dense[step] = along(blocks[spot], -step) if step else blocks[spot]
        return (blocks[0],)

    def unpack_grad(index, after):
        chunk = chunks[index]
        blocks = unpack(
            spots[index, 0], slots, grads[index, 0], len(chunk), (grad_far[index],), (), after
        )
        for spot, step in enumerate(chunk):
            grad_dense[step] = along(blocks[spot], -step) if step else blocks[spot]
        return (blocks[0],)

    done = unpack_far(0, done)
    done = merge_out(1, done)
    done = unpack_far(1, done)
    done = merge_out(0, done)
    done = unpack_out(1, done + (grad_far[0],))
    done = unpack_grad(0, done)
    done = unpack_out(0, done)
    done = unpack_grad(1, done)

    expert_total = sum(out_dense[step][:seq_len].astype(jnp.float32) for step in range(line))
    input_total = sum(grad_dense[step].astype(jnp.float32) for step in range(line))
    layer_out = (residual + expert_total).astype(jnp.bfloat16)

    named = chosen[:, :, None] == expert_list
    score_lines = jnp.zeros((per_section, sections, seq_len), jnp.float32)
    for step in range(line):
        sender = 2 * ((place + step) % line) // PARTS_SIZE
        lines = out_dense[step][seq_len : seq_len + sections, :seq_len].astype(jnp.float32)
        score_lines += jnp.where((jnp.arange(per_section) == sender)[:, None, None], lines, 0.0)
    token_scores = (
        jnp.take(score_lines, relative, axis=1).transpose(1, 0, 2).reshape(experts, seq_len).T
    )
    picked_logit = jnp.sum(jnp.where(named, own_logits[:, None, :], 0.0), axis=2)
    gate_values = 1.0 / (1.0 + jnp.exp(picked_logit[:, ::-1] - picked_logit))
    gate_spread = jnp.sum(jnp.where(named, gate_values[:, :, None], 0.0), axis=1)
    spread_grad = token_scores - gate_spread * jnp.sum(token_scores, axis=1, keepdims=True)
    mixed_grad = input_total + jnp.einsum(
        "se,de->sd", spread_grad, router_weight.astype(jnp.float32), precision=lax.Precision.HIGHEST
    )
    residual_grad = upstream.astype(jnp.float32) + norm_back(mixed_grad)[0]
    picture_grad, joined_grad = attend_back(residual_grad)
    input_grad = (picture_grad + project_back(joined_grad)[0]).astype(jnp.bfloat16)
    return (layer_out[None, None], input_grad[None, None])


def solution(mesh):
    placed = (
        P("segment", "expert", None, None),
        P("segment", "expert", None, None),
        P("segment", "expert", None, None),
        P(),
        P(),
        P(),
        P(),
        P(),
        P("segment", "expert", None, None),
        P("segment", "expert", None, None),
    )
    return jax.shard_map(
        shards,
        mesh=mesh,
        in_specs=placed,
        out_specs=(P("segment", "expert", None, None), P("segment", "expert", None, None)),
        check_vma=False,
    )
```

```python
from functools import partial

import jax
import jax.numpy as jnp
from jax import lax
from jax.experimental import pallas as pl
from jax.experimental.pallas import tpu as pltpu
from jax.sharding import PartitionSpec as P

HD = 104
PARTS_SIZE = 4
TOP = 2


EPSILON = 1e-06
ROOT_HALF = 0.7071067811865476
INV_ROOT_TWO_PI = 0.3989422804014327


def layer_norm(row_block, gain_vector):
    center = row_block - jnp.mean(row_block, axis=-1, keepdims=True)
    spread = jnp.mean(center * center, axis=-1, keepdims=True)
    return center * lax.rsqrt(spread + EPSILON) * gain_vector


def gelu_parts(preact):
    half_cdf = 0.5 * (1.0 + lax.erf(preact * ROOT_HALF))
    slope = half_cdf + preact * INV_ROOT_TWO_PI * jnp.exp(-0.5 * preact * preact)
    return preact * half_cdf, slope


def project_in(picture, first_gain, in_projection):
    normed = layer_norm(picture, first_gain).astype(jnp.bfloat16)
    return jnp.dot(normed, in_projection, preferred_element_type=jnp.float32).astype(jnp.bfloat16)


def attend(picture, joined, out_projection):
    seq_len = picture.shape[0]
    head_width = out_projection.shape[0]
    head_count = head_width // HD
    queries = joined[:, :head_width].reshape(seq_len, head_count, HD)
    key_rows = joined[:, head_width : 2 * head_width].reshape(seq_len, head_count, HD)
    value_rows = joined[:, 2 * head_width :].reshape(seq_len, head_count, HD)
    scores = jnp.einsum(
        "qhd,khd->hqk", queries, key_rows, preferred_element_type=jnp.float32
    ) * HD ** (-0.5)
    weights = jnp.exp(scores)
    attention = (weights / jnp.sum(weights, axis=-1, keepdims=True)).astype(jnp.bfloat16)
    context = jnp.einsum(
        "hqk,khd->qhd", attention, value_rows, preferred_element_type=jnp.float32
    ).astype(jnp.bfloat16)
    return picture + jnp.dot(
        context.reshape(seq_len, head_width), out_projection, preferred_element_type=jnp.float32
    )


def params():
    return pltpu.CompilerParams(vmem_limit_bytes=60 * 1024 * 1024)


SMALL = pl.CostEstimate(flops=1000, bytes_accessed=1000, transcendentals=0)
SCALARS = pl.BlockSpec(memory_space=pltpu.SMEM)
UNREAD = pl.BlockSpec(memory_space=pl.ANY)


def slot_table(spots_ref, slots_ref, images, sections, count):
    capacity = count // images
    rows = []
    for d in range(sections):
        columns = []
        for i in range(images):
            slots = slots_ref[spots_ref[i]][d : d + 1, :]
            lanes = lax.broadcasted_iota(jnp.int32, (count, slots.shape[1]), 0)
            hit = (lanes == slots + i * capacity) & (slots >= 0)
            columns.append(jnp.where(hit, 1.0, 0.0))
        rows.append(jnp.concatenate(columns, axis=1))
    return jnp.concatenate(rows, axis=0)


def pack_kernel(images, sections, inputs, *refs):
    spots_ref, slots_ref = refs[:2]
    dense = refs[2 : 2 + inputs]
    if inputs > 1:
        joined, blocks = refs[-1], refs[-1 - sections : -1]
        seq_len = dense[0].shape[0]
        for i in range(images):
            joined[i * seq_len : (i + 1) * seq_len, :] = dense[i][...]
    else:
        joined, blocks = dense[0], refs[-sections:]
    count = blocks[0].shape[0]
    table = slot_table(spots_ref, slots_ref, images, sections, count).astype(jnp.bfloat16)
    total = jnp.dot(table, joined[...], preferred_element_type=jnp.float32).astype(jnp.bfloat16)
    for d in range(sections):
        blocks[d][...] = total[d * count : (d + 1) * count, :]


def pack(spots, slots, dense, capacity, after=()):
    sections, seq_len = slots.shape[1:]
    width = dense[0].shape[1]
    inputs = len(dense)
    images = sum(block.shape[0] for block in dense) // seq_len
    count = images * capacity
    whole = pl.BlockSpec(memory_space=pltpu.VMEM)
    shapes = [jax.ShapeDtypeStruct((count, width), jnp.bfloat16)] * sections
    if inputs > 1:
        shapes.append(jax.ShapeDtypeStruct((images * seq_len, width), jnp.bfloat16))
    results = pl.pallas_call(
        partial(pack_kernel, images, sections, inputs),
        name="pack",
        in_specs=[SCALARS] + [whole] * (1 + inputs) + [UNREAD] * len(after),
        out_specs=[whole] * len(shapes),
        out_shape=shapes,
        compiler_params=params(),
        cost_estimate=SMALL,
    )(spots, slots, *dense, *after)
    return results[:sections], results[sections:]


EXTRA = 16


def unpack_kernel(images, sections, extra, scored, *refs):
    spots_ref, slots_ref = refs[:2]
    blocks = refs[2 : 2 + sections]
    addend = refs[2 + sections : 2 + sections + extra]
    partners = refs[2 + sections + extra : 2 + sections + extra + scored]
    joined = refs[-1]
    dense = refs[-1 - (images if extra or scored else 1) : -1]
    count = blocks[0].shape[0]
    seq_len = slots_ref.shape[2]
    for d in range(sections):
        joined[d * count : (d + 1) * count, :] = blocks[d][...]
    table = slot_table(spots_ref, slots_ref, images, sections, count)
    total = jnp.dot(
        table.T.astype(jnp.bfloat16), joined[...], preferred_element_type=jnp.float32
    )
    if scored:
        lines = []
        for d in range(sections):
            product = blocks[d][...].astype(jnp.float32) * partners[d][...].astype(jnp.float32)
            column = jnp.sum(product, axis=1, keepdims=True)
            lines.append(
                jnp.sum(table[d * count : (d + 1) * count, :] * column, axis=0, keepdims=True)
            )
        lines = jnp.concatenate(
            lines + [jnp.zeros((EXTRA - sections, lines[0].shape[1]), jnp.float32)], axis=0
        )
    if not (extra or scored):
        dense[0][...] = total.astype(jnp.bfloat16)
        return
    for i in range(images):
        part = total[i * seq_len : (i + 1) * seq_len, :]
        if extra:
            part = part + addend[0][i * seq_len : (i + 1) * seq_len, :].astype(jnp.float32)
        dense[i][:seq_len, :] = part.astype(jnp.bfloat16)
        if scored:
            dense[i][seq_len:, :] = jnp.zeros((EXTRA, total.shape[1]), jnp.bfloat16)
            dense[i][seq_len:, :seq_len] = lines[:, i * seq_len : (i + 1) * seq_len].astype(
                jnp.bfloat16
            )


def unpack(spots, slots, blocks, images, addend=(), partners=(), after=()):
    sections, seq_len = slots.shape[1:]
    count, width = blocks[0].shape
    whole = pl.BlockSpec(memory_space=pltpu.VMEM)
    inputs = sections + len(addend) + len(partners)
    height = seq_len + (EXTRA if partners else 0)
    parts = images if addend or partners else 1
    if parts == 1:
        height = images * seq_len
    return pl.pallas_call(
        partial(unpack_kernel, images, sections, len(addend), len(partners)),
        name="unpack",
        in_specs=[SCALARS] + [whole] * (1 + inputs) + [UNREAD] * len(after),
        out_specs=[whole] * parts,
        out_shape=[jax.ShapeDtypeStruct((height, width), jnp.bfloat16)] * parts,
        scratch_shapes=[pltpu.VMEM((sections * count, width), jnp.bfloat16)],
        compiler_params=params(),
        cost_estimate=SMALL,
    )(spots, slots, *blocks, *addend, *partners, *after)


def merge_kernel(sections, *refs):
    met = refs[sections]
    merged = refs[-sections:]
    count = merged[0].shape[0]
    for d in range(sections):
        total = refs[d][...].astype(jnp.float32)
        total = total + met[d * count : (d + 1) * count, :].astype(jnp.float32)
        merged[d][...] = total.astype(jnp.bfloat16)


def merge(blocks, met, after=()):
    sections = len(blocks)
    whole = pl.BlockSpec(memory_space=pltpu.VMEM)
    return pl.pallas_call(
        partial(merge_kernel, sections),
        name="merge",
        in_specs=[whole] * (sections + 1) + [UNREAD] * len(after),
        out_specs=[whole] * sections,
        out_shape=[jax.ShapeDtypeStruct(blocks[0].shape, jnp.bfloat16)] * sections,
        compiler_params=params(),
        cost_estimate=SMALL,
    )(*blocks, met, *after)


def expert_kernel(sections, images, split, unread, *refs):
    spots_ref, other_ref, router_ref = refs[:3]
    mixed_in = refs[3 : 3 + sections]
    pulls = 1 if split == 1 else sections
    grads_in = refs[3 + sections : 3 + sections + pulls]
    up_ref, down_ref = refs[3 + sections + pulls : 5 + sections + pulls]
    outs = refs[5 + sections + pulls + unread :]
    out_parts, grad_parts = outs[:split], outs[split : split + sections]
    mixed, grads = outs[split + sections :]
    count = mixed_in[0].shape[0]
    total = count * sections
    capacity = count // images
    at_row = lax.broadcasted_iota(jnp.int32, (count, capacity), 0)
    at_slot = lax.broadcasted_iota(jnp.int32, (count, capacity), 1)

    others = []
    for d in range(sections):
        mixed[d * count : (d + 1) * count, :] = mixed_in[d][...]
        if split > 1:
            grads[d * count : (d + 1) * count, :] = grads_in[d][...]
        column = jnp.zeros((count, 1), jnp.int32)
        for i in range(images):
            ids = other_ref[spots_ref[images + 1 + d], pl.ds(spots_ref[i], 1), :]
            own = at_row == at_slot + i * capacity
            column = column + jnp.sum(jnp.where(own, ids, 0), axis=1, keepdims=True)
        others.append(column)
    if split == 1:
        grads[...] = grads_in[0][...]
    logits = jnp.dot(mixed[...], router_ref[...], preferred_element_type=jnp.float32)
    lanes = lax.broadcasted_iota(jnp.int32, logits.shape, 1)
    mine = jnp.sum(jnp.where(lanes == spots_ref[images], logits, 0.0), axis=1, keepdims=True)
    is_other = lanes == jnp.concatenate(others, axis=0)
    other = jnp.sum(jnp.where(is_other, logits, 0.0), axis=1, keepdims=True)
    gate = 1.0 / (1.0 + jnp.exp(other - mine))
    preact = jnp.dot(mixed[...], up_ref[...], preferred_element_type=jnp.float32)
    pulled = gate * lax.dot_general(
        grads[...], down_ref[...], (((1,), (1,)), ((), ())), preferred_element_type=jnp.float32
    )
    hidden_wide, slope = gelu_parts(preact)
    hidden = hidden_wide.astype(jnp.bfloat16)
    hidden_grad = (pulled * slope).astype(jnp.bfloat16)
    out_all = jnp.dot(hidden, down_ref[...], preferred_element_type=jnp.float32) * gate
    size = total // split
    for part in range(split):
        out_parts[part][...] = out_all[part * size : (part + 1) * size, :].astype(jnp.bfloat16)
    grad_all = lax.dot_general(
        hidden_grad, up_ref[...], (((1,), (1,)), ((), ())), preferred_element_type=jnp.float32
    )
    for d in range(sections):
        grad_parts[d][...] = grad_all[d * count : (d + 1) * count, :].astype(jnp.bfloat16)


def expert_unit(spots, others, router, mixed_in, grads_in, up_local, down_local, split, after=()):
    sections = len(mixed_in)
    images = spots.shape[0] - 1 - sections
    count, width = mixed_in[0].shape
    total = count * sections
    hidden_units = up_local.shape[1]
    tile = hidden_units

    def whole(shape):
        return pl.BlockSpec(shape, lambda f: (0,) * len(shape))

    block = whole((count, width))
    results = pl.pallas_call(
        partial(expert_kernel, sections, images, split, len(after)),
        name="expert",
        grid=(hidden_units // tile,),
        in_specs=[SCALARS, whole(others.shape), whole(router.shape)]
        + [block] * sections
        + [whole(block_in.shape) for block_in in grads_in]
        + [
            pl.BlockSpec((width, tile), lambda f: (0, f)),
            pl.BlockSpec((tile, width), lambda f: (f, 0)),
        ]
        + [UNREAD] * len(after),
        out_specs=[whole((total // split, width))] * split + [block] * sections,
        out_shape=[jax.ShapeDtypeStruct((total // split, width), jnp.bfloat16)] * split
        + [jax.ShapeDtypeStruct((count, width), jnp.bfloat16)] * sections,
        scratch_shapes=[
            pltpu.VMEM((total, width), jnp.bfloat16),
            pltpu.VMEM((total, width), jnp.bfloat16),
        ],
        compiler_params=params(),
        cost_estimate=SMALL,
    )(spots, others, router, *mixed_in, *grads_in, up_local, down_local, *after)
    return results[:split], results[split:]


def shards(
    tokens,
    route_ids,
    cotangent,
    first_gain,
    in_projection,
    out_projection,
    second_gain,
    router_weight,
    up_weight,
    down_weight,
):
    picture = tokens[0, 0].astype(jnp.float32)
    chosen = route_ids[0, 0]
    upstream = cotangent[0, 0]
    up_local = up_weight[0, 0]
    down_local = down_weight[0, 0]
    seq_len, width = picture.shape
    experts = router_weight.shape[1]
    sections = lax.axis_size("segment")
    members = lax.axis_size("expert")
    per_section = members // PARTS_SIZE
    capacity = 3 * seq_len // experts
    line = members // 2
    here = lax.axis_index("expert")
    section = lax.axis_index("segment")
    place, side = here // 2, here % 2
    group = here // PARTS_SIZE
    my_expert = section * per_section + group
    relative = section ^ jnp.arange(sections)
    experts_here = relative * per_section + group

    def along(value, steps):
        pairs = [(j, (j + 2 * steps) % members) for j in range(members)]
        return lax.ppermute(value, "expert", pairs)

    def across(value):
        return lax.ppermute(value, "expert", [(j, j ^ 1) for j in range(members)])

    def deal(blocks):
        moved = [blocks[0]]
        for d in range(1, sections):
            pairs = [(s, s ^ d) for s in range(sections)]
            moved.append(lax.ppermute(blocks[d], "segment", pairs))
        return moved

    def deal_small(value):
        return lax.all_to_all(
            jnp.take(value, relative, axis=0), "segment", split_axis=0, concat_axis=0, tiled=True
        )

    half = line // 2
    chunks = [list(range(line - 1, half - 1, -1)), list(range(half - 1, -1, -1))]

    expert_list = jnp.arange(experts)
    hits = jnp.any(chosen.T[None] == expert_list[:, None, None], axis=1)
    tokens_before = jnp.arange(seq_len)[:, None] < jnp.arange(seq_len)[None, :]
    own_slots = jnp.dot(
        hits.astype(jnp.bfloat16),
        tokens_before.astype(jnp.bfloat16),
        preferred_element_type=jnp.float32,
    ).astype(jnp.int32)
    own_slots = jnp.where(hits, own_slots, -1)
    others = jnp.sum(chosen, axis=1)[None, :] - expert_list[:, None]
    at_slot = own_slots[:, None, :] == jnp.arange(capacity)[None, :, None]
    own_others = jnp.sum(jnp.where(at_slot, others[:, None, :], 0), axis=2)
    wide = jnp.concatenate([own_slots, own_others], axis=1)
    wide = jnp.take(wide.reshape(sections, per_section, -1), relative, axis=0).transpose(1, 0, 2)
    wide = jnp.broadcast_to(
        wide[:, None], (per_section, PARTS_SIZE) + wide.shape[1:]
    ).reshape(members, -1)
    lane = lax.all_to_all(wide, "expert", split_axis=0, concat_axis=0, tiled=True).reshape(
        members, sections, seq_len + capacity
    )
    slots = lane[:, :, :seq_len]
    slot_others = deal_small(lane[:, :, seq_len:].transpose(1, 0, 2))

    def spots_of(index, far):
        places = (place - jnp.array(chunks[index])) % line
        side_of = (1 - side) if far else side
        return jnp.concatenate(
            [2 * places + side_of, my_expert.reshape(1), relative]
        ).astype(jnp.int32)

    spots = {(index, far): spots_of(index, far) for index in (0, 1) for far in (0, 1)}

    cot_dense = {0: upstream, 1: along(upstream, 1)}
    slots, late_upstream = lax.optimization_barrier((slots, upstream))
    for step in range(2, line):
        cot_dense[step] = along(late_upstream, step)

    def cot_pack(index):
        dense = [cot_dense[step] for step in chunks[index]]
        return pack(spots[index, 0], slots, dense, capacity)[0]

    joined, project_back = jax.vjp(
        partial(project_in, first_gain=first_gain, in_projection=in_projection), picture
    )
    cot_packed, cot_rows = {}, {}
    cot_packed[1] = cot_pack(1)
    joined, cot_packed[1] = lax.optimization_barrier((joined, cot_packed[1]))
    cot_rows[1, 0] = deal(cot_packed[1])
    residual, attend_back = jax.vjp(partial(attend, out_projection=out_projection), picture, joined)
    residual, slot_others = lax.optimization_barrier((residual, slot_others))
    normed, norm_back = jax.vjp(partial(layer_norm, gain_vector=second_gain), residual)
    mixed = normed.astype(jnp.bfloat16)
    own_logits = jnp.dot(mixed, router_weight, preferred_element_type=jnp.float32)

    mixed_dense = {0: mixed}
    for step in range(1, line):
        mixed_dense[step] = along(mixed, step)

    cot_rows[1, 1] = [across(jnp.concatenate(cot_rows[1, 0], axis=0))]
    cot_packed[0] = cot_pack(0)
    cot_rows[0, 0] = deal(cot_packed[0])

    mixed_rows, far_dense = {}, {}

    def mixed_pack(index, after):
        dense = [mixed_dense[step] for step in chunks[index]]
        blocks, joined_dense = pack(spots[index, 0], slots, dense, capacity, after)
        far_dense[index] = across(joined_dense[0])
        mixed_rows[index, 0] = deal(blocks)
        return (blocks[0],)

    def far_pack(index, after):
        blocks, _ = pack(spots[index, 1], slots, [far_dense[index]], capacity, after)
        mixed_rows[index, 1] = deal(blocks)
        return (blocks[0],)

    outs, grads = {}, {}

    def unit(index, far, after):
        outs[index, far], grads[index, far] = expert_unit(
            spots[index, far],
            slot_others,
            router_weight,
            mixed_rows[index, far],
            cot_rows[index, far],
            up_local,
            down_local,
            1 if far else sections,
            after,
        )
        done = (grads[index, far][0],)
        if far:
            grads[index, far] = deal(grads[index, far])
        return done

    done = mixed_pack(1, (cot_packed[0][0],))
    done = mixed_pack(0, done + tuple(cot_rows[1, 1]))
    cot_rows[0, 1] = [across(jnp.concatenate(cot_rows[0, 0], axis=0))]
    done = far_pack(1, done)
    done = unit(1, 0, done)
    done = unit(0, 0, done)
    done = far_pack(0, done)
    done = unit(1, 1, done)
    met = {1: across(outs[1, 1][0])}
    done = unit(0, 1, done)
    met[0] = across(outs[0, 1][0])
    for index in (1, 0):
        held, _ = lax.optimization_barrier((grads[index, 0], done))
        grads[index, 0] = deal(held)

    grad_far, out_back, out_dense, grad_dense = {}, {}, {}, {}
    for index in (1, 0):
        count = len(chunks[index])
        grad_far[index] = unpack(spots[index, 1], slots, grads[index, 1], count, after=done)[0]
        done = (grad_far[index],)
        grad_far[index] = across(grad_far[index])
        merged = merge(outs[index, 0], met[index], done)
        done = (merged[0],)
        out_back[index] = deal(merged)
    for index in (1, 0):
        chunk = chunks[index]
        out_block = unpack(
            spots[index, 0], slots, out_back[index], len(chunk), (), cot_packed[index], done
        )
        done = (out_block[0],)
        for spot, step in enumerate(chunk):
            out_dense[step] = along(out_block[spot], -step) if step else out_block[spot]
    for index in (1, 0):
        chunk = chunks[index]
        grad_block = unpack(
            spots[index, 0], slots, grads[index, 0], len(chunk), (grad_far[index],), (), done
        )
        done = (grad_block[0],)
        for spot, step in enumerate(chunk):
            grad_dense[step] = along(grad_block[spot], -step) if step else grad_block[spot]

    expert_total = sum(out_dense[step][:seq_len].astype(jnp.float32) for step in range(line))
    input_total = sum(grad_dense[step].astype(jnp.float32) for step in range(line))
    layer_out = (residual + expert_total).astype(jnp.bfloat16)

    named = chosen[:, :, None] == expert_list
    score_lines = jnp.zeros((per_section, sections, seq_len), jnp.float32)
    for step in range(line):
        sender = 2 * ((place + step) % line) // PARTS_SIZE
        lines = out_dense[step][seq_len : seq_len + sections, :seq_len].astype(jnp.float32)
        score_lines += jnp.where((jnp.arange(per_section) == sender)[:, None, None], lines, 0.0)
    token_scores = (
        jnp.take(score_lines, relative, axis=1).transpose(1, 0, 2).reshape(experts, seq_len).T
    )
    picked_logit = jnp.sum(jnp.where(named, own_logits[:, None, :], 0.0), axis=2)
    gate_values = 1.0 / (1.0 + jnp.exp(picked_logit[:, ::-1] - picked_logit))
    gate_spread = jnp.sum(jnp.where(named, gate_values[:, :, None], 0.0), axis=1)
    spread_grad = token_scores - gate_spread * jnp.sum(token_scores, axis=1, keepdims=True)
    mixed_grad = input_total + jnp.einsum(
        "se,de->sd", spread_grad, router_weight.astype(jnp.float32), precision=lax.Precision.HIGHEST
    )
    residual_grad = upstream.astype(jnp.float32) + norm_back(mixed_grad)[0]
    picture_grad, joined_grad = attend_back(residual_grad)
    input_grad = (picture_grad + project_back(joined_grad)[0]).astype(jnp.bfloat16)
    return (layer_out[None, None], input_grad[None, None])


def solution(mesh):
    placed = (
        P("segment", "expert", None, None),
        P("segment", "expert", None, None),
        P("segment", "expert", None, None),
        P(),
        P(),
        P(),
        P(),
        P(),
        P("segment", "expert", None, None),
        P("segment", "expert", None, None),
    )
    return jax.shard_map(
        shards,
        mesh=mesh,
        in_specs=placed,
        out_specs=(P("segment", "expert", None, None), P("segment", "expert", None, None)),
        check_vma=False,
    )
```
